128 devices in a mesh: dp: 16 (over y_lo, z, core), fsdp: 8 (over y_hi, x).
Axes of the slice: x: 4, y: 4 (y_hi: 2, y_lo: 2; y = y_hi * 2 + y_lo), z: 4, core: 2. Of those that a mesh axis runs over, the one named last changes fastest.
Arguments:
- tokens: bfloat16 [49152, 1024], P(('dp', 'fsdp')), may hold values from -6 to 6
- norm1_gain: bfloat16 [1024], P('fsdp'), may hold values from 0.25 to 1.75
- norm1_bias: bfloat16 [1024], P('fsdp'), may hold values from -1.75 to 1.75
- qkv_weight: bfloat16 [1024, 3072], P('fsdp'), may hold values from -0.1875 to 0.1875
- query_bias: bfloat16 [1024], P('fsdp'), may hold values from -1.75 to 1.75
- value_bias: bfloat16 [1024], P('fsdp'), may hold values from -1.25 to 1.25
- out_weight: bfloat16 [1024, 1024], P('fsdp'), may hold values from -0.75 to 0.75
- out_bias: bfloat16 [1024], P('fsdp'), may hold values from -1.25 to 1.25
- norm2_gain: bfloat16 [1024], P('fsdp'), may hold values from 0.25 to 1.75
- norm2_bias: bfloat16 [1024], P('fsdp'), may hold values from -1.75 to 1.75
- fc1_weight: bfloat16 [1024, 4096], P('fsdp'), may hold values from -0.1875 to 0.1875
- fc1_bias: bfloat16 [4096], P('fsdp'), may hold values from -1.25 to 1.25
- fc2_weight: bfloat16 [4096, 1024], P('fsdp'), may hold values from -0.09375 to 0.09375
- fc2_bias: bfloat16 [1024], P('fsdp'), may hold values from -1.25 to 1.25
- cotangent: bfloat16 [49152, 1024], P(('dp', 'fsdp')), may hold values from -6 to 6
- group_of: int32 [16], replicated, may hold values from 0 to 1, as said below
- keep_mask: int32 [49152], P(('dp', 'fsdp')), may hold values from 0 to 1, as said below
- group_tokens: int32 [2], replicated, may hold values from 1000 to 4999
Outputs:
- block_out: bfloat16 [49152, 1024], P(('dp', 'fsdp'))
- input_grad: bfloat16 [49152, 1024], P(('dp', 'fsdp'))
- grad_norm1_gain: float32 [1024], P('fsdp')
- grad_norm1_bias: float32 [1024], P('fsdp')
- grad_qkv_weight: float32 [1024, 3072], P('fsdp')
- grad_query_bias: float32 [1024], P('fsdp')
- grad_value_bias: float32 [1024], P('fsdp')
- grad_out_weight: float32 [1024, 1024], P('fsdp')
- grad_out_bias: float32 [1024], P('fsdp')
- grad_norm2_gain: float32 [1024], P('fsdp')
- grad_norm2_bias: float32 [1024], P('fsdp')
- grad_fc1_weight: float32 [1024, 4096], P('fsdp')
- grad_fc1_bias: float32 [4096], P('fsdp')
- grad_fc2_weight: float32 [4096, 1024], P('fsdp')
- grad_fc2_bias: float32 [1024], P('fsdp')
The draws below stay inside these ranges and needn't reach their ends.
Inputs may be any that keep to these rules, and one draw needn't show every extreme that they name: `group_of`: exactly 6 indices of dp hold 1; each device of such an index holds 2 images in slots of 192 rows, every other device 6 images in slots of 64 rows. `keep_mask`: in every image slot the kept tokens are the first n slots and the rest are 0; n is 25 to 50 for a slot of 64 rows and 72 to 145 for a slot of 192 rows, and every device has an image that keeps the most.
All inputs are finite; a program needn't handle non-finite values.
Results may differ from the reference program's by a relative error of at most 0.018.
Values may be sent and summed in bfloat16 or wider, within the bound.
No kernel may reach another device: no remote copies, remote signals or barrier semaphores. Data moves between devices by JAX's collectives and lax.ppermute only.
A program may use at most 256 MiB of HBM per device.

```python
import jax
import jax.numpy as jnp
from jax import lax

D = 1024
HEAD_DIM = 64
FF = 4096
SLOT_S = 64
SLOT_L = 192
ROWS_DEV = 384
TOKENS = 49152
N_DP = 16
N_FSDP = 8


def group_lanes(key):
    shuffled = jax.random.permutation(key, N_DP)
    return (shuffled < 3 * N_DP // 8).astype(jnp.int32)


def draw_group_of(key, part):
    lane_groups = group_lanes(key)
    return lane_groups


def draw_keep_mask(key, part):
    lane_groups = group_lanes(key)
    key = jax.random.fold_in(key, 23)
    device_count = TOKENS // ROWS_DEV
    slots_most = ROWS_DEV // SLOT_S
    key_small, key_large, key_chosen = jax.random.split(key, 3)
    small_counts = jax.random.randint(key_small, (device_count, slots_most), 25, 51)
    large_counts = jax.random.randint(key_large, (device_count, slots_most), 72, 146)
    dev_group = jnp.repeat(lane_groups, N_FSDP)
    image_total = jnp.where(dev_group == 1, ROWS_DEV // SLOT_L, slots_most)
    chosen = jax.random.randint(key_chosen, (device_count,), 0, 1 << 20) % image_total
    slot_ids = jnp.arange(slots_most)
    small_counts = jnp.where(slot_ids[None, :] == chosen[:, None], 50, small_counts)
    large_counts = jnp.where(slot_ids[None, :] == chosen[:, None], 145, large_counts)
    counts = jnp.where(dev_group[:, None] == 1, large_counts, small_counts)
    row_ids = jnp.arange(ROWS_DEV)
    slot_rows = jnp.where(dev_group == 1, SLOT_L, SLOT_S)[:, None]
    image_index = row_ids[None, :] // slot_rows
    position = row_ids[None, :] % slot_rows
    onehot = image_index[:, :, None] == slot_ids[None, None, :]
    kept_limit = jnp.sum(jnp.where(onehot, counts[:, None, :], 0), axis=-1)
    return (position < kept_limit).astype(jnp.int32).reshape(TOKENS)


def level_of(own_key, shape, shards, low, top_value):
    level = 1.0
    for dim, parts in shards:
        heights = jax.random.uniform(jax.random.fold_in(jax.random.fold_in(own_key, 6), dim), (parts,), jnp.float32, low / len(shards), top_value / len(shards))
        level = level * jnp.repeat(jnp.exp(heights), shape[dim] // parts).reshape((-1,) + (1,) * (len(shape) - 1 - dim))
    return level


def gaussian(key, extent, scale, limit, cuts=(), held_as=jnp.bfloat16):
    drawn = jax.random.normal(key, extent, jnp.float32) * scale
    if len(cuts) > 0:
        drawn = level_of(key, extent, cuts, -0.22, 0.18) * drawn
    return jnp.clip(drawn, min=-limit, max=limit).astype(held_as)


def setup_inputs(seed: int = 0) -> dict:
    arg_keys = jax.random.split(jax.random.key(seed), 19)
    return {
        "tokens": gaussian(arg_keys[0], (TOKENS, D), 1.0, 6.0, ((0, 128),)),
        "norm1_gain": jnp.clip(1.0 + 0.15 * jax.random.normal(arg_keys[1], (D,), jnp.float32), 0.25, 1.75).astype(jnp.bfloat16),
        "norm1_bias": gaussian(arg_keys[2], (D,), 0.3, 1.75, ((0, 8),)),
        "qkv_weight": gaussian(arg_keys[3], (D, 3 * D), D ** -0.5, 0.1875, ((0, 8),)),
        "query_bias": gaussian(arg_keys[4], (D,), 0.3, 1.75, ((0, 8),)),
        "value_bias": gaussian(arg_keys[5], (D,), 0.2, 1.25, ((0, 8),)),
        "out_weight": gaussian(arg_keys[6], (D, D), (D // 16) ** -0.5, 0.75, ((0, 8),)),
        "out_bias": gaussian(arg_keys[7], (D,), 0.2, 1.25, ((0, 8),)),
        "norm2_gain": jnp.clip(1.0 + 0.15 * jax.random.normal(arg_keys[8], (D,), jnp.float32), 0.25, 1.75).astype(jnp.bfloat16),
        "norm2_bias": gaussian(arg_keys[9], (D,), 0.3, 1.75, ((0, 8),)),
        "fc1_weight": gaussian(arg_keys[10], (D, FF), D ** -0.5, 0.1875, ((0, 8),)),
        "fc1_bias": gaussian(arg_keys[11], (FF,), 0.2, 1.25, ((0, 8),)),
        "fc2_weight": gaussian(arg_keys[12], (FF, D), FF ** -0.5, 0.09375, ((0, 8),)),
        "fc2_bias": gaussian(arg_keys[13], (D,), 0.2, 1.25, ((0, 8),)),
        "cotangent": gaussian(arg_keys[14], (TOKENS, D), 1.0, 6.0, ((0, 128),)),
        "group_of": draw_group_of(jax.random.fold_in(arg_keys[18], 71), 0),
        "keep_mask": draw_keep_mask(jax.random.fold_in(arg_keys[18], 71), 0),
        "group_tokens": jax.random.randint(arg_keys[17], (2,), 1000, 5000).astype(jnp.int32),
    }


@jax.custom_vjp
def low(v):
    return lax.optimization_barrier(v.astype(jnp.bfloat16)).astype(jnp.float32)

@jax.custom_vjp
def low_back(v):
    return v

def low_keep(v):
    return (low(v), None)

def low_pass(kept, grad):
    return (grad,)

def back_keep(v):
    return (v, None)

def back_low(kept, grad):
    return (low(grad),)
low.defvjp(low_keep, low_pass)
low_back.defvjp(back_keep, back_low)
precise = lax.Precision.HIGHEST
eps_norm = 1e-06

def product(left, right):
    return jnp.dot(left, right, precision=precise, preferred_element_type=jnp.float32)

def layer_norm(values, norm_gain, norm_shift):
    center = values - lax.optimization_barrier(jnp.mean(values, axis=-1, keepdims=True))
    spread = lax.optimization_barrier(jnp.mean(center * center, axis=-1, keepdims=True))
    return center * lax.rsqrt(spread + eps_norm) * norm_gain + norm_shift

def gelu_exact(values):
    return jax.nn.gelu(values, approximate=False)

def device_block(device_item, params):
    block_rows, group_id, kept = device_item
    norm1_gain, norm1_bias, qkv_weight, query_bias, value_bias, out_weight, out_bias, norm2_gain, norm2_bias, fc1_weight, fc1_bias, fc2_weight, fc2_bias = params
    row_count = block_rows.shape[0]
    model_width = block_rows.shape[1]
    head_count = model_width // HEAD_DIM
    slot_rows = jnp.where(group_id == 1, SLOT_L, SLOT_S).astype(jnp.int32)
    image_index = jnp.arange(row_count, dtype=jnp.int32) // slot_rows
    allowed = (image_index[:, None] == image_index[None, :]) & (kept[None, :] == 1)
    mask_col = kept.astype(jnp.float32)[:, None]
    normed = low(layer_norm(block_rows, norm1_gain, norm1_bias))
    packed = product(normed, qkv_weight)
    query_rows = low_back(low(packed[:, :model_width] + query_bias))
    key_rows = low_back(low(packed[:, model_width:2 * model_width]))
    value_rows = low_back(low(packed[:, 2 * model_width:] + value_bias))
    query_heads = query_rows.reshape(row_count, head_count, HEAD_DIM)
    key_heads = key_rows.reshape(row_count, head_count, HEAD_DIM)
    value_heads = value_rows.reshape(row_count, head_count, HEAD_DIM)
    scores = jnp.einsum('ihd,jhd->hij', query_heads, key_heads, precision=precise) * HEAD_DIM ** (-0.5)
    scores = low_back(jnp.where(allowed[None], scores, jnp.float32(-1e+30)))
    row_max = lax.optimization_barrier(jnp.max(scores, axis=-1, keepdims=True))
    exp_scores = jnp.exp(scores - row_max)
    attn_probs = low(exp_scores / lax.optimization_barrier(jnp.sum(exp_scores, axis=-1, keepdims=True)))
    mixed_rows = jnp.einsum('hij,jhd->ihd', attn_probs, value_heads, precision=precise)
    mixed_rows = low_back(low(mixed_rows.reshape(row_count, model_width)))
    attended = low_back(product(mixed_rows, out_weight) + out_bias)
    middle = block_rows + mask_col * attended
    normed_two = low(layer_norm(middle, norm2_gain, norm2_bias))
    hidden_pre = low_back(product(normed_two, fc1_weight) + fc1_bias)
    hidden = low(gelu_exact(hidden_pre))
    branch = low_back(product(hidden, fc2_weight) + fc2_bias)
    return middle + mask_col * branch

def reference(tokens, norm1_gain, norm1_bias, qkv_weight, query_bias, value_bias, out_weight, out_bias, norm2_gain, norm2_bias, fc1_weight, fc1_bias, fc2_weight, fc2_bias, cotangent, group_of, keep_mask, group_tokens):
    params = tuple((weight_arg.astype(jnp.float32) for weight_arg in (norm1_gain, norm1_bias, qkv_weight, query_bias, value_bias, out_weight, out_bias, norm2_gain, norm2_bias, fc1_weight, fc1_bias, fc2_weight, fc2_bias)))
    devices = TOKENS // ROWS_DEV
    block_rows = tokens.astype(jnp.float32).reshape(devices, ROWS_DEV, D)
    dev_group = jnp.repeat(group_of, N_FSDP).astype(jnp.int32)
    kept_rows = keep_mask.reshape(devices, ROWS_DEV)

    def whole_block(all_rows, all_params):
        return lax.map(lambda device_item: jax.checkpoint(device_block)(device_item, all_params), (all_rows, dev_group, kept_rows))
    block_result, pullback = jax.vjp(whole_block, block_rows, params)
    counts = group_tokens.astype(jnp.float32)
    group_share = counts / jnp.sum(counts)
    own_share = jnp.where(dev_group == 1, group_share[1], group_share[0])
    cot_rows = cotangent.astype(jnp.float32).reshape(devices, ROWS_DEV, D) * own_share[:, None, None]
    grad_rows, grad_params = pullback(cot_rows)
    g_gain1, g_bias1, g_qkv, g_query, g_value, g_out, g_outb, g_gain2, g_bias2, g_fc1, g_fc1b, g_fc2, g_fc2b = grad_params
    return (block_result.reshape(TOKENS, D).astype(jnp.bfloat16), grad_rows.reshape(TOKENS, D).astype(jnp.bfloat16), g_gain1, g_bias1, g_qkv, g_query, g_value, g_out, g_outb, g_gain2, g_bias2, g_fc1, g_fc1b, g_fc2, g_fc2b)
```

```python
import jax
import jax.numpy as jnp
from jax import lax
from jax.experimental import pallas as pl
from jax.experimental.pallas import tpu as pltpu
from jax.sharding import PartitionSpec as P

HEAD_DIM = 64
SLOT_S = 64
SLOT_L = 192
BLOCK = 192
EPS = 1e-06
AXES = ("dp", "fsdp")
BF = jnp.bfloat16
F32 = jnp.float32

Z_GROUPS = [[lo * 8 + 2 * z + c for z in range(4)] for lo in range(2) for c in range(2)]
X_GROUPS = [[0, 1, 2, 3], [4, 5, 6, 7]]


def place(linear):
    dp, fs = divmod(linear, 8)
    return fs % 4, (fs // 4) * 2 + dp // 8, (dp // 2) % 4, dp % 2


def linear_of(x, y, z, c):
    x, y, z = x % 4, y % 4, z % 4
    return (((y % 2) * 4 + z) * 2 + c) * 8 + (y // 2) * 4 + x


def permute(value, move):
    return lax.ppermute(
        value, AXES, [(l, linear_of(*move(*place(l)))) for l in range(128)]
    )


def ring_move(axis):
    def move(x, y, z, c):
        s = 1 - 2 * c
        return (x + s * (axis == "x"), y + s * (axis == "y"), z + s * (axis == "z"), c)

    return move


def swap_core(x, y, z, c):
    return x, y, z, 1 - c


def flip_hi(x, y, z, c):
    return x, 3 - y, z, c


def flip_lo(x, y, z, c):
    return x, y ^ 1, z, c


class Where:
    def __init__(self):
        dp, fs = lax.axis_index("dp"), lax.axis_index("fsdp")
        self.dp, self.fs = dp, fs
        self.c = dp % 2
        self.z = (dp // 2) % 4
        self.lo = dp // 8
        self.x = fs % 4
        self.hi = fs // 4
        self.y = self.hi * 2 + self.lo
        self.sign = 1 - 2 * self.c

    def along(self, axis):
        return {"x": self.x, "y": self.y, "z": self.z}[axis]

    def source(self, axis, step):
        return lax.rem(self.along(axis) - self.sign * step + 8, 4)


def pick(stacked, index, axis=0):
    return lax.dynamic_index_in_dim(stacked, index, axis, keepdims=False)


def ring_gather(here, value, axis, buffer, put):
    for step in range(4):
        if step:
            value = permute(value, ring_move(axis))
        buffer = put(buffer, value, here.source(axis, step))
    return buffer


def ring_reduce(here, axis, term):
    total = term(here.source(axis, 1))
    for step in range(2, 5):
        total = permute(total, ring_move(axis))
        total = (total.astype(F32) + term(here.source(axis, step)).astype(F32)).astype(BF)
    return total


def put_at(buffer, value, starts):
    return lax.dynamic_update_slice(buffer, value.reshape(value.shape), tuple(starts))


def both_hi(here, value):
    return jnp.stack([value, permute(value, flip_hi)])


def gather_rows_x(here, value):
    r, n = value.shape
    pair = both_hi(here, value)

    def put(buffer, block, x):
        buffer = lax.dynamic_update_slice(buffer, block[0][None, None], (here.hi, x, 0, 0))
        return lax.dynamic_update_slice(buffer, block[1][None, None], (1 - here.hi, x, 0, 0))

    return ring_gather(here, pair, "x", jnp.zeros((2, 4, r, n), value.dtype), put)


def gather_rows_z(here, value):
    r, n = value.shape
    q = r // 4
    quarter = lax.dynamic_slice_in_dim(value, here.z * q, q, 0)
    slab = gather_rows_x(here, quarter)[:, :, None]

    def put(buffer, block, z):
        return lax.dynamic_update_slice(buffer, block, (0, 0, z, 0, 0))

    full = ring_gather(here, slab, "z", jnp.zeros((2, 4, 4, q, n), value.dtype), put)
    return full.reshape(8 * r, n)


def gather_rows_y(here, value):
    r, n = value.shape
    q = r // 2
    half = lax.dynamic_slice_in_dim(value, here.lo * q, q, 0)

    def put_x(buffer, block, x):
        return lax.dynamic_update_slice(buffer, block[None], (x, 0, 0))

    row = ring_gather(here, half, "x", jnp.zeros((4, q, n), value.dtype), put_x)

    def put_y(buffer, block, y):
        return lax.dynamic_update_slice(buffer, block[None, :, None], (y // 2, 0, y % 2, 0, 0))

    full = ring_gather(here, row, "y", jnp.zeros((2, 4, 2, q, n), value.dtype), put_y)
    return full.reshape(8 * r, n)


def sum_first(blocks):
    return jnp.sum(blocks.astype(F32), axis=0)


def reduce_lo(here, value):
    halves = value.reshape((2, value.shape[0] // 2) + value.shape[1:])
    sent = permute(pick(halves, 1 - here.lo).astype(BF), flip_lo)
    return pick(halves, here.lo).astype(F32) + sent.astype(F32)


def all_to_all(value, axis, groups=None):
    return lax.all_to_all(value, axis, 0, 0, tiled=True, axis_index_groups=groups)


def ordered_pair(flag, own, other):
    return jnp.stack([jnp.where(flag == 0, own, other), jnp.where(flag == 0, other, own)])


def gather_slices(here, piece):
    pair = ordered_pair(here.lo, piece, permute(piece, flip_lo))

    def put(buffer, block, z):
        return lax.dynamic_update_slice(buffer, block[None], (z, 0, 0, 0))

    full = ring_gather(here, pair, "z", jnp.zeros((4,) + pair.shape, piece.dtype), put)
    return ordered_pair(here.c, full, permute(full, swap_core))


def butterfly(value):
    for move in (
        lambda x, y, z, c: (x ^ 1, y, z, c),
        lambda x, y, z, c: (3 - x, y, z, c),
        flip_lo,
        flip_hi,
        lambda x, y, z, c: (x, y, z ^ 1, c),
        lambda x, y, z, c: (x, y, 3 - z, c),
        swap_core,
    ):
        value = value + permute(value, move)
    return value


RATE = 0.51
ERFC = (
    0.28791757708249816,
    0.28415126012743,
    0.2790719172776486,
    0.055036978129087616,
    0.35846874221749475,
    -0.3591518512954867,
    0.09450494290776956,
)


def hidden_kernel(rows, weight, shift, hidden, slope):
    u = jnp.dot(rows[...], weight[...], preferred_element_type=F32) + shift[...]
    bell = jnp.exp(-0.5 * u * u)
    t = 1.0 / (1.0 + (RATE * 0.5**0.5) * jnp.abs(u))
    tail = jnp.full_like(u, 0.5 * ERFC[-1])
    for coefficient in ERFC[-2::-1]:
        tail = tail * t + 0.5 * coefficient
    tail = tail * t * bell
    area = jnp.where(u >= 0, 1.0 - tail, tail)
    hidden[...] = (u * area).astype(BF)
    slope[...] = (area + u * bell * 0.3989422804014327).astype(BF)


def hidden_layer(rows, weight, shift):
    m, k = rows.shape
    n = weight.shape[1]
    cols = 256
    out = pl.BlockSpec((m, cols), lambda i: (0, i))
    return pl.pallas_call(
        hidden_kernel,
        grid=(n // cols,),
        in_specs=[
            pl.BlockSpec((m, k), lambda i: (0, 0)),
            pl.BlockSpec((k, cols), lambda i: (0, i)),
            pl.BlockSpec((1, cols), lambda i: (0, i)),
        ],
        out_specs=[out, out],
        out_shape=[jax.ShapeDtypeStruct((m, n), BF)] * 2,
        compiler_params=pltpu.CompilerParams(vmem_limit_bytes=32 << 20),
        cost_estimate=pl.CostEstimate(
            flops=2 * m * n * k, bytes_accessed=2 * (m * k + k * n + 2 * m * n), transcendentals=m * n
        ),
        name="hidden_layer",
    )(rows, weight, shift)


def dot(left, right):
    return jnp.dot(left, right, preferred_element_type=F32)


def dot_nt(left, right):
    return lax.dot_general(left, right, (((1,), (1,)), ((), ())), preferred_element_type=F32)


def dot_tn(left, right):
    return lax.dot_general(left, right, (((0,), (0,)), ((), ())), preferred_element_type=F32)


def normalize(values):
    center = values - jnp.mean(values, axis=-1, keepdims=True)
    rstd = lax.rsqrt(jnp.mean(center * center, axis=-1, keepdims=True) + EPS)
    return center * rstd, rstd


def normalize_back(grad, yhat, rstd, gain):
    t = grad * gain
    return rstd * (
        t
        - jnp.mean(t, axis=-1, keepdims=True)
        - yhat * jnp.mean(t * yhat, axis=-1, keepdims=True)
    )


def body(
    tokens,
    norm1_gain,
    norm1_bias,
    qkv_weight,
    query_bias,
    value_bias,
    out_weight,
    out_bias,
    norm2_gain,
    norm2_bias,
    fc1_weight,
    fc1_bias,
    fc2_weight,
    fc2_bias,
    cotangent,
    group_of,
    keep_mask,
    group_tokens,
):
    here = Where()
    own_rows, width = tokens.shape
    c = here.c

    vectors = jnp.concatenate(
        [norm1_gain, norm1_bias, query_bias, value_bias, out_bias, norm2_gain, norm2_bias, fc2_bias, fc1_bias]
    ).reshape(12, 128)
    vectors = gather_rows_x(here, vectors).reshape(8, 12, 128)
    qkv_half = pick(qkv_weight.reshape(128, 24, 2, 64), c, 2).reshape(128, 1536)
    out_half = pick(out_weight.reshape(2, 64, 1024), c)
    fc1_half = pick(fc1_weight.reshape(128, 8, 2, 256), c, 2).reshape(128, 2048)
    fc2_half = pick(fc2_weight.reshape(2, 256, 1024), c)
    rows_low = jnp.concatenate([tokens, permute(tokens, swap_core)])
    keep = jnp.concatenate([keep_mask, permute(keep_mask, swap_core)])
    qkv_all = gather_rows_y(here, qkv_half)
    fc1_all = gather_rows_x(here, fc1_half).reshape(1024, 2048)
    out_all = gather_rows_x(here, out_half).reshape(512, 1024)
    fc2_all = gather_rows_z(here, fc2_half)
    cot = jnp.concatenate([cotangent, permute(cotangent, swap_core)])

    def vector(k):
        return vectors[:, k].astype(F32)

    def half_vector(k):
        return pick(vector(k).reshape(8, 2, 64), c, 1).reshape(512)

    gain_one, shift_one, out_shift, gain_two, shift_two, fc2_shift = (
        vector(k).reshape(1024) for k in (0, 1, 4, 5, 6, 7)
    )
    query_shift, value_shift = half_vector(2), half_vector(3)
    fc1_shift = pick(vectors[:, 8:12].astype(F32).reshape(8, 2, 256), c, 1).reshape(1, 2048)

    groups = jnp.stack([pick(group_of, here.dp), pick(group_of, here.dp + here.sign)])
    counts = group_tokens.astype(F32)
    share = counts / jnp.sum(counts)
    share = jnp.where(groups == 1, share[1], share[0])
    share_col = jnp.repeat(share, own_rows)[:, None]
    mask_col = keep.astype(F32)[:, None]
    row_count = 2 * own_rows
    blocks = row_count // BLOCK
    block_group = jnp.repeat(groups, blocks // 2)
    image = jnp.where(
        block_group[:, None] == 1, 0, jnp.arange(BLOCK, dtype=jnp.int32)[None] // SLOT_S
    )
    allowed = (image[:, :, None] == image[:, None, :]) & (keep.reshape(blocks, 1, BLOCK) == 1)

    rows = rows_low.astype(F32)
    yhat_one, rstd_one = normalize(rows)
    normed = (yhat_one * gain_one + shift_one).astype(BF)
    packed = dot(normed, qkv_all)
    heads = 8

    def split(v):
        return v.astype(BF).reshape(blocks, BLOCK, heads, HEAD_DIM)

    query = split(packed[:, :512] + query_shift)
    key = split(packed[:, 512:1024])
    value = split(packed[:, 1024:] + value_shift)
    scale = HEAD_DIM ** (-0.5)
    scores = jnp.einsum("bihd,bjhd->bhij", query, key, preferred_element_type=F32) * scale
    scores = jnp.where(allowed[:, None], scores, F32(-1e30))
    exps = jnp.exp(scores - jnp.max(scores, axis=-1, keepdims=True))
    probs = exps / jnp.sum(exps, axis=-1, keepdims=True)
    probs_low = probs.astype(BF)
    mixed = jnp.einsum("bhij,bjhd->bihd", probs_low, value, preferred_element_type=F32)
    mixed = mixed.astype(BF).reshape(row_count, 512)

    def both_cores(part):
        other = permute(part.astype(BF), swap_core).astype(F32)
        return part + jnp.concatenate([other[own_rows:], other[:own_rows]])

    def own_part(part):
        return part[:own_rows] + permute(part[own_rows:].astype(BF), swap_core).astype(F32)

    attended = both_cores(dot(mixed, out_all)) + out_shift
    middle = rows + mask_col * attended
    yhat_two, rstd_two = normalize(middle)
    normed_two = (yhat_two * gain_two + shift_two).astype(BF)
    hidden, slope = hidden_layer(normed_two, fc1_all, fc1_shift)
    branch = own_part(dot(hidden, fc2_all)) + fc2_shift
    block_out = (middle[:own_rows] + mask_col[:own_rows] * branch).astype(BF)

    incoming = cot.astype(F32) * share_col
    d_branch = (mask_col * incoming).astype(BF)
    grad_fc2 = dot_tn(hidden, d_branch).astype(BF)
    d_pre_float = dot_nt(d_branch, fc2_all) * slope.astype(F32)
    d_pre = d_pre_float.astype(BF)
    grad_fc1 = dot_tn(normed_two, d_pre).astype(BF)
    d_normed_two = both_cores(dot_nt(d_pre, fc1_all))
    d_middle = incoming + normalize_back(d_normed_two, yhat_two, rstd_two, gain_two)
    d_attended = (mask_col * d_middle).astype(BF)
    grad_out = dot_tn(mixed, d_attended).astype(BF)
    d_mixed = split(dot_nt(d_attended, out_all))
    d_probs = jnp.einsum("bihd,bjhd->bhij", d_mixed, value, preferred_element_type=F32)
    d_value = jnp.einsum("bhij,bihd->bjhd", probs_low, d_mixed, preferred_element_type=F32)
    d_scores = probs * (d_probs - jnp.sum(probs * d_probs, axis=-1, keepdims=True))
    d_scores = d_scores.astype(BF)
    d_query = jnp.einsum("bhij,bjhd->bihd", d_scores, key, preferred_element_type=F32) * scale
    d_key = jnp.einsum("bhij,bihd->bjhd", d_scores, query, preferred_element_type=F32) * scale

    def join(v):
        return v.astype(BF).reshape(row_count, 512)

    d_query, d_key, d_value = join(d_query), join(d_key), join(d_value)
    d_packed = jnp.concatenate([d_query, d_key, d_value], axis=1)
    grad_qkv = dot_tn(normed, d_packed).astype(BF)
    d_normed = own_part(dot_nt(d_packed, qkv_all))
    input_grad = (
        d_middle[:own_rows]
        + normalize_back(d_normed, yhat_one[:own_rows], rstd_one[:own_rows], gain_one)
    ).astype(BF)

    def column_sum(v):
        return jnp.sum(v.astype(F32), axis=0)

    def own_sum(v):
        return column_sum(v[:own_rows]).reshape(8, 1, 128)

    def half_sum(v):
        n = v.shape[1] // 8
        terms = column_sum(v).reshape(8, 1, n)
        return jnp.concatenate(
            [jnp.where(c == 0, terms, 0.0), jnp.where(c == 0, 0.0, terms)], axis=1
        ).reshape(8, n // 64, 128)

    vector_terms = jnp.concatenate(
        [
            own_sum(d_normed * yhat_one[:own_rows]),
            own_sum(d_normed),
            half_sum(d_query),
            half_sum(d_value),
            own_sum(d_attended),
            own_sum(d_normed_two * yhat_two),
            own_sum(d_normed_two),
            own_sum(d_branch),
            half_sum(d_pre),
        ],
        axis=1,
    )
    vector_sums = pick(butterfly(vector_terms), here.fs)

    fc2_terms = grad_fc2.reshape(8, 4, 64, 1024)
    fc2_sum = ring_reduce(here, "z", lambda z: pick(fc2_terms, z, 1))
    fc2_sum = reduce_lo(here, sum_first(all_to_all(fc2_sum, "fsdp"))).astype(BF)

    fc1_terms = grad_fc1.reshape(2, 4, 128, 2048)
    fc1_sum = ring_reduce(here, "x", lambda x: pick(fc1_terms, x, 1))
    fc1_sum = jnp.swapaxes(fc1_sum.reshape(2, 4, 32, 2048), 0, 1)
    fc1_sum = sum_first(all_to_all(fc1_sum, "dp", Z_GROUPS))
    sent = permute(pick(fc1_sum, 1 - here.hi).astype(BF), flip_hi)
    fc1_sum = pick(fc1_sum, here.hi) + sent.astype(F32)
    fc1_sum = reduce_lo(here, fc1_sum).astype(BF)

    out_sum = sum_first(all_to_all(grad_out.reshape(8, 64, 1024), "fsdp"))
    out_sum = reduce_lo(here, out_sum).astype(BF).reshape(4, 8, 1024)
    out_sum = sum_first(all_to_all(out_sum, "dp", Z_GROUPS)).astype(BF)

    qkv_terms = grad_qkv.reshape(2, 4, 2, 64, 1536)
    qkv_sum = ring_reduce(
        here,
        "y",
        lambda y: lax.dynamic_slice(
            qkv_terms, (y // 2, 0, y % 2, 0, 0), (1, 4, 1, 64, 1536)
        ).reshape(4, 64, 1536),
    )
    qkv_sum = sum_first(all_to_all(qkv_sum, "fsdp", X_GROUPS)).astype(BF).reshape(4, 16, 1536)
    qkv_sum = sum_first(all_to_all(qkv_sum, "dp", Z_GROUPS)).astype(BF)

    mlp_piece = jnp.concatenate([fc2_sum, fc1_sum.reshape(32, 1024)])
    mlp_full = gather_slices(here, mlp_piece)
    grad_fc2_weight = mlp_full[:, :, :, :32].reshape(512, 1024).astype(F32)
    grad_fc1_weight = (
        mlp_full[:, :, :, 32:]
        .reshape(2, 128, 8, 256)
        .transpose(1, 2, 0, 3)
        .reshape(128, 4096)
        .astype(F32)
    )
    out_full = gather_slices(here, out_sum)
    grad_out_weight = jnp.swapaxes(out_full, 1, 2).reshape(128, 1024).astype(F32)
    qkv_full = gather_slices(here, qkv_sum)
    grad_qkv_weight = (
        jnp.swapaxes(qkv_full, 1, 2)
        .reshape(2, 128, 24, 64)
        .transpose(1, 2, 0, 3)
        .reshape(128, 3072)
        .astype(F32)
    )
    return (
        block_out,
        input_grad,
        vector_sums[0],
        vector_sums[1],
        grad_qkv_weight,
        vector_sums[2],
        vector_sums[3],
        grad_out_weight,
        vector_sums[4],
        vector_sums[5],
        vector_sums[6],
        grad_fc1_weight,
        vector_sums[8:12].reshape(512),
        grad_fc2_weight,
        vector_sums[7],
    )


def solution(mesh):
    rows, cols, both = P("fsdp", None), P("fsdp"), ("dp", "fsdp")
    in_specs = (
        P(both, None),
        cols,
        cols,
        rows,
        cols,
        cols,
        rows,
        cols,
        cols,
        cols,
        rows,
        cols,
        rows,
        cols,
        P(both, None),
        P(),
        P(both),
        P(),
    )
    out_specs = (
        P(both, None),
        P(both, None),
        cols,
        cols,
        rows,
        cols,
        cols,
        rows,
        cols,
        cols,
        cols,
        rows,
        cols,
        rows,
        cols,
    )
    return jax.shard_map(body, mesh=mesh, in_specs=in_specs, out_specs=out_specs, check_vma=False)
```

```python
import jax
import jax.numpy as jnp
from jax import lax
from jax.experimental import pallas as pl
from jax.experimental.pallas import tpu as pltpu
from jax.sharding import PartitionSpec as P

HEAD_DIM = 64
SLOT_S = 64
SLOT_L = 192
BLOCK = 192
EPS = 1e-06
AXES = ("dp", "fsdp")
BF = jnp.bfloat16
F32 = jnp.float32

Z_GROUPS = [[lo * 8 + 2 * z + c for z in range(4)] for lo in range(2) for c in range(2)]
X_GROUPS = [[0, 1, 2, 3], [4, 5, 6, 7]]


def place(linear):
    dp, fs = divmod(linear, 8)
    return fs % 4, (fs // 4) * 2 + dp // 8, (dp // 2) % 4, dp % 2


def linear_of(x, y, z, c):
    x, y, z = x % 4, y % 4, z % 4
    return (((y % 2) * 4 + z) * 2 + c) * 8 + (y // 2) * 4 + x


def permute(value, move):
    return lax.ppermute(
        value, AXES, [(l, linear_of(*move(*place(l)))) for l in range(128)]
    )


def ring_move(axis):
    def move(x, y, z, c):
        s = 1 - 2 * c
        return (x + s * (axis == "x"), y + s * (axis == "y"), z + s * (axis == "z"), c)

    return move


def swap_core(x, y, z, c):
    return x, y, z, 1 - c


def flip_hi(x, y, z, c):
    return x, 3 - y, z, c


def flip_lo(x, y, z, c):
    return x, y ^ 1, z, c


class Where:
    def __init__(self):
        dp, fs = lax.axis_index("dp"), lax.axis_index("fsdp")
        self.dp, self.fs = dp, fs
        self.c = dp % 2
        self.z = (dp // 2) % 4
        self.lo = dp // 8
        self.x = fs % 4
        self.hi = fs // 4
        self.y = self.hi * 2 + self.lo
        self.sign = 1 - 2 * self.c

    def along(self, axis):
        return {"x": self.x, "y": self.y, "z": self.z}[axis]

    def source(self, axis, step):
        return lax.rem(self.along(axis) - self.sign * step + 8, 4)


def pick(stacked, index, axis=0):
    return lax.dynamic_index_in_dim(stacked, index, axis, keepdims=False)


def ring_gather(here, value, axis, buffer, put):
    for step in range(4):
        if step:
            value = permute(value, ring_move(axis))
        buffer = put(buffer, value, here.source(axis, step))
    return buffer


def ring_reduce(here, axis, term):
    total = term(here.source(axis, 1))
    for step in range(2, 5):
        total = permute(total, ring_move(axis))
        total = (total.astype(F32) + term(here.source(axis, step)).astype(F32)).astype(BF)
    return total


def ring_blocks(value, axis):
    blocks = [value]
    for _ in range(3):
        blocks.append(permute(blocks[-1], ring_move(axis)))
    return blocks


def kernel_call(kernel, name, out_shape, flops=0, moved=0, vmem=40 << 20, **kwargs):
    return pl.pallas_call(
        kernel,
        out_shape=out_shape,
        name=name,
        compiler_params=pltpu.CompilerParams(vmem_limit_bytes=vmem),
        cost_estimate=pl.CostEstimate(flops=flops, bytes_accessed=moved, transcendentals=0),
        **kwargs,
    )


def struct(shape, dtype):
    return jax.ShapeDtypeStruct(shape, dtype)


ANY = pl.BlockSpec(memory_space=pl.ANY)
SMEM = pl.BlockSpec(memory_space=pltpu.SMEM)


def assemble(name, parts, spots, shape, target):
    spots = jnp.stack([jnp.asarray(s, jnp.int32) for s in spots])

    def kernel(spots_ref, *refs):
        ins, out, sems = refs[: len(parts)], refs[len(parts)], refs[len(parts) + 1]
        copies = [
            pltpu.make_async_copy(ins[n], target(out, spots_ref[n]), sems.at[n])
            for n in range(len(parts))
        ]
        for copy in copies:
            copy.start()
        for copy in copies:
            copy.wait()

    size = 2 * 2
    for d in shape:
        size *= d
    return kernel_call(
        kernel,
        name,
        struct(shape, BF),
        moved=size,
        in_specs=[SMEM] + [ANY] * len(parts),
        out_specs=ANY,
        scratch_shapes=[pltpu.SemaphoreType.DMA((len(parts),))],
    )(spots, *parts)


def with_other_hi(here, name, value):
    other = permute(value, flip_hi)
    return assemble(
        name, [value, other], [here.hi, 1 - here.hi], (2,) + value.shape, lambda o, s: o.at[s]
    )


def gather_x(here, name, value):
    two, r, n = value.shape
    return assemble(
        name,
        ring_blocks(value, "x"),
        [here.source("x", s) for s in range(4)],
        (two, 4, r, n),
        lambda o, s: o.at[:, s],
    )


def lane_halves(c, left, right):
    first = lax.broadcasted_iota(jnp.int32, left.shape, 1) < 64
    low = jnp.where(first, left, pltpu.roll(right, 64, 1))
    high = jnp.where(first, pltpu.roll(left, 64, 1), right)
    return jnp.where(c == 0, low, high)


def halves_kernel(place_ref, qkv, fc1, qkv_half, fc1_half):
    c = place_ref[0]
    for g in range(12):
        left = qkv[:, g * 256 : g * 256 + 128].astype(F32)
        right = qkv[:, g * 256 + 128 : g * 256 + 256].astype(F32)
        qkv_half[:, g * 128 : (g + 1) * 128] = lane_halves(c, left, right).astype(BF)
    for f in range(8):
        fc1_half[:, f * 256 : (f + 1) * 256] = jnp.where(
            c == 0, fc1[:, f * 512 : f * 512 + 256], fc1[:, f * 512 + 256 : (f + 1) * 512]
        )


def vectors_kernel(place_ref, packed, *outs):
    c = place_ref[0]

    def row(f, k):
        return packed[f, k : k + 1, :].astype(F32)

    for out, k in zip(outs[:6], (0, 1, 4, 5, 6, 7)):
        for f in range(8):
            out[:, f * 128 : (f + 1) * 128] = row(f, k)
    for out, k in zip(outs[6:8], (2, 3)):
        for p in range(4):
            out[:, p * 128 : (p + 1) * 128] = lane_halves(c, row(2 * p, k), row(2 * p + 1, k))
    for f in range(8):
        for j in range(2):
            at = f * 256 + j * 128
            outs[8][:, at : at + 128] = jnp.where(c == 0, row(f, 8 + j), row(f, 10 + j))


def ring_add_kernel(place_ref, arrived, terms, out):
    total = (arrived[...].astype(F32) + terms[...].astype(F32)).astype(BF)
    out[...] = total.reshape(out.shape)


def ring_reduce(here, name, axis, terms, block, spot, piece, steps, last=None):
    pieces = jnp.stack([here.source(axis, s) for s in range(1, 5)]).astype(jnp.int32)
    lead = (None,) * 0

    def add(arrived, step):
        shape = piece if (step < 4 or last is None) else last
        whole = [d for d in piece]
        spec = pl.BlockSpec((piece[0] // steps,) + piece[1:], lambda i, at: (i,) + (0,) * (len(piece) - 1))
        if step < 4 or last is None:
            out_spec = spec
        else:
            out_spec = pl.BlockSpec((last[0], None) + last[2:], lambda i, at: (0, i) + (0,) * (len(last) - 2))
        grid_spec = pltpu.PrefetchScalarGridSpec(
            num_scalar_prefetch=1,
            grid=(steps,),
            in_specs=[spec, pl.BlockSpec(block, lambda i, at: spot(i, at[0]))],
            out_specs=out_spec,
        )
        size = 2
        for d in piece:
            size *= d
        return pl.pallas_call(
            ring_add_kernel,
            grid_spec=grid_spec,
            out_shape=struct(shape, BF),
            name=name,
            compiler_params=pltpu.CompilerParams(vmem_limit_bytes=24 << 20),
            cost_estimate=pl.CostEstimate(flops=0, bytes_accessed=3 * size, transcendentals=0),
        )(pieces[step - 1 : step], arrived, terms)

    def first():
        grid_spec = pltpu.PrefetchScalarGridSpec(
            num_scalar_prefetch=1,
            grid=(steps,),
            in_specs=[pl.BlockSpec(block, lambda i, at: spot(i, at[0]))],
            out_specs=pl.BlockSpec(
                (piece[0] // steps,) + piece[1:], lambda i, at: (i,) + (0,) * (len(piece) - 1)
            ),
        )

        def kernel(at_ref, source, out):
            out[...] = source[...].reshape(out.shape)

        size = 2
        for d in piece:
            size *= d
        return pl.pallas_call(
            kernel,
            grid_spec=grid_spec,
            out_shape=struct(piece, BF),
            name=name,
            compiler_params=pltpu.CompilerParams(vmem_limit_bytes=24 << 20),
            cost_estimate=pl.CostEstimate(flops=0, bytes_accessed=2 * size, transcendentals=0),
        )(pieces[:1], terms)

    total = first()
    for step in range(2, 5):
        total = add(permute(total, ring_move(axis)), step)
    return total


def sum_kernel(place_ref, blocks, out):
    out[...] = jnp.sum(blocks[...].astype(F32), axis=0).astype(out.dtype)


def sum_blocks(here, name, blocks, steps=2):
    k, r, n = blocks.shape
    return kernel_call(
        sum_kernel,
        name,
        struct((r, n), BF),
        moved=2 * (k + 1) * r * n,
        grid=(steps,),
        in_specs=[SMEM, pl.BlockSpec((k, r // steps, n), lambda i: (0, i, 0))],
        out_specs=pl.BlockSpec((r // steps, n), lambda i: (i, 0)),
    )(here.table, blocks)


def split_kernel(place_ref, blocks, kept, sent):
    total = jnp.sum(blocks[...].astype(F32), axis=0)
    half = total.shape[0] // 2
    low, high = total[:half], total[half:]
    flag = place_ref[1]
    kept[...] = jnp.where(flag == 0, low, high)
    sent[...] = jnp.where(flag == 0, high, low).astype(BF)


def sum_and_halve(name, flag, blocks, move):
    k, r, n = blocks.shape
    whole = pl.BlockSpec((r // 2, n), lambda: (0, 0))
    kept, sent = kernel_call(
        split_kernel,
        name,
        [struct((r // 2, n), F32), struct((r // 2, n), BF)],
        moved=2 * (k + 2) * r * n,
        in_specs=[SMEM, pl.BlockSpec((k, r, n), lambda: (0, 0, 0))],
        out_specs=[whole, whole],
    )(jnp.stack([flag, flag]).astype(jnp.int32), blocks)
    return kept + permute(sent, move).astype(F32)


def all_to_all(value, axis, groups=None):
    return lax.all_to_all(value, axis, 0, 0, tiled=True, axis_index_groups=groups)


def gather_slices(here, name, piece):
    r, n = piece.shape
    pair = assemble(
        name + "_lo",
        [piece, permute(piece, flip_lo)],
        [here.lo, 1 - here.lo],
        (2, r, n),
        lambda o, s: o.at[s],
    )
    full = assemble(
        name + "_z",
        ring_blocks(pair, "z"),
        [here.source("z", s) for s in range(4)],
        (4, 2, r, n),
        lambda o, s: o.at[s],
    )
    other = permute(full, swap_core)
    return jnp.where(here.c == 0, full, other), jnp.where(here.c == 0, other, full)


def butterfly(value):
    for move in (
        lambda x, y, z, c: (x ^ 1, y, z, c),
        lambda x, y, z, c: (3 - x, y, z, c),
        flip_lo,
        flip_hi,
        lambda x, y, z, c: (x, y, z ^ 1, c),
        lambda x, y, z, c: (x, y, 3 - z, c),
        swap_core,
    ):
        value = value + permute(value, move)
    return value


RATE = 0.51
ERFC = (
    0.28791757708249816,
    0.28415126012743,
    0.2790719172776486,
    0.055036978129087616,
    0.35846874221749475,
    -0.3591518512954867,
    0.09450494290776956,
)


def hidden_kernel(rows, weight, shift, hidden, slope):
    u = jnp.dot(rows[...], weight[...], preferred_element_type=F32) + shift[...]
    bell = jnp.exp(-0.5 * u * u)
    t = 1.0 / (1.0 + (RATE * 0.5**0.5) * jnp.abs(u))
    tail = jnp.full_like(u, 0.5 * ERFC[-1])
    for coefficient in ERFC[-2::-1]:
        tail = tail * t + 0.5 * coefficient
    tail = tail * t * bell
    area = jnp.where(u >= 0, 1.0 - tail, tail)
    hidden[...] = (u * area).astype(BF)
    slope[...] = (area + u * bell * 0.3989422804014327).astype(BF)


def hidden_layer(rows, weight, shift):
    m, k = rows.shape
    n = weight.shape[1]
    cols = 256
    out = pl.BlockSpec((m, cols), lambda i: (0, i))
    return kernel_call(
        hidden_kernel,
        "hidden_layer",
        [struct((m, n), BF)] * 2,
        flops=2 * m * n * k,
        moved=2 * (m * k + k * n + 2 * m * n),
        grid=(n // cols,),
        in_specs=[
            pl.BlockSpec((m, k), lambda i: (0, 0)),
            pl.BlockSpec((k, cols), lambda i: (0, i)),
            pl.BlockSpec((1, cols), lambda i: (0, i)),
        ],
        out_specs=[out, out],
    )(rows, weight, shift)


def d_pre_kernel(grad, weight, slope, d_pre, total):
    back = dot_nt(grad[...], weight[...]) * slope[...].astype(F32)
    low = back.astype(BF)
    d_pre[...] = low
    total[...] = jnp.sum(low.astype(F32), axis=0, keepdims=True)


def hidden_back(grad, weight, slope):
    m, k = grad.shape
    n = weight.shape[0]
    cols = 256
    out = pl.BlockSpec((m, cols), lambda i: (0, i))
    return kernel_call(
        d_pre_kernel,
        "hidden_back",
        [struct((m, n), BF), struct((1, n), F32)],
        flops=2 * m * n * k,
        moved=2 * (m * k + k * n + 2 * m * n),
        grid=(n // cols,),
        in_specs=[
            pl.BlockSpec((m, k), lambda i: (0, 0)),
            pl.BlockSpec((cols, k), lambda i: (i, 0)),
            out,
        ],
        out_specs=[out, pl.BlockSpec((1, cols), lambda i: (0, i))],
    )(grad, weight, slope)


def head_pair(packed, query_shift, value_shift, p):
    at = slice(p * 128, (p + 1) * 128)
    query = (packed[:, p * 128 : (p + 1) * 128] + query_shift[:, at]).astype(BF)
    key = packed[:, 512 + p * 128 : 512 + (p + 1) * 128].astype(BF)
    value = (packed[:, 1024 + p * 128 : 1024 + (p + 1) * 128] + value_shift[:, at]).astype(BF)
    return query, key, value


SCALE = HEAD_DIM ** (-0.5)


def softmax_of(query, key, blocked, first, e):
    only = jnp.where(first if e == 0 else ~first, query, jnp.zeros_like(query))
    scores = dot_nt(only, key) * SCALE + blocked
    exps = jnp.exp(scores - jnp.max(scores, axis=-1, keepdims=True))
    return exps * (1.0 / jnp.sum(exps, axis=-1, keepdims=True))


def attention_kernel(packed, query_shift, value_shift, blocked, mixed):
    first = lax.broadcasted_iota(jnp.int32, (BLOCK, 128), 1) < 64
    for p in range(4):
        query, key, value = head_pair(packed, query_shift, value_shift, p)
        parts = [
            dot(softmax_of(query, key, blocked[...], first, e).astype(BF), value) for e in range(2)
        ]
        mixed[:, p * 128 : (p + 1) * 128] = jnp.where(first, parts[0], parts[1]).astype(BF)


def attention(packed, query_shift, value_shift, blocked):
    rows = packed.shape[0]
    shift = pl.BlockSpec((1, 512), lambda i: (0, 0))
    return kernel_call(
        attention_kernel,
        "attention",
        struct((rows, 512), BF),
        flops=4 * rows * BLOCK * 512,
        moved=4 * rows * 1536 + 2 * rows * 512 + 4 * rows * BLOCK,
        grid=(rows // BLOCK,),
        in_specs=[
            pl.BlockSpec((BLOCK, 1536), lambda i: (i, 0)),
            shift,
            shift,
            pl.BlockSpec((None, BLOCK, BLOCK), lambda i: (i, 0, 0)),
        ],
        out_specs=pl.BlockSpec((BLOCK, 512), lambda i: (i, 0)),
    )(packed, query_shift, value_shift, blocked)


def attention_back_kernel(packed, query_shift, value_shift, blocked, d_mixed, d_packed, total):
    first = lax.broadcasted_iota(jnp.int32, (BLOCK, 128), 1) < 64

    @pl.when(pl.program_id(0) == 0)
    def _():
        total[...] = jnp.zeros_like(total)

    for p in range(4):
        query, key, value = head_pair(packed, query_shift, value_shift, p)
        grad = d_mixed[:, p * 128 : (p + 1) * 128]
        d_query, d_key, d_value = [], [], []
        for e in range(2):
            probs = softmax_of(query, key, blocked[...], first, e)
            only = jnp.where(first if e == 0 else ~first, grad, jnp.zeros_like(grad))
            d_probs = dot_nt(only, value)
            d_scores = probs * (d_probs - jnp.sum(probs * d_probs, axis=-1, keepdims=True))
            d_scores = d_scores.astype(BF)
            d_value.append(dot_tn(probs.astype(BF), only))
            d_query.append(dot(d_scores, key))
            d_key.append(dot_tn(d_scores, query))
        parts = (
            jnp.where(first, d_query[0], d_query[1]) * SCALE,
            jnp.where(first, d_key[0], d_key[1]) * SCALE,
            d_value[0] + d_value[1],
        )
        for k, part in enumerate(parts):
            at = slice(k * 512 + p * 128, k * 512 + (p + 1) * 128)
            low = part.astype(BF)
            d_packed[:, at] = low
            total[:, at] += jnp.sum(low.astype(F32), axis=0, keepdims=True)


def attention_back(packed, query_shift, value_shift, blocked, d_mixed):
    rows = packed.shape[0]
    shift = pl.BlockSpec((1, 512), lambda i: (0, 0))
    return kernel_call(
        attention_back_kernel,
        "attention_back",
        [struct((rows, 1536), BF), struct((1, 1536), F32)],
        flops=10 * rows * BLOCK * 512,
        moved=4 * rows * 1536 + 2 * rows * 2048 + 4 * rows * BLOCK,
        grid=(rows // BLOCK,),
        in_specs=[
            pl.BlockSpec((BLOCK, 1536), lambda i: (i, 0)),
            shift,
            shift,
            pl.BlockSpec((None, BLOCK, BLOCK), lambda i: (i, 0, 0)),
            pl.BlockSpec((BLOCK, 512), lambda i: (i, 0)),
        ],
        out_specs=[
            pl.BlockSpec((BLOCK, 1536), lambda i: (i, 0)),
            pl.BlockSpec((1, 1536), lambda i: (0, 0)),
        ],
    )(packed, query_shift, value_shift, blocked, d_mixed)


def dot(left, right):
    return jnp.dot(left, right, preferred_element_type=F32)


def dot_nt(left, right):
    return lax.dot_general(left, right, (((1,), (1,)), ((), ())), preferred_element_type=F32)


def dot_tn(left, right):
    return lax.dot_general(left, right, (((0,), (0,)), ((), ())), preferred_element_type=F32)


def normalize(values):
    center = values - jnp.mean(values, axis=-1, keepdims=True)
    rstd = lax.rsqrt(jnp.mean(center * center, axis=-1, keepdims=True) + EPS)
    return center * rstd, rstd


def normalize_back(grad, yhat, rstd, gain):
    t = grad * gain
    return rstd * (
        t
        - jnp.mean(t, axis=-1, keepdims=True)
        - yhat * jnp.mean(t * yhat, axis=-1, keepdims=True)
    )


TILE = 96


def middle_kernel(part, other, tokens, keep, shift, gain, bias, middle, normed):
    attended = part[...].astype(F32) + other[...].astype(F32) + shift[...]
    rows = tokens[...].astype(F32) + keep[...] * attended
    middle[...] = rows
    yhat, _ = normalize(rows)
    normed[...] = (yhat * gain[...] + bias[...]).astype(BF)


def row_specs(count, width=1024):
    half = count // 2
    return (
        pl.BlockSpec((TILE, width), lambda i: (i, 0)),
        pl.BlockSpec((TILE, width), lambda i: (lax.rem(i + half, count), 0)),
        pl.BlockSpec((TILE, 1), lambda i: (i, 0)),
        pl.BlockSpec((1, width), lambda i: (0, 0)),
    )


def middle_layer(part, other, tokens, keep, shift, gain, bias):
    rows = part.shape[0]
    tile, swapped, column, vector = row_specs(rows // TILE)
    return kernel_call(
        middle_kernel,
        "middle_layer",
        [struct((rows, 1024), F32), struct((rows, 1024), BF)],
        moved=rows * 1024 * 12,
        grid=(rows // TILE,),
        in_specs=[tile, swapped, tile, column, vector, vector, vector],
        out_specs=[tile, tile],
    )(part, other, tokens, keep, shift, gain, bias)


def middle_back_kernel(part, other, middle, cot, keep, share, gain, d_middle, d_attended, sums):
    step = pl.program_id(0)
    grad = part[...].astype(F32) + other[...].astype(F32)
    yhat, rstd = normalize(middle[...])
    incoming = cot[...].astype(F32) * share[...]
    d_rows = incoming + normalize_back(grad, yhat, rstd, gain[...])
    d_middle[...] = d_rows
    low = (keep[...] * d_rows).astype(BF)
    d_attended[...] = low
    branch = (keep[...] * incoming).astype(BF)

    @pl.when(step == 0)
    def _():
        sums[...] = jnp.zeros_like(sums)

    @pl.when(step < pl.num_programs(0) // 2)
    def _():
        for k, v in enumerate((grad * yhat, grad, low.astype(F32), branch.astype(F32))):
            sums[k : k + 1, :] += jnp.sum(v, axis=0, keepdims=True)


def middle_back(part, other, middle, cot, keep, share, gain):
    rows = part.shape[0]
    tile, swapped, column, vector = row_specs(rows // TILE)
    return kernel_call(
        middle_back_kernel,
        "middle_back",
        [struct((rows, 1024), F32), struct((rows, 1024), BF), struct((8, 1024), F32)],
        moved=rows * 1024 * 16,
        grid=(rows // TILE,),
        in_specs=[tile, swapped, tile, tile, column, column, vector],
        out_specs=[tile, tile, pl.BlockSpec((8, 1024), lambda i: (0, 0))],
    )(part, other, middle, cot, keep, share, gain)


def input_back_kernel(part, other, tokens, d_middle, gain, grad_rows, sums):
    grad = part[...].astype(F32) + other[...].astype(F32)
    yhat, rstd = normalize(tokens[...].astype(F32))
    grad_rows[...] = (d_middle[...] + normalize_back(grad, yhat, rstd, gain[...])).astype(BF)

    @pl.when(pl.program_id(0) == 0)
    def _():
        sums[...] = jnp.zeros_like(sums)

    for k, v in enumerate((grad * yhat, grad)):
        sums[k : k + 1, :] += jnp.sum(v, axis=0, keepdims=True)


def input_back(part, other, tokens, d_middle, gain):
    rows = part.shape[0]
    tile, _, _, vector = row_specs(rows // TILE)
    return kernel_call(
        input_back_kernel,
        "input_back",
        [struct((rows, 1024), BF), struct((8, 1024), F32)],
        moved=rows * 1024 * 12,
        grid=(rows // TILE,),
        in_specs=[tile, tile, tile, tile, vector],
        out_specs=[tile, pl.BlockSpec((8, 1024), lambda i: (0, 0))],
    )(part, other, tokens, d_middle, gain)


def body(
    tokens,
    norm1_gain,
    norm1_bias,
    qkv_weight,
    query_bias,
    value_bias,
    out_weight,
    out_bias,
    norm2_gain,
    norm2_bias,
    fc1_weight,
    fc1_bias,
    fc2_weight,
    fc2_bias,
    cotangent,
    group_of,
    keep_mask,
    group_tokens,
):
    here = Where()
    own_rows, width = tokens.shape
    c = here.c
    here.table = jnp.stack([c, here.lo]).astype(jnp.int32)

    packed_vectors = jnp.concatenate(
        [norm1_gain, norm1_bias, query_bias, value_bias, out_bias, norm2_gain, norm2_bias, fc2_bias, fc1_bias]
    ).reshape(12, 128)
    packed_vectors = jnp.concatenate([packed_vectors, jnp.zeros((4, 128), BF)])
    qkv_half, fc1_half = kernel_call(
        halves_kernel,
        "halves",
        [struct((128, 1536), BF), struct((128, 2048), BF)],
        moved=2 * 128 * 7168 * 2,
        in_specs=[SMEM] + [pl.BlockSpec(memory_space=pltpu.VMEM)] * 2,
    )(here.table, qkv_weight, fc1_weight)
    out_half = pick(out_weight.reshape(2, 64, 1024), c)
    fc2_quarter = pick(fc2_weight.reshape(8, 64, 1024), 4 * c + here.z)
    fc1_part = pick(fc1_half.reshape(2, 64, 2048), here.lo)

    vectors = gather_x(here, "vectors_x", with_other_hi(here, "vectors_y", packed_vectors))
    qkv_all = gather_x(here, "qkv_x", with_other_hi(here, "qkv_y", qkv_half)).reshape(1024, 1536)
    fc2_slab = gather_x(here, "fc2_x", with_other_hi(here, "fc2_y", fc2_quarter))
    fc2_all = assemble(
        "fc2_z",
        ring_blocks(fc2_slab, "z"),
        [here.source("z", s) for s in range(4)],
        (2, 4, 4, 64, 1024),
        lambda o, s: o.at[:, :, s],
    ).reshape(2048, 1024)
    fc1_row = assemble(
        "fc1_x",
        ring_blocks(fc1_part, "x"),
        [here.source("x", s) for s in range(4)],
        (4, 64, 2048),
        lambda o, s: o.at[s],
    )
    fc1_all = assemble(
        "fc1_y",
        ring_blocks(fc1_row, "y"),
        [here.source("y", s) for s in range(4)],
        (2, 4, 2, 64, 2048),
        lambda o, s: o.at[s // 2, :, lax.rem(s, 2)],
    ).reshape(1024, 2048)
    out_all = gather_x(here, "out_x", with_other_hi(here, "out_y", out_half)).reshape(512, 1024)
    rows_low = jnp.concatenate([tokens, permute(tokens, swap_core)])
    keep = jnp.concatenate([keep_mask, permute(keep_mask, swap_core)])
    cot = jnp.concatenate([cotangent, permute(cotangent, swap_core)])

    (
        gain_one,
        shift_one,
        out_shift,
        gain_two,
        shift_two,
        fc2_shift,
        query_shift,
        value_shift,
        fc1_shift,
    ) = kernel_call(
        vectors_kernel,
        "vectors",
        [struct((1, 1024), F32)] * 6 + [struct((1, 512), F32)] * 2 + [struct((1, 2048), F32)],
        moved=1 << 16,
        in_specs=[SMEM, pl.BlockSpec(memory_space=pltpu.VMEM)],
    )(here.table, vectors.reshape(8, 16, 128))

    groups = jnp.stack([pick(group_of, here.dp), pick(group_of, here.dp + here.sign)])
    counts = group_tokens.astype(F32)
    share = counts / jnp.sum(counts)
    share = jnp.where(groups == 1, share[1], share[0])
    share_col = jnp.repeat(share, own_rows)[:, None]
    mask_col = keep.astype(F32)[:, None]
    row_count = 2 * own_rows
    blocks = row_count // BLOCK
    block_group = jnp.repeat(groups, blocks // 2)
    image = jnp.where(
        block_group[:, None] == 1, 0, jnp.arange(BLOCK, dtype=jnp.int32)[None] // SLOT_S
    )
    allowed = (image[:, :, None] == image[:, None, :]) & (keep.reshape(blocks, 1, BLOCK) == 1)
    blocked = jnp.where(allowed, F32(0), F32(-1e30))
    incoming = cot.astype(F32) * share_col
    d_branch = (mask_col * incoming).astype(BF)

    yhat_one, _ = normalize(rows_low.astype(F32))
    normed = (yhat_one * gain_one + shift_one).astype(BF)
    packed = dot(normed, qkv_all)
    mixed = attention(packed, query_shift, value_shift, blocked)
    attended = dot(mixed, out_all).astype(BF)
    middle, normed_two = middle_layer(
        attended, permute(attended, swap_core), rows_low, mask_col, out_shift, gain_two, shift_two
    )
    hidden, slope = hidden_layer(normed_two, fc1_all, fc1_shift)

    d_pre, fc1_bias_sum = hidden_back(d_branch, fc2_all, slope)
    d_normed_two = dot_nt(d_pre, fc1_all).astype(BF)
    d_middle, d_attended, middle_sums = middle_back(
        d_normed_two, permute(d_normed_two, swap_core), middle, cot, mask_col, share_col, gain_two
    )
    grad_fc2 = dot_tn(hidden, d_branch).astype(BF)
    grad_fc1 = dot_tn(normed_two, d_pre).astype(BF)
    d_mixed = dot_nt(d_attended, out_all).astype(BF)
    d_packed, packed_sums = attention_back(packed, query_shift, value_shift, blocked, d_mixed)
    grad_out = dot_tn(mixed, d_attended).astype(BF)
    grad_qkv = dot_tn(normed, d_packed).astype(BF)

    d_normed_sent = permute(dot_nt(d_packed[own_rows:], qkv_all).astype(BF), swap_core)
    d_normed_own = dot_nt(d_packed[:own_rows], qkv_all).astype(BF)
    input_grad, input_sums = input_back(d_normed_own, d_normed_sent, tokens, d_middle, gain_one)

    branch_sent = permute(dot(hidden[own_rows:], fc2_all).astype(BF), swap_core)
    branch = dot(hidden[:own_rows], fc2_all) + branch_sent.astype(F32) + fc2_shift
    block_out = (middle[:own_rows] + mask_col[:own_rows] * branch).astype(BF)

    def own_sum(v):
        return v.reshape(8, 1, 128)

    def half_sum(v):
        n = v.size // 8
        terms = v.reshape(8, 1, n)
        return jnp.concatenate(
            [jnp.where(c == 0, terms, 0.0), jnp.where(c == 0, 0.0, terms)], axis=1
        ).reshape(8, n // 64, 128)

    vector_terms = jnp.concatenate(
        [
            own_sum(input_sums[0]),
            own_sum(input_sums[1]),
            half_sum(packed_sums[0, :512]),
            half_sum(packed_sums[0, 1024:]),
            own_sum(middle_sums[2]),
            own_sum(middle_sums[0]),
            own_sum(middle_sums[1]),
            own_sum(middle_sums[3]),
            half_sum(fc1_bias_sum),
        ],
        axis=1,
    )
    vector_sums = pick(butterfly(vector_terms), here.fs)

    fc2_sum = ring_reduce(
        here,
        "fc2_ring",
        "z",
        grad_fc2.reshape(8, 4, 64, 1024),
        (4, None, 64, 1024),
        lambda i, t: (i, t, 0, 0),
        (8, 64, 1024),
        2,
    )
    fc2_sum = sum_and_halve("fc2_sum", here.lo, all_to_all(fc2_sum, "fsdp"), flip_lo).astype(BF)

    fc1_sum = ring_reduce(
        here,
        "fc1_ring",
        "x",
        grad_fc1.reshape(2, 4, 128, 2048),
        (1, None, 128, 2048),
        lambda i, t: (i, t, 0, 0),
        (2, 128, 2048),
        2,
        last=(4, 2, 32, 2048),
    )
    fc1_sum = all_to_all(fc1_sum, "dp", Z_GROUPS).reshape(4, 64, 2048)
    fc1_sum = sum_and_halve("fc1_sum", here.hi, fc1_sum, flip_hi)
    fc1_sum = sum_and_halve("fc1_lo", here.lo, fc1_sum.astype(BF)[None], flip_lo).astype(BF)

    out_sum = all_to_all(grad_out.reshape(8, 64, 1024), "fsdp")
    out_sum = sum_and_halve("out_sum", here.lo, out_sum, flip_lo).astype(BF).reshape(4, 8, 1024)
    out_sum = sum_blocks(here, "out_z", all_to_all(out_sum, "dp", Z_GROUPS), 1)

    qkv_sum = ring_reduce(
        here,
        "qkv_ring",
        "y",
        grad_qkv.reshape(2, 4, 2, 64, 1536),
        (None, 2, None, 64, 1536),
        lambda i, t: (t // 2, i, lax.rem(t, 2), 0, 0),
        (4, 64, 1536),
        2,
    )
    qkv_sum = sum_blocks(here, "qkv_sum", all_to_all(qkv_sum, "fsdp", X_GROUPS)).reshape(4, 16, 1536)
    qkv_sum = sum_blocks(here, "qkv_z", all_to_all(qkv_sum, "dp", Z_GROUPS), 1)

    mlp_piece = jnp.concatenate([fc2_sum, fc1_sum.reshape(32, 1024)])
    mlp_full = jnp.stack(gather_slices(here, "mlp", mlp_piece))
    grad_fc2_weight = mlp_full[:, :, :, :32].reshape(512, 1024).astype(F32)
    grad_fc1_weight = (
        mlp_full[:, :, :, 32:]
        .reshape(2, 128, 8, 256)
        .transpose(1, 2, 0, 3)
        .reshape(128, 4096)
        .astype(F32)
    )
    out_full = jnp.stack(gather_slices(here, "out", out_sum))
    grad_out_weight = jnp.swapaxes(out_full, 1, 2).reshape(128, 1024).astype(F32)
    qkv_full = jnp.stack(gather_slices(here, "qkv", qkv_sum))
    grad_qkv_weight = (
        jnp.swapaxes(qkv_full, 1, 2)
        .reshape(2, 128, 24, 64)
        .transpose(1, 2, 0, 3)
        .reshape(128, 3072)
        .astype(F32)
    )
    return (
        block_out,
        input_grad,
        vector_sums[0],
        vector_sums[1],
        grad_qkv_weight,
        vector_sums[2],
        vector_sums[3],
        grad_out_weight,
        vector_sums[4],
        vector_sums[5],
        vector_sums[6],
        grad_fc1_weight,
        vector_sums[8:12].reshape(512),
        grad_fc2_weight,
        vector_sums[7],
    )


def solution(mesh):
    rows, cols, both = P("fsdp", None), P("fsdp"), ("dp", "fsdp")
    in_specs = (
        P(both, None),
        cols,
        cols,
        rows,
        cols,
        cols,
        rows,
        cols,
        cols,
        cols,
        rows,
        cols,
        rows,
        cols,
        P(both, None),
        P(),
        P(both),
        P(),
    )
    out_specs = (
        P(both, None),
        P(both, None),
        cols,
        cols,
        rows,
        cols,
        cols,
        rows,
        cols,
        cols,
        cols,
        rows,
        cols,
        rows,
        cols,
    )
    return jax.shard_map(body, mesh=mesh, in_specs=in_specs, out_specs=out_specs, check_vma=False)
```

```python
import functools

import jax
import jax.numpy as jnp
from jax import lax
from jax.experimental import pallas as pl
from jax.experimental.pallas import tpu as pltpu
from jax.sharding import PartitionSpec as P

HEAD_DIM = 64
SLOT_S = 64
SLOT_L = 192
BLOCK = 192
EPS = 1e-06
AXES = ("dp", "fsdp")
BF = jnp.bfloat16
F32 = jnp.float32

Z_GROUPS = [[lo * 8 + 2 * z + c for z in range(4)] for lo in range(2) for c in range(2)]
SLICE_GROUPS = [[lo * 8 + 2 * z + c for lo in range(2) for z in range(4)] for c in range(2)]
X_GROUPS = [[0, 1, 2, 3], [4, 5, 6, 7]]


def place(linear):
    dp, fs = divmod(linear, 8)
    return fs % 4, (fs // 4) * 2 + dp // 8, (dp // 2) % 4, dp % 2


def linear_of(x, y, z, c):
    x, y, z = x % 4, y % 4, z % 4
    return (((y % 2) * 4 + z) * 2 + c) * 8 + (y // 2) * 4 + x


def permute(value, move):
    return lax.ppermute(
        value, AXES, [(l, linear_of(*move(*place(l)))) for l in range(128)]
    )


def ring_move(axis):
    def move(x, y, z, c):
        s = 1 - 2 * c
        return (x + s * (axis == "x"), y + s * (axis == "y"), z + s * (axis == "z"), c)

    return move


def swap_core(x, y, z, c):
    return x, y, z, 1 - c


def flip_hi(x, y, z, c):
    return x, 3 - y, z, c


def flip_lo(x, y, z, c):
    return x, y ^ 1, z, c


class Where:
    def __init__(self):
        dp, fs = lax.axis_index("dp"), lax.axis_index("fsdp")
        self.dp, self.fs = dp, fs
        self.c = dp % 2
        self.z = (dp // 2) % 4
        self.lo = dp // 8
        self.x = fs % 4
        self.hi = fs // 4
        self.y = self.hi * 2 + self.lo
        self.sign = 1 - 2 * self.c

    def along(self, axis):
        return {"x": self.x, "y": self.y, "z": self.z}[axis]

    def source(self, axis, step):
        return lax.rem(self.along(axis) - self.sign * step + 8, 4)

    def make_table(self):
        self.table = jnp.stack([self.c, self.z, self.lo, self.hi, self.x, self.y]).astype(jnp.int32)


C, Z, LO, HI, X, Y = range(6)


def source_in(table, at, step):
    return lax.rem(table[at] - (1 - 2 * table[C]) * step + 8, 4)


def pick(stacked, index, axis=0):
    return lax.dynamic_index_in_dim(stacked, index, axis, keepdims=False)


def ring_gather(here, value, axis, buffer, put):
    for step in range(4):
        if step:
            value = permute(value, ring_move(axis))
        buffer = put(buffer, value, here.source(axis, step))
    return buffer


def ring_reduce(here, axis, term):
    total = term(here.source(axis, 1))
    for step in range(2, 5):
        total = permute(total, ring_move(axis))
        total = (total.astype(F32) + term(here.source(axis, step)).astype(F32)).astype(BF)
    return total


def ring_blocks(value, axis):
    blocks = [value]
    for _ in range(3):
        blocks.append(permute(blocks[-1], ring_move(axis)))
    return blocks


ANY = pl.BlockSpec(memory_space=pl.ANY)
SMEM = pl.BlockSpec(memory_space=pltpu.SMEM)
VMEM = pl.BlockSpec(memory_space=pltpu.VMEM)


def kernel_call(
    kernel, name, out_shape, in_specs, us=1, vmem=16 << 20, pinned=False, late=(), **kwargs
):
    count = len(in_specs)

    def body(*refs):
        kernel(*refs[:count], *refs[count + len(late) :])

    call = pl.pallas_call(
        body,
        out_shape=out_shape,
        in_specs=list(in_specs) + [ANY] * len(late),
        name=name,
        compiler_params=pltpu.CompilerParams(vmem_limit_bytes=vmem),
        cost_estimate=pl.CostEstimate(
            flops=int(us * 1.15e9), bytes_accessed=1 << 16, transcendentals=0
        ),
        **kwargs,
    )

    def run(*args):
        return call(
            *(
                pltpu.with_memory_space_constraint(a, pltpu.HBM) if pinned and a.dtype == BF else a
                for a in args
            ),
            *late,
        )

    return run


def struct(shape, dtype):
    return jax.ShapeDtypeStruct(shape, dtype)


def assemble(here, name, parts, shape, target, source=lambda ref: ref, late=()):
    def kernel(table, *refs):
        ins, out, sems = refs[: len(parts)], refs[len(parts)], refs[len(parts) + 1]
        copies = [
            pltpu.make_async_copy(source(ins[n]), target(out, table, n), sems.at[n])
            for n in range(len(parts))
        ]
        for copy in copies:
            copy.start()
        for copy in copies:
            copy.wait()

    return kernel_call(
        kernel,
        name,
        struct(shape, BF),
        in_specs=[SMEM] + [ANY] * len(parts),
        us=2.5,
        late=late,
        out_specs=VMEM,
        scratch_shapes=[pltpu.SemaphoreType.DMA((len(parts),))],
    )(here.table, *parts)


def lane_halves(c, left, right):
    first = lax.broadcasted_iota(jnp.int32, left.shape, 1) < 64
    low = jnp.where(first, left, pltpu.roll(right, 64, 1))
    high = jnp.where(first, pltpu.roll(left, 64, 1), right)
    return jnp.where(c == 0, low, high)


def prepare_kernel(place_ref, qkv, fc1, fc2, out, *refs):
    vectors, (qkv_rep, fc1_rep, fc2_half, out_half) = refs[:9], refs[9:]
    c, z, lo = place_ref[0], place_ref[1], place_ref[2]
    rows = pl.ds(pl.multiple_of(z * 32, 32), 32)
    for g in range(12):
        left = qkv[rows, g * 256 : g * 256 + 128].astype(F32)
        right = qkv[rows, g * 256 + 128 : g * 256 + 256].astype(F32)
        half = lane_halves(c, left, right).astype(BF)
        for d in range(8):
            qkv_rep[d, :, g * 128 : (g + 1) * 128] = half
    packed = [ref[...].astype(F32).reshape(-1, 128) for ref in vectors]
    packed = jnp.concatenate(packed + [jnp.zeros((20, 128), F32)]).astype(BF)
    for d in range(8):
        qkv_rep[d, :, 1536:] = packed
    rows = pl.ds(pl.multiple_of(lo * 64, 64), 64)
    for f in range(8):
        half = jnp.where(
            c == 0, fc1[rows, f * 512 : f * 512 + 256], fc1[rows, f * 512 + 256 : (f + 1) * 512]
        )
        for d in range(4):
            fc1_rep[d, :, f * 256 : (f + 1) * 256] = half
    fc2_half[...] = fc2[pl.ds(pl.multiple_of(c * 256, 256), 256), :]
    out_half[...] = out[pl.ds(pl.multiple_of(c * 64, 64), 64), :]


def vectors_kernel(place_ref, packed, *outs):
    c = place_ref[0]
    rows = [packed[f].astype(F32) for f in range(8)]

    def row(f, k):
        return rows[f][k : k + 1, :]

    for out, k in zip(outs[:6], (0, 1, 4, 5, 6, 7)):
        for f in range(8):
            out[:, f * 128 : (f + 1) * 128] = row(f, k)
    for out, k in zip(outs[6:8], (2, 3)):
        for p in range(4):
            out[:, p * 128 : (p + 1) * 128] = lane_halves(c, row(2 * p, k), row(2 * p + 1, k))
    for f in range(8):
        for j in range(2):
            at = f * 256 + j * 128
            outs[8][:, at : at + 128] = jnp.where(c == 0, row(f, 8 + j), row(f, 10 + j))


def vector_terms_kernel(place_ref, input_sums, packed_sums, middle_sums, fc1_sums, out):
    c = place_ref[0]
    first = lax.broadcasted_iota(jnp.int32, (1, 128), 1) < 64
    zero = jnp.zeros((1, 128), F32)
    out[...] = jnp.zeros_like(out)
    whole = (
        (0, input_sums, 0),
        (1, input_sums, 1),
        (4, middle_sums, 2),
        (5, middle_sums, 0),
        (6, middle_sums, 1),
        (7, middle_sums, 3),
    )
    for f in range(8):
        for k, ref, r in whole:
            out[f, k : k + 1, :] = ref[r : r + 1, f * 128 : (f + 1) * 128]
        for j in range(4):
            at = f * 256 + (j % 2) * 128
            out[f, 8 + j : 9 + j, :] = jnp.where(c == j // 2, fc1_sums[:, at : at + 128], zero)
    for k, base in ((2, 0), (3, 1024)):
        for p in range(4):
            pair = packed_sums[:, base + p * 128 : base + (p + 1) * 128]
            turned = pltpu.roll(pair, 64, 1)
            for e in range(2):
                low = jnp.where(first, pair if e == 0 else turned, zero)
                high = jnp.where(first, zero, turned if e == 0 else pair)
                out[2 * p + e, k : k + 1, :] = jnp.where(c == 0, low, high)


def grad_kernel(left, right, out):
    out[...] = dot_tn(left[...], right[...]).astype(BF).reshape(out.shape)


def grad_fc2_terms(hidden, d_branch, late):
    m = hidden.shape[0]
    return kernel_call(
        grad_kernel,
        "grad_fc2",
        struct((4, 4, 2, 64, 1024), BF),
        us=6,
        late=late,
        grid=(8,),
        in_specs=[
            pl.BlockSpec((m, 256), lambda i: (0, i)),
            pl.BlockSpec((m, 1024), lambda i: (0, 0)),
        ],
        out_specs=pl.BlockSpec(
            (4, None, None, 64, 1024), lambda i: (0, lax.rem(i, 4), i // 4, 0, 0)
        ),
    )(hidden, d_branch)


def grad_fc1_kernel(left, right, out):
    terms = dot_tn(left[...], right[...]).astype(BF)
    for x in range(2):
        for lo in range(2):
            at = (2 * x + lo) * 64
            out[lo, x] = terms[at : at + 64]


def grad_fc1_terms(normed, d_pre, late):
    m = normed.shape[0]
    return kernel_call(
        grad_fc1_kernel,
        "grad_fc1",
        struct((2, 2, 4, 64, 2048), BF),
        us=5,
        late=late,
        grid=(4,),
        in_specs=[
            pl.BlockSpec((m, 256), lambda i: (0, i)),
            pl.BlockSpec((m, 2048), lambda i: (0, 0)),
        ],
        out_specs=pl.BlockSpec(
            (None, 2, 2, 64, 2048), lambda i: (i // 2, 0, lax.rem(i, 2), 0, 0)
        ),
    )(normed, d_pre)


def ring_add_kernel(place_ref, arrived, terms, out):
    out[...] = (arrived[...].astype(F32) + terms[...].astype(F32)).astype(BF)


def ring_add(here, name, arrived, terms, at, step, late):
    k, r, n = arrived.shape
    block = pl.BlockSpec((1, r, n), lambda i, table: (i, 0, 0))

    def kernel(table, arrived_ref, terms_ref, *refs):
        ring_add_kernel(table, arrived_ref, terms_ref, refs[-1])

    return pl.pallas_call(
        kernel,
        grid_spec=pltpu.PrefetchScalarGridSpec(
            num_scalar_prefetch=1,
            grid=(k,),
            in_specs=[
                block,
                pl.BlockSpec(
                    (None, 1, r, n), lambda i, table: (source_in(table, at, step), i, 0, 0)
                ),
            ]
            + [ANY] * len(late),
            out_specs=block,
        ),
        out_shape=struct((k, r, n), BF),
        name=name,
        compiler_params=pltpu.CompilerParams(vmem_limit_bytes=16 << 20),
        cost_estimate=pl.CostEstimate(flops=2 << 30, bytes_accessed=1 << 16, transcendentals=0),
    )(here.table, arrived, terms, *late)


def halve_kernel(at, table, blocks, kept, sent):
    flag = table[at]
    kept[...] = blocks[flag].astype(F32)
    sent[...] = blocks[1 - flag]


def halve(here, name, at, blocks, move):
    _, r, n = blocks.shape
    kept, sent = kernel_call(
        functools.partial(halve_kernel, at),
        name,
        [struct((r, n), F32), struct((r, n), BF)],
        grid=(1,),
        in_specs=[SMEM, pl.BlockSpec((2, r, n), lambda i: (0, 0, 0))],
        out_specs=[pl.BlockSpec((r, n), lambda i: (0, 0))] * 2,
    )(here.table, blocks)
    return kept, permute(sent, move)


def merge_kernel(table, qkv, out, fc1, merged):
    qkv_sum = jnp.sum(qkv[...].astype(F32), axis=0)
    out_sum = jnp.sum(out[...].astype(F32), axis=0)
    here = pl.program_id(0) // 2 == table[LO]
    fc1_part = jnp.where(here, fc1[...], jnp.zeros(fc1.shape, BF))
    for k in range(2):
        rows = slice(k * 16, (k + 1) * 16)
        part = out_sum[k * 8 : (k + 1) * 8]
        merged[k, :16, :1536] = qkv_sum[rows].astype(BF)
        merged[k, :16, 1536:] = jnp.concatenate([part[:, :512], part[:, 512:]]).astype(BF)
        merged[k, 16:, :] = fc1_part[rows]


def merge(here, qkv, out, fc1, late):
    return kernel_call(
        merge_kernel,
        "merge",
        struct((8, 32, 2048), BF),
        us=1.5,
        late=late,
        grid=(4,),
        in_specs=[
            SMEM,
            pl.BlockSpec((8, 32, 1536), lambda i: (0, i, 0)),
            pl.BlockSpec((8, 16, 1024), lambda i: (0, i, 0)),
            pl.BlockSpec((32, 2048), lambda i: (lax.rem(i, 2), 0)),
        ],
        out_specs=pl.BlockSpec((2, 32, 2048), lambda i: (i, 0, 0)),
    )(here.table, qkv, out, fc1)


def pack_kernel(slices, fc2_kept, fc2_sent, packed):
    fc2 = (fc2_kept[...] + fc2_sent[...].astype(F32)).astype(BF)
    total = jnp.sum(slices[...].astype(F32), axis=0).astype(BF)
    for d in range(8):
        packed[d, :32, :] = total
        packed[d, 32:, :1024] = fc2[:16]
        packed[d, 32:, 1024:] = fc2[16:]


def unpack_kernel(place_ref, own, other, qkv, out, fc1, fc2):
    c = place_ref[0]
    low = jnp.where(c == 0, own[...], other[...]).astype(F32)
    high = jnp.where(c == 0, other[...], own[...]).astype(F32)
    for k, half in enumerate((low, high)):
        out[k, :, :512] = half[:8, 1536:]
        out[k, :, 512:] = half[8:16, 1536:]
        fc2[k, :16] = half[32:, :1024]
        fc2[k, 16:] = half[32:, 1024:]
        for f in range(8):
            at = f * 512 + k * 256
            fc1[:, at : at + 256] = half[16:32, f * 256 : (f + 1) * 256]
    first = lax.broadcasted_iota(jnp.int32, (16, 128), 1) < 64
    for p in range(12):
        left, right = low[:16, p * 128 : (p + 1) * 128], high[:16, p * 128 : (p + 1) * 128]
        qkv[:, p * 256 : p * 256 + 128] = jnp.where(first, left, pltpu.roll(right, 64, 1))
        qkv[:, p * 256 + 128 : (p + 1) * 256] = jnp.where(first, pltpu.roll(left, 64, 1), right)


def all_to_all(value, axis, groups=None):
    return lax.all_to_all(value, axis, 0, 0, tiled=True, axis_index_groups=groups)


def add_over(value, *moves):
    for move in moves:
        value = value + permute(value, move)
    return value


RATE = 0.51
ERFC = (
    0.28791757708249816,
    0.28415126012743,
    0.2790719172776486,
    0.055036978129087616,
    0.35846874221749475,
    -0.3591518512954867,
    0.09450494290776956,
)


def hidden_kernel(rows, weight, shift, hidden, slope):
    u = jnp.dot(rows[...], weight[...], preferred_element_type=F32) + shift[...]
    bell = jnp.exp(-0.5 * u * u)
    t = 1.0 / (1.0 + (RATE * 0.5**0.5) * jnp.abs(u))
    tail = jnp.full_like(u, 0.5 * ERFC[-1])
    for coefficient in ERFC[-2::-1]:
        tail = tail * t + 0.5 * coefficient
    tail = tail * t * bell
    area = jnp.where(u >= 0, 1.0 - tail, tail)
    hidden[...] = (u * area).astype(BF)
    slope[...] = (area + u * bell * 0.3989422804014327).astype(BF)


def hidden_layer(rows, weight, shift):
    m, k = rows.shape
    n = weight.shape[1]
    cols = 256
    out = pl.BlockSpec((m, cols), lambda i: (0, i))
    return kernel_call(
        hidden_kernel,
        "hidden_layer",
        [struct((m, n), BF)] * 2,
        us=11,
        grid=(n // cols,),
        in_specs=[
            pl.BlockSpec((m, k), lambda i: (0, 0)),
            pl.BlockSpec((k, cols), lambda i: (0, i)),
            pl.BlockSpec((1, cols), lambda i: (0, i)),
        ],
        out_specs=[out, out],
    )(rows, weight, shift)


def d_pre_kernel(grad, weight, slope, d_pre, total):
    back = dot_nt(grad[...], weight[...]) * slope[...].astype(F32)
    low = back.astype(BF)
    d_pre[...] = low
    total[...] = jnp.sum(low.astype(F32), axis=0, keepdims=True)


def hidden_back(grad, weight, slope):
    m, k = grad.shape
    n = weight.shape[0]
    cols = 256
    out = pl.BlockSpec((m, cols), lambda i: (0, i))
    return kernel_call(
        d_pre_kernel,
        "hidden_back",
        [struct((m, n), BF), struct((1, n), F32)],
        us=6,
        grid=(n // cols,),
        in_specs=[
            pl.BlockSpec((m, k), lambda i: (0, 0)),
            pl.BlockSpec((cols, k), lambda i: (i, 0)),
            out,
        ],
        out_specs=[out, pl.BlockSpec((1, cols), lambda i: (0, i))],
    )(grad, weight, slope)


def head_pair(packed, query_shift, value_shift, p):
    at = slice(p * 128, (p + 1) * 128)
    query = (packed[:, p * 128 : (p + 1) * 128] + query_shift[:, at]).astype(BF)
    key = packed[:, 512 + p * 128 : 512 + (p + 1) * 128].astype(BF)
    value = (packed[:, 1024 + p * 128 : 1024 + (p + 1) * 128] + value_shift[:, at]).astype(BF)
    return query, key, value


SCALE = HEAD_DIM ** (-0.5)


def softmax_of(query, key, blocked, first, e):
    only = jnp.where(first if e == 0 else ~first, query, jnp.zeros_like(query))
    scores = dot_nt(only, key) * SCALE + blocked
    exps = jnp.exp(scores - jnp.max(scores, axis=-1, keepdims=True))
    return exps * (1.0 / jnp.sum(exps, axis=-1, keepdims=True))


def attention_kernel(packed, query_shift, value_shift, blocked, mixed):
    first = lax.broadcasted_iota(jnp.int32, (BLOCK, 128), 1) < 64
    for p in range(4):
        query, key, value = head_pair(packed, query_shift, value_shift, p)
        parts = [
            dot(softmax_of(query, key, blocked[...], first, e).astype(BF), value) for e in range(2)
        ]
        mixed[:, p * 128 : (p + 1) * 128] = jnp.where(first, parts[0], parts[1]).astype(BF)


def attention(packed, query_shift, value_shift, blocked):
    rows = packed.shape[0]
    shift = pl.BlockSpec((1, 512), lambda i: (0, 0))
    return kernel_call(
        attention_kernel,
        "attention",
        struct((rows, 512), BF),
        us=5,
        grid=(rows // BLOCK,),
        in_specs=[
            pl.BlockSpec((BLOCK, 1536), lambda i: (i, 0)),
            shift,
            shift,
            pl.BlockSpec((None, BLOCK, BLOCK), lambda i: (i, 0, 0)),
        ],
        out_specs=pl.BlockSpec((BLOCK, 512), lambda i: (i, 0)),
    )(packed, query_shift, value_shift, blocked)


def attention_back_kernel(packed, query_shift, value_shift, blocked, d_mixed, d_packed, total):
    first = lax.broadcasted_iota(jnp.int32, (BLOCK, 128), 1) < 64

    @pl.when(pl.program_id(0) == 0)
    def _():
        total[...] = jnp.zeros_like(total)

    for p in range(4):
        query, key, value = head_pair(packed, query_shift, value_shift, p)
        grad = d_mixed[:, p * 128 : (p + 1) * 128]
        d_query, d_key, d_value = [], [], []
        for e in range(2):
            probs = softmax_of(query, key, blocked[...], first, e)
            only = jnp.where(first if e == 0 else ~first, grad, jnp.zeros_like(grad))
            d_probs = dot_nt(only, value)
            d_scores = probs * (d_probs - jnp.sum(probs * d_probs, axis=-1, keepdims=True))
            d_scores = d_scores.astype(BF)
            d_value.append(dot_tn(probs.astype(BF), only))
            d_query.append(dot(d_scores, key))
            d_key.append(dot_tn(d_scores, query))
        parts = (
            jnp.where(first, d_query[0], d_query[1]) * SCALE,
            jnp.where(first, d_key[0], d_key[1]) * SCALE,
            d_value[0] + d_value[1],
        )
        for k, part in enumerate(parts):
            at = slice(k * 512 + p * 128, k * 512 + (p + 1) * 128)
            low = part.astype(BF)
            d_packed[:, at] = low
            total[:, at] += jnp.sum(low.astype(F32), axis=0, keepdims=True)


def attention_back(packed, query_shift, value_shift, blocked, d_mixed, late):
    rows = packed.shape[0]
    shift = pl.BlockSpec((1, 512), lambda i: (0, 0))
    return kernel_call(
        attention_back_kernel,
        "attention_back",
        [struct((rows, 1536), BF), struct((1, 1536), F32)],
        us=16,
        late=late,
        grid=(rows // BLOCK,),
        in_specs=[
            pl.BlockSpec((BLOCK, 1536), lambda i: (i, 0)),
            shift,
            shift,
            pl.BlockSpec((None, BLOCK, BLOCK), lambda i: (i, 0, 0)),
            pl.BlockSpec((BLOCK, 512), lambda i: (i, 0)),
        ],
        out_specs=[
            pl.BlockSpec((BLOCK, 1536), lambda i: (i, 0)),
            pl.BlockSpec((1, 1536), lambda i: (0, 0)),
        ],
    )(packed, query_shift, value_shift, blocked, d_mixed)


def dot(left, right):
    return jnp.dot(left, right, preferred_element_type=F32)


def dot_nt(left, right):
    return lax.dot_general(left, right, (((1,), (1,)), ((), ())), preferred_element_type=F32)


def dot_tn(left, right):
    return lax.dot_general(left, right, (((0,), (0,)), ((), ())), preferred_element_type=F32)


def normalize(values):
    center = values - jnp.mean(values, axis=-1, keepdims=True)
    rstd = lax.rsqrt(jnp.mean(center * center, axis=-1, keepdims=True) + EPS)
    return center * rstd, rstd


def normalize_back(grad, yhat, rstd, gain):
    t = grad * gain
    return rstd * (
        t
        - jnp.mean(t, axis=-1, keepdims=True)
        - yhat * jnp.mean(t * yhat, axis=-1, keepdims=True)
    )


TILE = 96


def middle_kernel(part, other, tokens, keep, shift, gain, bias, middle, normed):
    attended = part[...].astype(F32) + other[...].astype(F32) + shift[...]
    rows = tokens[...].astype(F32) + keep[...] * attended
    middle[...] = rows
    yhat, _ = normalize(rows)
    normed[...] = (yhat * gain[...] + bias[...]).astype(BF)


def row_specs(count, width=1024):
    half = count // 2
    return (
        pl.BlockSpec((TILE, width), lambda i: (i, 0)),
        pl.BlockSpec((TILE, width), lambda i: (lax.rem(i + half, count), 0)),
        pl.BlockSpec((TILE, 1), lambda i: (i, 0)),
        pl.BlockSpec((1, width), lambda i: (0, 0)),
    )


def middle_layer(part, other, tokens, keep, shift, gain, bias):
    rows = part.shape[0]
    tile, swapped, column, vector = row_specs(rows // TILE)
    return kernel_call(
        middle_kernel,
        "middle_layer",
        [struct((rows, 1024), F32), struct((rows, 1024), BF)],
        us=6,
        grid=(rows // TILE,),
        in_specs=[tile, swapped, tile, column, vector, vector, vector],
        out_specs=[tile, tile],
    )(part, other, tokens, keep, shift, gain, bias)


def middle_back_kernel(part, other, middle, cot, keep, share, gain, d_middle, d_attended, sums):
    step = pl.program_id(0)
    grad = part[...].astype(F32) + other[...].astype(F32)
    yhat, rstd = normalize(middle[...])
    incoming = cot[...].astype(F32) * share[...]
    d_rows = incoming + normalize_back(grad, yhat, rstd, gain[...])
    d_middle[...] = d_rows
    low = (keep[...] * d_rows).astype(BF)
    d_attended[...] = low
    branch = (keep[...] * incoming).astype(BF)

    @pl.when(step == 0)
    def _():
        sums[...] = jnp.zeros_like(sums)

    @pl.when(step < pl.num_programs(0) // 2)
    def _():
        for k, v in enumerate((grad * yhat, grad, low.astype(F32), branch.astype(F32))):
            sums[k : k + 1, :] += jnp.sum(v, axis=0, keepdims=True)


def middle_back(part, other, middle, cot, keep, share, gain, late):
    rows = part.shape[0]
    tile, swapped, column, vector = row_specs(rows // TILE)
    return kernel_call(
        middle_back_kernel,
        "middle_back",
        [struct((rows, 1024), F32), struct((rows, 1024), BF), struct((8, 1024), F32)],
        us=7,
        late=late,
        grid=(rows // TILE,),
        in_specs=[tile, swapped, tile, tile, column, column, vector],
        out_specs=[tile, tile, pl.BlockSpec((8, 1024), lambda i: (0, 0))],
    )(part, other, middle, cot, keep, share, gain)


def input_back_kernel(part, other, tokens, d_middle, gain, grad_rows, sums):
    grad = part[...].astype(F32) + other[...].astype(F32)
    yhat, rstd = normalize(tokens[...].astype(F32))
    grad_rows[...] = (d_middle[...] + normalize_back(grad, yhat, rstd, gain[...])).astype(BF)

    @pl.when(pl.program_id(0) == 0)
    def _():
        sums[...] = jnp.zeros_like(sums)

    for k, v in enumerate((grad * yhat, grad)):
        sums[k : k + 1, :] += jnp.sum(v, axis=0, keepdims=True)


def input_back(part, other, tokens, d_middle, gain):
    rows = part.shape[0]
    tile, _, _, vector = row_specs(rows // TILE)
    return kernel_call(
        input_back_kernel,
        "input_back",
        [struct((rows, 1024), BF), struct((8, 1024), F32)],
        us=4,
        grid=(rows // TILE,),
        in_specs=[tile, tile, tile, tile, vector],
        out_specs=[tile, pl.BlockSpec((8, 1024), lambda i: (0, 0))],
    )(part, other, tokens, d_middle, gain)


def body(
    tokens,
    norm1_gain,
    norm1_bias,
    qkv_weight,
    query_bias,
    value_bias,
    out_weight,
    out_bias,
    norm2_gain,
    norm2_bias,
    fc1_weight,
    fc1_bias,
    fc2_weight,
    fc2_bias,
    cotangent,
    group_of,
    keep_mask,
    group_tokens,
):
    here = Where()
    own_rows, width = tokens.shape
    c = here.c
    here.make_table()
    place_table = here.table

    vectors = (
        norm1_gain,
        norm1_bias,
        query_bias,
        value_bias,
        out_bias,
        norm2_gain,
        norm2_bias,
        fc2_bias,
        fc1_bias,
    )

    def whole(v):
        return pl.BlockSpec(v.shape, lambda i: (0,) * len(v.shape))

    shapes = [
        struct(shape, BF) for shape in ((8, 32, 1664), (4, 64, 2048), (256, 1024), (64, 1024))
    ]
    weights = (qkv_weight, fc1_weight, fc2_weight, out_weight)
    qkv_rep, fc1_rep, fc2_half, out_half = kernel_call(
        prepare_kernel,
        "prepare",
        shapes,
        us=3,
        pinned=True,
        grid=(1,),
        in_specs=[SMEM] + [whole(v) for v in weights + vectors],
        out_specs=[whole(v) for v in shapes],
    )(place_table, *weights, *vectors)
    qkv_slab = all_to_all(qkv_rep, "fsdp")
    out_all = lax.all_gather(out_half, "fsdp", axis=0, tiled=True)
    fc2_other = permute(fc2_half, flip_hi)
    fc2_pair = assemble(
        here,
        "fc2_hi",
        [fc2_half, fc2_other],
        (2, 256, 1024),
        lambda o, t, n: o.at[t[HI] if n == 0 else 1 - t[HI]],
    )
    fc1_row = all_to_all(fc1_rep, "fsdp", X_GROUPS)
    qkv_all = assemble(
        here,
        "qkv_z",
        ring_blocks(qkv_slab, "z"),
        (8, 4, 32, 1536),
        lambda o, t, n: o.at[:, source_in(t, Z, n)],
        lambda ref: ref.at[:, :, pl.ds(0, 1536)],
    ).reshape(1024, 1536)
    fc1_blocks = ring_blocks(fc1_row, "y")
    fc2_blocks = ring_blocks(fc2_pair, "x")
    rows_low = jnp.concatenate([tokens, permute(tokens, swap_core)])
    keep = jnp.concatenate([keep_mask, permute(keep_mask, swap_core)])
    cot = jnp.concatenate([cotangent, permute(cotangent, swap_core)])

    (
        gain_one,
        shift_one,
        out_shift,
        gain_two,
        shift_two,
        fc2_shift,
        query_shift,
        value_shift,
        fc1_shift,
    ) = kernel_call(
        vectors_kernel,
        "vectors",
        [struct((1, 1024), F32)] * 6 + [struct((1, 512), F32)] * 2 + [struct((1, 2048), F32)],
        us=1,
        grid=(1,),
        in_specs=[SMEM, pl.BlockSpec((8, 16, 128), lambda i: (0, 0, 12))],
        out_specs=[pl.BlockSpec((1, n), lambda i: (0, 0)) for n in (1024,) * 6 + (512,) * 2 + (2048,)],
    )(place_table, qkv_slab)

    groups = jnp.stack([pick(group_of, here.dp), pick(group_of, here.dp + here.sign)])
    counts = group_tokens.astype(F32)
    share = counts / jnp.sum(counts)
    share = jnp.where(groups == 1, share[1], share[0])
    share_col = jnp.repeat(share, own_rows)[:, None]
    mask_col = keep.astype(F32)[:, None]
    row_count = 2 * own_rows
    blocks = row_count // BLOCK
    block_group = jnp.repeat(groups, blocks // 2)
    image = jnp.where(
        block_group[:, None] == 1, 0, jnp.arange(BLOCK, dtype=jnp.int32)[None] // SLOT_S
    )
    allowed = (image[:, :, None] == image[:, None, :]) & (keep.reshape(blocks, 1, BLOCK) == 1)
    blocked = jnp.where(allowed, F32(0), F32(-1e30))
    incoming = cot.astype(F32) * share_col
    d_branch = (mask_col * incoming).astype(BF)

    yhat_one, _ = normalize(rows_low.astype(F32))
    normed = (yhat_one * gain_one + shift_one).astype(BF)
    normed, blocked, d_branch, mask_col, share_col, cot = lax.optimization_barrier(
        (normed, blocked, d_branch, mask_col, share_col, cot)
    )
    packed = dot(normed, qkv_all)
    mixed = attention(packed, query_shift, value_shift, blocked)
    attended = dot(mixed, out_all).astype(BF)
    middle, normed_two = middle_layer(
        attended, permute(attended, swap_core), rows_low, mask_col, out_shift, gain_two, shift_two
    )
    fc1_all = assemble(
        here,
        "fc1_y",
        fc1_blocks,
        (2, 4, 2, 64, 2048),
        lambda o, t, n: o.at[source_in(t, Y, n) // 2, :, lax.rem(source_in(t, Y, n), 2)],
        late=(normed_two,),
    ).reshape(1024, 2048)
    hidden, slope = hidden_layer(normed_two, fc1_all, fc1_shift)
    fc2_all = assemble(
        here,
        "fc2_x",
        fc2_blocks,
        (2, 4, 256, 1024),
        lambda o, t, n: o.at[:, source_in(t, X, n)],
        late=(hidden,),
    ).reshape(2048, 1024)

    d_pre, fc1_bias_sum = hidden_back(d_branch, fc2_all, slope)
    d_normed_two = dot_nt(d_pre, fc1_all).astype(BF)
    grad_fc1 = grad_fc1_terms(normed_two, d_pre, (d_normed_two,)).reshape(4, 2, 128, 2048)
    fc1_sum = pick(grad_fc1, here.source("y", 1))
    fc1_arrived = permute(fc1_sum, ring_move("y"))
    grad_fc2 = grad_fc2_terms(hidden, d_branch, (fc1_sum,))
    fc2_sum = lax.psum_scatter(
        grad_fc2.reshape(2048, 1024),
        "dp",
        scatter_dimension=0,
        axis_index_groups=Z_GROUPS,
        tiled=True,
    )
    d_middle, d_attended, middle_sums = middle_back(
        d_normed_two,
        permute(d_normed_two, swap_core),
        middle,
        cot,
        mask_col,
        share_col,
        gain_two,
        (grad_fc2,),
    )
    grad_out = dot_tn(mixed, d_attended).astype(BF)
    out_sum = all_to_all(grad_out.reshape(8, 64, 1024), "fsdp")
    d_mixed = dot_nt(d_attended, out_all).astype(BF)
    fc1_sum = ring_add(here, "fc1_add", fc1_arrived, grad_fc1, Y, 2, (d_middle,))
    fc1_arrived = permute(fc1_sum, ring_move("y"))
    d_packed, packed_sums = attention_back(
        packed, query_shift, value_shift, blocked, d_mixed, (fc1_sum, grad_out)
    )
    fc1_sum = ring_add(here, "fc1_add", fc1_arrived, grad_fc1, Y, 3, (d_packed,))
    fc1_arrived = permute(fc1_sum, ring_move("y"))
    grad_qkv = dot_tn(normed, d_packed).astype(BF)
    grad_qkv, d_packed, hidden = lax.optimization_barrier((grad_qkv, d_packed, hidden))
    qkv_sum = all_to_all(grad_qkv.reshape(8, 128, 1536), "fsdp")

    d_normed_sent = permute(dot_nt(d_packed[own_rows:], qkv_all).astype(BF), swap_core)
    d_normed_own = dot_nt(d_packed[:own_rows], qkv_all).astype(BF)
    input_grad, input_sums = input_back(d_normed_own, d_normed_sent, tokens, d_middle, gain_one)

    branch_sent = permute(dot(hidden[own_rows:], fc2_all).astype(BF), swap_core)
    branch = dot(hidden[:own_rows], fc2_all) + branch_sent.astype(F32) + fc2_shift
    block_out = (middle[:own_rows] + mask_col[:own_rows] * branch).astype(BF)

    vector_terms = kernel_call(
        vector_terms_kernel,
        "vector_terms",
        struct((8, 16, 128), F32),
        us=1,
        in_specs=[SMEM] + [VMEM] * 4,
        out_specs=VMEM,
    )(place_table, input_sums, packed_sums, middle_sums, fc1_bias_sum)
    vector_sums = add_over(
        vector_terms,
        lambda x, y, z, c: (x, y, z ^ 1, c),
        lambda x, y, z, c: (x, y, 3 - z, c),
        swap_core,
        flip_lo,
    )

    fc1_sum = ring_add(here, "fc1_add", fc1_arrived, grad_fc1, Y, 4, (grad_qkv,))
    fc1_sum = lax.psum_scatter(
        fc1_sum.reshape(256, 2048),
        "fsdp",
        scatter_dimension=0,
        axis_index_groups=X_GROUPS,
        tiled=True,
    )
    fc2_sum = lax.psum_scatter(
        fc2_sum,
        "fsdp",
        scatter_dimension=0,
        axis_index_groups=X_GROUPS,
        tiled=True,
    ).reshape(2, 64, 1024)
    slices = merge(here, qkv_sum, out_sum, fc1_sum, (input_grad, block_out, vector_sums))
    slices = all_to_all(slices, "dp", SLICE_GROUPS)
    vector_sums = add_over(
        vector_sums,
        lambda x, y, z, c: (x ^ 1, y, z, c),
        lambda x, y, z, c: (3 - x, y, z, c),
        flip_hi,
    )
    vector_sums = pick(vector_sums, here.fs)
    fc2_kept, fc2_sent = halve(here, "fc2_hi", HI, fc2_sum, flip_hi)
    fc2_sum = (fc2_kept + fc2_sent.astype(F32)).astype(BF).reshape(2, 32, 1024)
    fc2_kept, fc2_sent = halve(here, "fc2_lo", LO, fc2_sum, flip_lo)
    packed_slices = kernel_call(
        pack_kernel,
        "pack",
        struct((8, 48, 2048), BF),
        us=1.5,
        late=(vector_sums,),
        grid=(1,),
        in_specs=[whole(slices), whole(fc2_kept), whole(fc2_sent)],
        out_specs=whole(struct((8, 48, 2048), BF)),
    )(slices, fc2_kept, fc2_sent)
    own = all_to_all(packed_slices, "dp", SLICE_GROUPS)
    half = pl.BlockSpec((None, 48, 2048), lambda i: (i, 0, 0))
    grad_qkv_weight, grad_out_weight, grad_fc1_weight, grad_fc2_weight = kernel_call(
        unpack_kernel,
        "unpack",
        [
            struct((128, 3072), F32),
            struct((2, 8, 8, 1024), F32),
            struct((128, 4096), F32),
            struct((2, 8, 32, 1024), F32),
        ],
        us=5,
        grid=(8,),
        in_specs=[SMEM, half, half],
        out_specs=[
            pl.BlockSpec((16, 3072), lambda i: (i, 0)),
            pl.BlockSpec((2, None, 8, 1024), lambda i: (0, i, 0, 0)),
            pl.BlockSpec((16, 4096), lambda i: (i, 0)),
            pl.BlockSpec((2, None, 32, 1024), lambda i: (0, lax.rem(i, 4) * 2 + i // 4, 0, 0)),
        ],
    )(place_table, own, permute(own, swap_core))
    return (
        block_out,
        input_grad,
        vector_sums[0],
        vector_sums[1],
        grad_qkv_weight,
        vector_sums[2],
        vector_sums[3],
        grad_out_weight.reshape(128, 1024),
        vector_sums[4],
        vector_sums[5],
        vector_sums[6],
        grad_fc1_weight,
        vector_sums[8:12].reshape(512),
        grad_fc2_weight.reshape(512, 1024),
        vector_sums[7],
    )


def solution(mesh):
    rows, cols, both = P("fsdp", None), P("fsdp"), ("dp", "fsdp")
    in_specs = (
        P(both, None),
        cols,
        cols,
        rows,
        cols,
        cols,
        rows,
        cols,
        cols,
        cols,
        rows,
        cols,
        rows,
        cols,
        P(both, None),
        P(),
        P(both),
        P(),
    )
    out_specs = (
        P(both, None),
        P(both, None),
        cols,
        cols,
        rows,
        cols,
        cols,
        rows,
        cols,
        cols,
        cols,
        rows,
        cols,
        rows,
        cols,
    )
    return jax.shard_map(body, mesh=mesh, in_specs=in_specs, out_specs=out_specs, check_vma=False)
```

```python
import functools

import jax
import jax.numpy as jnp
from jax import lax
from jax.experimental import pallas as pl
from jax.experimental.pallas import tpu as pltpu
from jax.sharding import PartitionSpec as P

HEAD_DIM = 64
SLOT_S = 64
SLOT_L = 192
SPAN = 192
MOST_S = 50
USED = SPAN // SLOT_S * MOST_S
BLOCK = 160
EPS = 1e-06
AXES = ("dp", "fsdp")
BF = jnp.bfloat16
F32 = jnp.float32

Z_GROUPS = [[lo * 8 + 2 * z + c for z in range(4)] for lo in range(2) for c in range(2)]
SLICE_GROUPS = [[lo * 8 + 2 * z + c for z in range(4) for lo in range(2)] for c in range(2)]
X_GROUPS = [[0, 1, 2, 3], [4, 5, 6, 7]]


def place(linear):
    dp, fs = divmod(linear, 8)
    return fs % 4, (fs // 4) * 2 + dp // 8, (dp // 2) % 4, dp % 2


def linear_of(x, y, z, c):
    x, y, z = x % 4, y % 4, z % 4
    return (((y % 2) * 4 + z) * 2 + c) * 8 + (y // 2) * 4 + x


def permute(value, move):
    return lax.ppermute(
        value, AXES, [(l, linear_of(*move(*place(l)))) for l in range(128)]
    )


def ring_move(axis):
    def move(x, y, z, c):
        s = 1 - 2 * c
        return (x + s * (axis == "x"), y + s * (axis == "y"), z + s * (axis == "z"), c)

    return move


def shift(axis, s):
    def move(x, y, z, c):
        return (x + s * (axis == "x"), y + s * (axis == "y"), z + s * (axis == "z"), c)

    return move


HOPS = (1, 2, 3)


def swap_core(x, y, z, c):
    return x, y, z, 1 - c


def flip_hi(x, y, z, c):
    return x, 3 - y, z, c


def flip_lo(x, y, z, c):
    return x, y ^ 1, z, c


class Where:
    def __init__(self):
        dp, fs = lax.axis_index("dp"), lax.axis_index("fsdp")
        self.dp, self.fs = dp, fs
        self.c = dp % 2
        self.z = (dp // 2) % 4
        self.lo = dp // 8
        self.x = fs % 4
        self.hi = fs // 4
        self.y = self.hi * 2 + self.lo
        self.sign = 1 - 2 * self.c

    def along(self, axis):
        return {"x": self.x, "y": self.y, "z": self.z}[axis]

    def source(self, axis, step):
        return lax.rem(self.along(axis) - self.sign * step + 8, 4)

    def make_table(self):
        self.table = jnp.stack([self.c, self.z, self.lo, self.hi, self.x, self.y]).astype(jnp.int32)


C, Z, LO, HI, X, Y = range(6)


def source_in(table, at, step):
    return lax.rem(table[at] - (1 - 2 * table[C]) * step + 8, 4)


def place_in(table, at, r):
    return lax.rem(table[at] + r + 4, 4)


def pick(stacked, index, axis=0):
    return lax.dynamic_index_in_dim(stacked, index, axis, keepdims=False)


def ring_gather(here, value, axis, buffer, put):
    for step in range(4):
        if step:
            value = permute(value, ring_move(axis))
        buffer = put(buffer, value, here.source(axis, step))
    return buffer


def ring_reduce(here, axis, term):
    total = term(here.source(axis, 1))
    for step in range(2, 5):
        total = permute(total, ring_move(axis))
        total = (total.astype(F32) + term(here.source(axis, step)).astype(F32)).astype(BF)
    return total


def ring_blocks(value, axis):
    blocks = [value]
    for _ in range(3):
        blocks.append(permute(blocks[-1], ring_move(axis)))
    return blocks


def exchange(blocks, axis):
    return [blocks[0]] + [permute(blocks[r], shift(axis, r)) for r in HOPS]


ANY = pl.BlockSpec(memory_space=pl.ANY)
SMEM = pl.BlockSpec(memory_space=pltpu.SMEM)
VMEM = pl.BlockSpec(memory_space=pltpu.VMEM)


TOKEN = jax.ShapeDtypeStruct((8, 128), jnp.float32)
TOKEN_SPEC = pl.BlockSpec((8, 128), lambda i: (0, 0))


def in_hbm(value):
    return pltpu.with_memory_space_constraint(value, pltpu.HBM)


def kernel_call(
    kernel,
    name,
    out_shape,
    in_specs,
    us=1,
    vmem=16 << 20,
    pinned=(),
    pinned_out=(),
    late=(),
    **kwargs,
):
    count = len(in_specs)
    if pinned_out:
        shapes = out_shape if isinstance(out_shape, list) else [out_shape]
        shapes = [
            pltpu.HBM(s.shape, s.dtype) if n in pinned_out else s for n, s in enumerate(shapes)
        ]
        out_shape = shapes if isinstance(out_shape, list) else shapes[0]

    def body(*refs):
        kernel(*refs[:count], *refs[count + len(late) :])

    call = pl.pallas_call(
        body,
        out_shape=out_shape,
        in_specs=list(in_specs) + [ANY] * len(late),
        name=name,
        compiler_params=pltpu.CompilerParams(vmem_limit_bytes=vmem),
        cost_estimate=pl.CostEstimate(
            flops=int(us * 0.25 * 1.15e9), bytes_accessed=1 << 16, transcendentals=0
        ),
        **kwargs,
    )

    def run(*args):
        return call(
            *(in_hbm(a) if n in pinned else a for n, a in enumerate(args)),
            *(in_hbm(a) if a.size > 1 << 16 else a for a in late),
        )

    return run


def struct(shape, dtype):
    return jax.ShapeDtypeStruct(shape, dtype)


def assemble(here, name, parts, shape, target, source=lambda ref: ref, late=()):
    def kernel(table, *refs):
        ins, out, sems = refs[: len(parts)], refs[len(parts)], refs[len(parts) + 1]
        copies = [
            pltpu.make_async_copy(source(ins[n]), target(out, table, n), sems.at[n])
            for n in range(len(parts))
        ]
        for copy in copies:
            copy.start()
        for copy in copies:
            copy.wait()

    return kernel_call(
        kernel,
        name,
        struct(shape, BF),
        in_specs=[SMEM] + [ANY] * len(parts),
        us=2.5,
        pinned=range(1, 1 + len(parts)),
        late=late,
        out_specs=VMEM,
        scratch_shapes=[pltpu.SemaphoreType.DMA((len(parts),))],
    )(here.table, *parts)


def lane_halves(c, left, right):
    first = lax.broadcasted_iota(jnp.int32, left.shape, 1) < 64
    low = jnp.where(first, left, pltpu.roll(right, 64, 1))
    high = jnp.where(first, pltpu.roll(left, 64, 1), right)
    return jnp.where(c == 0, low, high)


def prepare_kernel(place_ref, qkv, fc1, fc2, out, *refs):
    vectors, (qkv_rep, fc1_part, fc2_half, out_half) = refs[:9], refs[9:]
    c, z, lo = place_ref[0], place_ref[1], place_ref[2]
    rows = pl.ds(pl.multiple_of(z * 32, 32), 32)
    for g in range(12):
        left = qkv[rows, g * 256 : g * 256 + 128].astype(F32)
        right = qkv[rows, g * 256 + 128 : g * 256 + 256].astype(F32)
        half = lane_halves(c, left, right).astype(BF)
        for d in range(8):
            qkv_rep[d, :, g * 128 : (g + 1) * 128] = half
    packed = [ref[...].astype(F32).reshape(-1, 128) for ref in vectors]
    packed = jnp.concatenate(packed + [jnp.zeros((20, 128), F32)]).astype(BF)
    for d in range(8):
        qkv_rep[d, :, 1536:] = packed
    out_half[...] = out[pl.ds(pl.multiple_of(c * 64, 64), 64), :]
    rows = pl.ds(pl.multiple_of(lo * 64, 64), 64)
    for f in range(8):
        half = jnp.where(
            c == 0, fc1[rows, f * 512 : f * 512 + 256], fc1[rows, f * 512 + 256 : (f + 1) * 512]
        )
        fc1_part[:, f * 256 : (f + 1) * 256] = half
    fc2_half[...] = fc2[pl.ds(pl.multiple_of(c * 256, 256), 256), :]


def row_choice(group):
    i = lax.broadcasted_iota(jnp.int32, (BLOCK, SPAN), 0)
    j = lax.broadcasted_iota(jnp.int32, (BLOCK, SPAN), 1)
    slot = (i >= MOST_S).astype(jnp.int32) + (i >= 2 * MOST_S).astype(jnp.int32)
    source = jnp.where(group == 1, i, i + slot * (SLOT_S - MOST_S))
    return jnp.where((j == source) & (i < USED), 1.0, 0.0)


def chosen_rows(group):
    j = lax.broadcasted_iota(jnp.int32, (SPAN, 1), 0)
    slot = (j >= SLOT_S).astype(jnp.int32) + (j >= 2 * SLOT_S).astype(jnp.int32)
    place = jnp.where(group == 1, j, j - slot * SLOT_S)
    return place < jnp.where(group == 1, USED, MOST_S)


def image_of(group, shape, axis):
    i = lax.broadcasted_iota(jnp.int32, shape, axis)
    slot = (i >= MOST_S).astype(jnp.int32) + (i >= 2 * MOST_S).astype(jnp.int32)
    return jnp.where(group == 1, 0, slot)


def compact_kernel(
    groups, shares, tokens, tokens_other, cot, cot_other, keep, keep_other, rows, cots, d_branch, column, blocked
):
    step = pl.program_id(0)
    own = step < 2
    group = groups[step // 2]
    choice = row_choice(group)
    low = choice.astype(BF)
    kept = jnp.where(own, keep[...], keep_other[...]).astype(F32)
    rows[...] = dot(low, jnp.where(own, tokens[...], tokens_other[...])).astype(BF)
    chosen = dot(low, jnp.where(own, cot[...], cot_other[...]))
    cots[...] = chosen.astype(BF)
    mask = jnp.sum(choice * kept, axis=-1, keepdims=True)
    column[...] = mask
    d_branch[...] = (mask * (chosen * shares[step // 2])).astype(BF)
    across = dot_nt(jnp.broadcast_to(kept, (16, SPAN)).astype(BF), low)[:1]
    same = image_of(group, (BLOCK, BLOCK), 0) == image_of(group, (BLOCK, BLOCK), 1)
    blocked[...] = jnp.where(same & (across > 0.5), 0.0, -1e30)


def compact(groups, shares, tokens, tokens_other, cot, cot_other, keep, keep_other):
    def mine(shape, rows):
        return pl.BlockSpec(shape, lambda i: (jnp.minimum(i, 1),) + (0,) * (len(shape) - 1))

    def theirs(shape, rows):
        return pl.BlockSpec(shape, lambda i: (jnp.maximum(i - 2, 0),) + (0,) * (len(shape) - 1))

    row = (SPAN, 1024)
    flag = (None, 1, SPAN)
    tile = pl.BlockSpec((BLOCK, 1024), lambda i: (i, 0))
    return kernel_call(
        compact_kernel,
        "compact",
        [struct((4 * BLOCK, 1024), BF)] * 3
        + [struct((4 * BLOCK, 1), F32), struct((4, BLOCK, BLOCK), F32)],
        us=5,
        grid=(4,),
        in_specs=[
            SMEM,
            SMEM,
            mine(row, 2),
            theirs(row, 2),
            mine(row, 2),
            theirs(row, 2),
            mine(flag, 2),
            theirs(flag, 2),
        ],
        out_specs=[
            tile,
            tile,
            tile,
            pl.BlockSpec((BLOCK, 1), lambda i: (i, 0)),
            pl.BlockSpec((None, BLOCK, BLOCK), lambda i: (i, 0, 0)),
        ],
    )(
        groups,
        shares,
        tokens,
        tokens_other,
        cot,
        cot_other,
        keep.reshape(2, 1, SPAN),
        keep_other.reshape(2, 1, SPAN),
    )


def spread(group, values, rest):
    back = dot_tn(row_choice(group).astype(BF), values)
    return jnp.where(chosen_rows(group), back, rest.astype(F32)).astype(BF)


def block_out_kernel(groups, branch, sent, middle, column, shift, tokens, out):
    total = branch[...] + sent[...].astype(F32) + shift[...]
    values = (middle[...] + column[...] * total).astype(BF)
    out[...] = spread(groups[0], values, tokens[...])


def block_out_layer(groups, branch, sent, middle, column, shift, tokens):
    tile = pl.BlockSpec((BLOCK, 1024), lambda i: (i, 0))
    span = pl.BlockSpec((SPAN, 1024), lambda i: (i, 0))
    return kernel_call(
        lambda *refs: block_out_kernel(*refs[:-1]),
        "block_out",
        [struct(tokens.shape, BF), TOKEN],
        us=4,
        grid=(2,),
        in_specs=[
            SMEM,
            tile,
            tile,
            tile,
            pl.BlockSpec((BLOCK, 1), lambda i: (i, 0)),
            pl.BlockSpec((1, 1024), lambda i: (0, 0)),
            span,
        ],
        out_specs=[span, TOKEN_SPEC],
    )(groups, branch, sent, middle, column, shift, tokens)


def vectors_kernel(place_ref, packed, *outs):
    c = place_ref[0]
    rows = [packed[f].astype(F32) for f in range(8)]

    def row(f, k):
        return rows[f][k : k + 1, :]

    for out, k in zip(outs[:6], (0, 1, 4, 5, 6, 7)):
        for f in range(8):
            out[:, f * 128 : (f + 1) * 128] = row(f, k)
    for out, k in zip(outs[6:8], (2, 3)):
        for p in range(4):
            out[:, p * 128 : (p + 1) * 128] = lane_halves(c, row(2 * p, k), row(2 * p + 1, k))
    for f in range(8):
        for j in range(2):
            at = f * 256 + j * 128
            outs[8][:, at : at + 128] = jnp.where(c == 0, row(f, 8 + j), row(f, 10 + j))


def vector_terms_kernel(place_ref, input_sums, packed_sums, middle_sums, fc1_sums, out):
    c = place_ref[0]
    first = lax.broadcasted_iota(jnp.int32, (1, 128), 1) < 64
    zero = jnp.zeros((1, 128), F32)
    out[...] = jnp.zeros_like(out)
    whole = (
        (0, input_sums, 0),
        (1, input_sums, 1),
        (4, middle_sums, 2),
        (5, middle_sums, 0),
        (6, middle_sums, 1),
        (7, middle_sums, 3),
    )
    for f in range(8):
        for k, ref, r in whole:
            out[f, k : k + 1, :] = ref[r : r + 1, f * 128 : (f + 1) * 128]
        for j in range(4):
            at = f * 256 + (j % 2) * 128
            out[f, 8 + j : 9 + j, :] = jnp.where(c == j // 2, fc1_sums[:, at : at + 128], zero)
    for k, base in ((2, 0), (3, 1024)):
        for p in range(4):
            pair = packed_sums[:, base + p * 128 : base + (p + 1) * 128]
            turned = pltpu.roll(pair, 64, 1)
            for e in range(2):
                low = jnp.where(first, pair if e == 0 else turned, zero)
                high = jnp.where(first, zero, turned if e == 0 else pair)
                out[2 * p + e, k : k + 1, :] = jnp.where(c == 0, low, high)


def grad_fc2_kernel(left, right, out):
    terms = dot_tn(left[...], right[...]).astype(BF)
    for x in range(2):
        for z in range(4):
            at = (4 * x + z) * 64
            out[z, x] = terms[at : at + 64]


def grad_fc2_terms(hidden, d_branch, late):
    m = hidden.shape[0]
    return kernel_call(
        lambda *refs: grad_fc2_kernel(*refs[:-1]),
        "grad_fc2",
        [struct((4, 8, 64, 1024), BF), TOKEN],
        us=5,
        late=late,
        pinned_out=(0,),
        grid=(4,),
        in_specs=[
            pl.BlockSpec((m, 512), lambda i: (0, i)),
            pl.BlockSpec((m, 1024), lambda i: (0, 0)),
        ],
        out_specs=[
            pl.BlockSpec((4, 2, 64, 1024), lambda i: (0, i, 0, 0)),
            TOKEN_SPEC,
        ],
    )(hidden, d_branch)


def grad_fc1_kernel(table, left, right, *refs):
    outs = refs[:4]
    terms = dot_tn(left[...], right[...]).astype(BF)
    hi = lax.rem(pl.program_id(0), 2)
    for n, out in enumerate(outs):
        y = source_in(table, Y, n + 1)
        for lo in range(2):

            @pl.when(y == hi * 2 + lo)
            def _():
                for x in range(2):
                    at = (2 * x + lo) * 64
                    out[x] = terms[at : at + 64]


def grad_fc1_terms(here, normed, d_pre, late):
    m = normed.shape[0]
    return kernel_call(
        grad_fc1_kernel,
        "grad_fc1",
        [struct((4, 64, 2048), BF)] * 4 + [TOKEN],
        us=5,
        late=late,
        pinned_out=range(4),
        grid=(4,),
        in_specs=[
            SMEM,
            pl.BlockSpec((m, 256), lambda i: (0, lax.rem(i, 2) * 2 + i // 2)),
            pl.BlockSpec((m, 2048), lambda i: (0, 0)),
        ],
        out_specs=[pl.BlockSpec((2, 64, 2048), lambda i: (i // 2, 0, 0))] * 4 + [TOKEN_SPEC],
    )(here.table, normed, d_pre)


def grad_qkv_kernel(normed, d_packed, mixed, d_attended, out):
    qkv = dot_tn(normed[...], d_packed[...]).astype(BF)
    rest = dot_tn(mixed[...], d_attended[...])
    for f in range(2):
        parts = []
        for k in range(8):
            rows = rest[f * 64 + k * 8 : f * 64 + (k + 1) * 8]
            parts += [rows[:, :512], rows[:, 512:]]
        parts = jnp.concatenate(parts).astype(BF)
        for z in range(4):
            out[z, f, :, :1536] = qkv[f * 128 + z * 32 : f * 128 + (z + 1) * 32]
            out[z, f, :, 1536:] = parts[z * 32 : (z + 1) * 32]


def grad_qkv_terms(normed, d_packed, mixed, d_attended, late):
    m = normed.shape[0]
    return kernel_call(
        grad_qkv_kernel,
        "grad_qkv",
        struct((4, 8, 32, 2048), BF),
        us=5,
        late=late,
        pinned_out=(0,),
        grid=(4,),
        in_specs=[
            pl.BlockSpec((m, 256), lambda i: (0, i)),
            pl.BlockSpec((m, 1536), lambda i: (0, 0)),
            pl.BlockSpec((m, 128), lambda i: (0, i)),
            pl.BlockSpec((m, 1024), lambda i: (0, 0)),
        ],
        out_specs=pl.BlockSpec((4, 2, 32, 2048), lambda i: (0, i, 0, 0)),
    )(normed, d_packed, mixed, d_attended)


def total_of(refs):
    total = refs[0][...].astype(F32)
    for ref in refs[1:]:
        total = total + ref[...].astype(F32)
    return total


def sum_kernel(*refs):
    refs[-1][...] = total_of(refs[:-1]).astype(BF)


def sum_of(name, blocks, late=()):
    block = pl.BlockSpec((2,) + blocks[0].shape[1:], lambda i: (i, 0, 0))
    return kernel_call(
        lambda *refs: sum_kernel(*refs[:-1]),
        name,
        [struct(blocks[0].shape, BF), TOKEN],
        us=2,
        late=late,
        grid=(2,),
        in_specs=[block] * len(blocks),
        out_specs=[block, TOKEN_SPEC],
    )(*blocks)


def sum_first_kernel(blocks, out):
    out[...] = jnp.sum(blocks[...].astype(F32), axis=0).astype(BF)


def sum_first(name, blocks):
    k, r, n = blocks.shape
    return kernel_call(
        sum_first_kernel,
        name,
        struct((r, n), BF),
        us=1,
        grid=(1,),
        in_specs=[pl.BlockSpec((k, r, n), lambda i: (0, 0, 0))],
        out_specs=pl.BlockSpec((r, n), lambda i: (0, 0)),
    )(blocks)


def join_kernel(qkv, vectors, out):
    for f in range(8):
        out[f, :, :2048] = qkv[f]
        out[f, :16, 2048:] = vectors[f].astype(BF)
        out[f, 16:, 2048:] = jnp.zeros((16, 128), BF)


def join(qkv, vectors, late):
    return kernel_call(
        join_kernel,
        "join",
        struct((8, 32, 2176), BF),
        us=1,
        late=late,
        grid=(1,),
        in_specs=[
            pl.BlockSpec((8, 32, 2048), lambda i: (0, 0, 0)),
            pl.BlockSpec((8, 16, 128), lambda i: (0, 0, 0)),
        ],
        out_specs=pl.BlockSpec((8, 32, 2176), lambda i: (0, 0, 0)),
    )(qkv, vectors)


def split_kernel(table, blocks, kept, sent, vectors):
    total = jnp.sum(blocks[...].astype(F32), axis=0)
    half, n = kept.shape
    low, high = total[:half, :n], total[half:, :n]
    kept[...] = jnp.where(table[LO] == 0, low, high)
    sent[...] = jnp.where(table[LO] == 0, high, low).astype(BF)
    if total.shape[1] > n:
        vectors[...] = total[:16, n:]


def sum_and_halve(here, name, blocks, n):
    k, r, wide = blocks.shape
    half = pl.BlockSpec((r // 2, n), lambda i: (0, 0))
    kept, sent, vectors = kernel_call(
        split_kernel,
        name,
        [struct((r // 2, n), F32), struct((r // 2, n), BF), struct((16, 128), F32)],
        us=1,
        grid=(1,),
        in_specs=[SMEM, pl.BlockSpec((k, r, wide), lambda i: (0, 0, 0))],
        out_specs=[half, half, pl.BlockSpec((16, 128), lambda i: (0, 0))],
    )(here.table, blocks)
    return kept, permute(sent, flip_lo), vectors


def pack_kernel(qkv_kept, qkv_sent, fc2_kept, fc2_sent, fc1, vectors, packed):
    qkv = (qkv_kept[...] + qkv_sent[...].astype(F32)).astype(BF)
    fc2 = (fc2_kept[...] + fc2_sent[...].astype(F32)).astype(BF)
    fc1 = jnp.sum(fc1[...].astype(F32), axis=0).astype(BF)
    for d in range(8):
        packed[d, :16, :2048] = qkv
        packed[d, 16:32, :2048] = fc1
        packed[d, 32:, :1024] = fc2[:16]
        packed[d, 32:, 1024:2048] = fc2[16:]
        packed[d, :16, 2048:] = vectors[...].astype(BF)
        packed[d, 16:, 2048:] = jnp.zeros((32, 128), BF)


def unpack_kernel(place_ref, own, other, qkv, out, fc1, fc2, *vectors):
    c = place_ref[0]
    low = jnp.where(c == 0, own[...], other[...]).astype(F32)
    high = jnp.where(c == 0, other[...], own[...]).astype(F32)
    for k, half in enumerate((low, high)):
        out[k, :, :512] = half[:8, 1536:2048]
        out[k, :, 512:] = half[8:16, 1536:2048]
        fc2[k, :16] = half[32:, :1024]
        fc2[k, 16:] = half[32:, 1024:2048]
        for f in range(8):
            at = f * 512 + k * 256
            fc1[:, at : at + 256] = half[16:32, f * 256 : (f + 1) * 256]
    terms = low[:16, 2048:] + high[:16, 2048:]

    start = pl.program_id(0) == 0
    for k, ref in enumerate(vectors):
        rows = terms[k : k + ref.shape[0]]
        ref[...] = jnp.where(start, rows, ref[...] + rows)

    first = lax.broadcasted_iota(jnp.int32, (16, 128), 1) < 64
    for p in range(12):
        left, right = low[:16, p * 128 : (p + 1) * 128], high[:16, p * 128 : (p + 1) * 128]
        qkv[:, p * 256 : p * 256 + 128] = jnp.where(first, left, pltpu.roll(right, 64, 1))
        qkv[:, p * 256 + 128 : (p + 1) * 256] = jnp.where(first, pltpu.roll(left, 64, 1), right)


def all_to_all(value, axis, groups=None):
    return lax.all_to_all(value, axis, 0, 0, tiled=True, axis_index_groups=groups)


def add_over(value, *moves):
    for move in moves:
        value = value + permute(value, move)
    return value


RATE = 0.51
ERFC = (
    0.28791757708249816,
    0.28415126012743,
    0.2790719172776486,
    0.055036978129087616,
    0.35846874221749475,
    -0.3591518512954867,
    0.09450494290776956,
)


def hidden_kernel(rows, weight, shift, hidden, slope):
    for k in range(weight.shape[1] // 256):
        at = slice(k * 256, (k + 1) * 256)
        u = jnp.dot(rows[...], weight[:, at], preferred_element_type=F32) + shift[:, at]
        bell = jnp.exp(-0.5 * u * u)
        t = 1.0 / (1.0 + (RATE * 0.5**0.5) * jnp.abs(u))
        tail = jnp.full_like(u, 0.5 * ERFC[-1])
        for coefficient in ERFC[-2::-1]:
            tail = tail * t + 0.5 * coefficient
        tail = tail * t * bell
        area = jnp.where(u >= 0, 1.0 - tail, tail)
        hidden[:, at] = (u * area).astype(BF)
        slope[:, at] = (area + u * bell * 0.3989422804014327).astype(BF)


def hidden_layer(rows, weight, shift):
    m, k = rows.shape
    n = weight.shape[1]
    cols = 512
    out = pl.BlockSpec((m, cols), lambda i: (0, i))
    return kernel_call(
        hidden_kernel,
        "hidden_layer",
        [struct((m, n), BF)] * 2,
        us=11,
        grid=(n // cols,),
        in_specs=[
            pl.BlockSpec((m, k), lambda i: (0, 0)),
            pl.BlockSpec((k, cols), lambda i: (0, i)),
            pl.BlockSpec((1, cols), lambda i: (0, i)),
        ],
        out_specs=[out, out],
    )(rows, weight, shift)


def d_pre_kernel(grad, weight, slope, d_pre, total):
    back = dot_nt(grad[...], weight[...]) * slope[...].astype(F32)
    low = back.astype(BF)
    d_pre[...] = low
    total[...] = jnp.sum(low.astype(F32), axis=0, keepdims=True)


def hidden_back(grad, weight, slope, late):
    m, k = grad.shape
    n = weight.shape[0]
    cols = 256
    out = pl.BlockSpec((m, cols), lambda i: (0, i))
    return kernel_call(
        d_pre_kernel,
        "hidden_back",
        [struct((m, n), BF), struct((1, n), F32)],
        late=late,
        us=6,
        grid=(n // cols,),
        in_specs=[
            pl.BlockSpec((m, k), lambda i: (0, 0)),
            pl.BlockSpec((cols, k), lambda i: (i, 0)),
            out,
        ],
        out_specs=[out, pl.BlockSpec((1, cols), lambda i: (0, i))],
    )(grad, weight, slope)


def head_pair(packed, query_shift, value_shift, p):
    at = slice(p * 128, (p + 1) * 128)
    query = (packed[:, p * 128 : (p + 1) * 128] + query_shift[:, at]).astype(BF)
    key = packed[:, 512 + p * 128 : 512 + (p + 1) * 128].astype(BF)
    value = (packed[:, 1024 + p * 128 : 1024 + (p + 1) * 128] + value_shift[:, at]).astype(BF)
    return query, key, value


SCALE = HEAD_DIM ** (-0.5)


def stacked(pair, first):
    zero = jnp.zeros_like(pair)
    return jnp.concatenate([jnp.where(first, pair, zero), jnp.where(first, zero, pair)])


def merged(both, first):
    half = both.shape[0] // 2
    return jnp.where(first, both[:half], both[half:])


def softmax_of(queries, key, blocked):
    scores = dot_nt(queries, key) * SCALE + blocked
    exps = jnp.exp(scores - jnp.max(scores, axis=-1, keepdims=True))
    return exps * (1.0 / jnp.sum(exps, axis=-1, keepdims=True))


def attention_kernel(packed, query_shift, value_shift, blocked, mixed):
    first = lax.broadcasted_iota(jnp.int32, (BLOCK, 128), 1) < 64
    both = jnp.concatenate([blocked[...], blocked[...]])
    for p in range(4):
        query, key, value = head_pair(packed, query_shift, value_shift, p)
        probs = softmax_of(stacked(query, first), key, both)
        parts = dot(probs.astype(BF), value)
        mixed[:, p * 128 : (p + 1) * 128] = merged(parts, first).astype(BF)


def attention(packed, query_shift, value_shift, blocked, late):
    rows = packed.shape[0]
    shift = pl.BlockSpec((1, 512), lambda i: (0, 0))
    return kernel_call(
        lambda *refs: attention_kernel(*refs[:-1]),
        "attention",
        [struct((rows, 512), BF), TOKEN],
        us=5,
        late=late,
        grid=(rows // BLOCK,),
        in_specs=[
            pl.BlockSpec((BLOCK, 1536), lambda i: (i, 0)),
            shift,
            shift,
            pl.BlockSpec((None, BLOCK, BLOCK), lambda i: (i, 0, 0)),
        ],
        out_specs=[pl.BlockSpec((BLOCK, 512), lambda i: (i, 0)), TOKEN_SPEC],
    )(packed, query_shift, value_shift, blocked)


def attention_back_kernel(packed, query_shift, value_shift, blocked, d_mixed, d_packed, total):
    first = lax.broadcasted_iota(jnp.int32, (BLOCK, 128), 1) < 64

    @pl.when(pl.program_id(0) == 0)
    def _():
        total[...] = jnp.zeros_like(total)

    both = jnp.concatenate([blocked[...], blocked[...]])
    for p in range(4):
        query, key, value = head_pair(packed, query_shift, value_shift, p)
        queries = stacked(query, first)
        grads = stacked(d_mixed[:, p * 128 : (p + 1) * 128], first)
        probs = softmax_of(queries, key, both)
        d_probs = dot_nt(grads, value)
        d_scores = probs * (d_probs - jnp.sum(probs * d_probs, axis=-1, keepdims=True))
        d_scores = d_scores.astype(BF)
        parts = (
            merged(dot(d_scores, key), first) * SCALE,
            dot_tn(d_scores, queries) * SCALE,
            dot_tn(probs.astype(BF), grads),
        )
        for k, part in enumerate(parts):
            at = slice(k * 512 + p * 128, k * 512 + (p + 1) * 128)
            low = part.astype(BF)
            d_packed[:, at] = low
            total[:, at] += jnp.sum(low.astype(F32), axis=0, keepdims=True)


def attention_back(packed, query_shift, value_shift, blocked, d_mixed, late):
    rows = packed.shape[0]
    shift = pl.BlockSpec((1, 512), lambda i: (0, 0))
    return kernel_call(
        attention_back_kernel,
        "attention_back",
        [struct((rows, 1536), BF), struct((1, 1536), F32)],
        us=16,
        late=late,
        grid=(rows // BLOCK,),
        in_specs=[
            pl.BlockSpec((BLOCK, 1536), lambda i: (i, 0)),
            shift,
            shift,
            pl.BlockSpec((None, BLOCK, BLOCK), lambda i: (i, 0, 0)),
            pl.BlockSpec((BLOCK, 512), lambda i: (i, 0)),
        ],
        out_specs=[
            pl.BlockSpec((BLOCK, 1536), lambda i: (i, 0)),
            pl.BlockSpec((1, 1536), lambda i: (0, 0)),
        ],
    )(packed, query_shift, value_shift, blocked, d_mixed)


def dot(left, right):
    return jnp.dot(left, right, preferred_element_type=F32)


def dot_nt(left, right):
    return lax.dot_general(left, right, (((1,), (1,)), ((), ())), preferred_element_type=F32)


def dot_tn(left, right):
    return lax.dot_general(left, right, (((0,), (0,)), ((), ())), preferred_element_type=F32)


def normalize(values):
    center = values - jnp.mean(values, axis=-1, keepdims=True)
    rstd = lax.rsqrt(jnp.mean(center * center, axis=-1, keepdims=True) + EPS)
    return center * rstd, rstd


def normalize_back(grad, yhat, rstd, gain):
    t = grad * gain
    return rstd * (
        t
        - jnp.mean(t, axis=-1, keepdims=True)
        - yhat * jnp.mean(t * yhat, axis=-1, keepdims=True)
    )


TILE = 160


def middle_kernel(part, other, tokens, keep, shift, gain, bias, middle, normed):
    attended = part[...].astype(F32) + other[...].astype(F32) + shift[...]
    rows = tokens[...].astype(F32) + keep[...] * attended
    middle[...] = rows
    yhat, _ = normalize(rows)
    normed[...] = (yhat * gain[...] + bias[...]).astype(BF)


def row_specs(count, width=1024):
    half = count // 2
    return (
        pl.BlockSpec((TILE, width), lambda i: (i, 0)),
        pl.BlockSpec((TILE, width), lambda i: (lax.rem(i + half, count), 0)),
        pl.BlockSpec((TILE, 1), lambda i: (i, 0)),
        pl.BlockSpec((1, width), lambda i: (0, 0)),
    )


def middle_layer(part, other, tokens, keep, shift, gain, bias):
    rows = part.shape[0]
    tile, swapped, column, vector = row_specs(rows // TILE)
    return kernel_call(
        middle_kernel,
        "middle_layer",
        [struct((rows, 1024), F32), struct((rows, 1024), BF)],
        us=6,
        pinned_out=(0,),
        grid=(rows // TILE,),
        in_specs=[tile, swapped, tile, column, vector, vector, vector],
        out_specs=[tile, tile],
    )(part, other, tokens, keep, shift, gain, bias)


def middle_back_kernel(shares, part, other, middle, cot, keep, gain, d_middle, d_attended, sums):
    step = pl.program_id(0)
    grad = part[...].astype(F32) + other[...].astype(F32)
    yhat, rstd = normalize(middle[...])
    incoming = cot[...].astype(F32) * shares[step // (pl.num_programs(0) // 2)]
    d_rows = incoming + normalize_back(grad, yhat, rstd, gain[...])
    d_middle[...] = d_rows
    low = (keep[...] * d_rows).astype(BF)
    d_attended[...] = low
    branch = (keep[...] * incoming).astype(BF)

    @pl.when(step == 0)
    def _():
        sums[...] = jnp.zeros_like(sums)

    @pl.when(step < pl.num_programs(0) // 2)
    def _():
        for k, v in enumerate((grad * yhat, grad, low.astype(F32), branch.astype(F32))):
            sums[k : k + 1, :] += jnp.sum(v, axis=0, keepdims=True)


def middle_back(shares, part, other, middle, cot, keep, gain, late):
    rows = part.shape[0]
    tile, swapped, column, vector = row_specs(rows // TILE)
    return kernel_call(
        middle_back_kernel,
        "middle_back",
        [struct((rows, 1024), F32), struct((rows, 1024), BF), struct((8, 1024), F32)],
        us=7,
        late=late,
        pinned=(3, 4),
        grid=(rows // TILE,),
        in_specs=[SMEM, tile, swapped, tile, tile, column, vector],
        out_specs=[tile, tile, pl.BlockSpec((8, 1024), lambda i: (0, 0))],
    )(shares, part, other, middle, cot, keep, gain)


def input_back_kernel(groups, shares, part, other, rows, d_middle, gain, cot, grad_rows, sums):
    grad = part[...].astype(F32) + other[...].astype(F32)
    yhat, rstd = normalize(rows[...].astype(F32))
    values = (d_middle[...] + normalize_back(grad, yhat, rstd, gain[...])).astype(BF)
    rest = (cot[...].astype(F32) * shares[0]).astype(BF)
    grad_rows[...] = spread(groups[0], values, rest)

    @pl.when(pl.program_id(0) == 0)
    def _():
        sums[...] = jnp.zeros_like(sums)

    for k, v in enumerate((grad * yhat, grad)):
        sums[k : k + 1, :] += jnp.sum(v, axis=0, keepdims=True)


def input_back(groups, shares, part, other, rows, d_middle, gain, cot, late):
    tile = pl.BlockSpec((BLOCK, 1024), lambda i: (i, 0))
    span = pl.BlockSpec((SPAN, 1024), lambda i: (i, 0))
    return kernel_call(
        input_back_kernel,
        "input_back",
        [struct(cot.shape, BF), struct((8, 1024), F32)],
        us=4,
        late=late,
        grid=(2,),
        in_specs=[
            SMEM,
            SMEM,
            tile,
            tile,
            tile,
            tile,
            pl.BlockSpec((1, 1024), lambda i: (0, 0)),
            span,
        ],
        out_specs=[span, pl.BlockSpec((8, 1024), lambda i: (0, 0))],
    )(groups, shares, part, other, rows, d_middle, gain, cot)


def body(
    tokens,
    norm1_gain,
    norm1_bias,
    qkv_weight,
    query_bias,
    value_bias,
    out_weight,
    out_bias,
    norm2_gain,
    norm2_bias,
    fc1_weight,
    fc1_bias,
    fc2_weight,
    fc2_bias,
    cotangent,
    group_of,
    keep_mask,
    group_tokens,
):
    here = Where()
    own_rows, width = tokens.shape
    c = here.c
    here.make_table()
    place_table = here.table

    vectors = (
        norm1_gain,
        norm1_bias,
        query_bias,
        value_bias,
        out_bias,
        norm2_gain,
        norm2_bias,
        fc2_bias,
        fc1_bias,
    )

    def whole(v):
        return pl.BlockSpec(v.shape, lambda i: (0,) * len(v.shape))

    shapes = [
        struct(shape, BF) for shape in ((8, 32, 1664), (64, 2048), (256, 1024), (64, 1024))
    ]
    weights = (qkv_weight, fc1_weight, fc2_weight, out_weight)
    qkv_rep, fc1_part, fc2_half, out_half = kernel_call(
        prepare_kernel,
        "prepare",
        shapes,
        us=3,
        pinned=range(1, 14),
        grid=(1,),
        in_specs=[SMEM] + [whole(v) for v in weights + vectors],
        out_specs=[whole(v) for v in shapes],
    )(place_table, *weights, *vectors)
    qkv_slab = all_to_all(qkv_rep, "fsdp")
    fc1_row = lax.all_gather(fc1_part, "fsdp", axis=0, axis_index_groups=X_GROUPS)
    out_all = lax.all_gather(out_half, "fsdp", axis=0, tiled=True)
    fc2_pair = assemble(
        here,
        "fc2_hi",
        [fc2_half, permute(fc2_half, flip_hi)],
        (2, 256, 1024),
        lambda o, t, n: o.at[t[HI] if n == 0 else 1 - t[HI]],
    )

    qkv_blocks = ring_blocks(qkv_slab, "z")
    fc1_blocks = ring_blocks(fc1_row, "y")
    fc2_blocks = ring_blocks(fc2_pair, "x")
    qkv_all = assemble(
        here,
        "qkv_z",
        qkv_blocks,
        (8, 4, 32, 1536),
        lambda o, t, n: o.at[:, source_in(t, Z, n)],
        lambda ref: ref.at[:, :, pl.ds(0, 1536)],
        late=fc2_blocks[3:],
    ).reshape(1024, 1536)
    (
        gain_one,
        shift_one,
        out_shift,
        gain_two,
        shift_two,
        fc2_shift,
        query_shift,
        value_shift,
        fc1_shift,
    ) = kernel_call(
        vectors_kernel,
        "vectors",
        [struct((1, 1024), F32)] * 6 + [struct((1, 512), F32)] * 2 + [struct((1, 2048), F32)],
        us=1,
        grid=(1,),
        in_specs=[SMEM, pl.BlockSpec((8, 16, 128), lambda i: (0, 0, 12))],
        out_specs=[pl.BlockSpec((1, n), lambda i: (0, 0)) for n in (1024,) * 6 + (512,) * 2 + (2048,)],
    )(place_table, qkv_slab)

    groups = jnp.stack([pick(group_of, here.dp), pick(group_of, here.dp + here.sign)])
    counts = group_tokens.astype(F32)
    shares = counts / jnp.sum(counts)
    shares = jnp.where(groups == 1, shares[1], shares[0])
    rows_low, cot, d_branch, mask_col, blocked = compact(
        groups,
        shares,
        tokens,
        permute(tokens, swap_core),
        cotangent,
        permute(cotangent, swap_core),
        keep_mask,
        permute(keep_mask, swap_core),
    )
    own_rows = 2 * BLOCK

    yhat_one, _ = normalize(rows_low.astype(F32))
    normed = (yhat_one * gain_one + shift_one).astype(BF)
    packed = dot(normed, qkv_all)
    mixed, attention_done = attention(packed, query_shift, value_shift, blocked, fc1_blocks[3:])
    attended = dot(mixed, out_all).astype(BF)
    middle, normed_two = middle_layer(
        attended, permute(attended, swap_core), rows_low, mask_col, out_shift, gain_two, shift_two
    )
    fc1_all = assemble(
        here,
        "fc1_y",
        fc1_blocks,
        (2, 4, 2, 64, 2048),
        lambda o, t, n: o.at[source_in(t, Y, n) // 2, :, lax.rem(source_in(t, Y, n), 2)],
        late=(attention_done,),
    ).reshape(1024, 2048)
    hidden, slope = hidden_layer(normed_two, fc1_all, fc1_shift)
    fc2_all = assemble(
        here,
        "fc2_x",
        fc2_blocks,
        (2, 4, 256, 1024),
        lambda o, t, n: o.at[:, source_in(t, X, n)],
        late=(attention_done,),
    ).reshape(2048, 1024)

    grad_fc2, fc2_done = grad_fc2_terms(hidden, d_branch, ())
    fc2_sum = lax.psum_scatter(
        grad_fc2.reshape(2048, 1024),
        "dp",
        scatter_dimension=0,
        axis_index_groups=Z_GROUPS,
        tiled=True,
    )
    d_pre, fc1_bias_sum = hidden_back(d_branch, fc2_all, slope, (fc2_done,))
    d_normed_two = dot_nt(d_pre, fc1_all).astype(BF)
    *grad_fc1, fc1_done = grad_fc1_terms(here, normed_two, d_pre, (d_normed_two,))
    fc1_arrived = permute(grad_fc1[0], ring_move("y"))
    d_middle, d_attended, middle_sums = middle_back(
        shares,
        d_normed_two,
        permute(d_normed_two, swap_core),
        middle,
        cot,
        mask_col,
        gain_two,
        (fc1_done,),
    )
    d_mixed = dot_nt(d_attended, out_all).astype(BF)
    d_packed, packed_sums = attention_back(
        packed, query_shift, value_shift, blocked, d_mixed, ()
    )
    fc1_sum, add_done = sum_of("fc1_add", (fc1_arrived, grad_fc1[1]), (packed_sums,))
    fc1_arrived = permute(fc1_sum, ring_move("y"))
    grad_qkv = grad_qkv_terms(normed, d_packed, mixed, d_attended, (add_done,))
    grad_qkv, d_packed, hidden = lax.optimization_barrier((grad_qkv, d_packed, hidden))
    qkv_sum = lax.psum_scatter(
        grad_qkv.reshape(1024, 2048),
        "dp",
        scatter_dimension=0,
        axis_index_groups=Z_GROUPS,
        tiled=True,
    ).reshape(8, 32, 2048)
    fc2_sum = all_to_all(fc2_sum.reshape(8, 64, 1024), "fsdp")
    fc2_kept, fc2_sent, _ = sum_and_halve(here, "fc2_lo", fc2_sum, 1024)
    fc1_sum, _ = sum_of("fc1_add", (fc1_arrived, grad_fc1[2]), (fc2_kept,))
    fc1_arrived = permute(fc1_sum, ring_move("y"))
    fc1_sum, _ = sum_of("fc1_add", (fc1_arrived, grad_fc1[3]))
    fc1_sum = all_to_all(fc1_sum, "fsdp", X_GROUPS)
    fc1_sum = sum_first("fc1_sum", fc1_sum).reshape(4, 16, 2048)
    fc1_sum = all_to_all(fc1_sum, "dp", Z_GROUPS)

    d_normed_sent = permute(dot_nt(d_packed[own_rows:], qkv_all).astype(BF), swap_core)
    d_normed_own = dot_nt(d_packed[:own_rows], qkv_all).astype(BF)
    input_grad, input_sums = input_back(
        groups,
        shares,
        d_normed_own,
        d_normed_sent,
        rows_low,
        d_middle,
        gain_one,
        cotangent,
        (),
    )

    branch_sent = permute(dot(hidden[own_rows:], fc2_all).astype(BF), swap_core)
    block_out, block_done = block_out_layer(
        groups,
        dot(hidden[:own_rows], fc2_all),
        branch_sent,
        middle,
        mask_col,
        fc2_shift,
        tokens,
    )

    vector_terms = kernel_call(
        vector_terms_kernel,
        "vector_terms",
        struct((8, 16, 128), F32),
        us=1,
        in_specs=[SMEM] + [VMEM] * 4,
        out_specs=VMEM,
    )(place_table, input_sums, packed_sums, middle_sums, fc1_bias_sum)
    qkv_sum = join(qkv_sum, vector_terms, (block_done, fc2_kept, fc1_sum))
    qkv_sum = all_to_all(qkv_sum, "fsdp")
    qkv_kept, qkv_sent, vector_sums = sum_and_halve(here, "qkv_lo", qkv_sum, 2048)
    sums = (qkv_kept, qkv_sent, fc2_kept, fc2_sent, fc1_sum, vector_sums)
    packed_slices = kernel_call(
        pack_kernel,
        "pack",
        struct((8, 48, 2176), BF),
        us=1.5,
        grid=(1,),
        in_specs=[whole(v) for v in sums],
        out_specs=whole(struct((8, 48, 2176), BF)),
    )(*sums)
    own = all_to_all(packed_slices, "dp", SLICE_GROUPS)
    half = pl.BlockSpec((None, 48, 2176), lambda i: (i, 0, 0))
    grad_qkv_weight, grad_out_weight, grad_fc1_weight, grad_fc2_weight, *vector_sums = kernel_call(
        unpack_kernel,
        "unpack",
        [
            struct((128, 3072), F32),
            struct((2, 8, 8, 1024), F32),
            struct((128, 4096), F32),
            struct((2, 8, 32, 1024), F32),
            *(struct((1, 128), F32),) * 8,
            struct((4, 128), F32),
        ],
        us=5,
        grid=(8,),
        in_specs=[SMEM, half, half],
        out_specs=[
            pl.BlockSpec((16, 3072), lambda i: (i, 0)),
            pl.BlockSpec((2, None, 8, 1024), lambda i: (0, i, 0, 0)),
            pl.BlockSpec((16, 4096), lambda i: (lax.rem(i, 2) * 4 + i // 2, 0)),
            pl.BlockSpec((2, None, 32, 1024), lambda i: (0, i, 0, 0)),
            *(pl.BlockSpec((1, 128), lambda i: (0, 0)),) * 8,
            pl.BlockSpec((4, 128), lambda i: (0, 0)),
        ],
    )(place_table, own, permute(own, swap_core))
    return (
        block_out,
        input_grad,
        vector_sums[0].reshape(128),
        vector_sums[1].reshape(128),
        grad_qkv_weight,
        vector_sums[2].reshape(128),
        vector_sums[3].reshape(128),
        grad_out_weight.reshape(128, 1024),
        vector_sums[4].reshape(128),
        vector_sums[5].reshape(128),
        vector_sums[6].reshape(128),
        grad_fc1_weight,
        vector_sums[8].reshape(512),
        grad_fc2_weight.reshape(512, 1024),
        vector_sums[7].reshape(128),
    )


def solution(mesh):
    rows, cols, both = P("fsdp", None), P("fsdp"), ("dp", "fsdp")
    in_specs = (
        P(both, None),
        cols,
        cols,
        rows,
        cols,
        cols,
        rows,
        cols,
        cols,
        cols,
        rows,
        cols,
        rows,
        cols,
        P(both, None),
        P(),
        P(both),
        P(),
    )
    out_specs = (
        P(both, None),
        P(both, None),
        cols,
        cols,
        rows,
        cols,
        cols,
        rows,
        cols,
        cols,
        cols,
        rows,
        cols,
        rows,
        cols,
    )
    return jax.shard_map(body, mesh=mesh, in_specs=in_specs, out_specs=out_specs, check_vma=False)
```

```python
import functools

import jax
import jax.numpy as jnp
from jax import lax
from jax.experimental import pallas as pl
from jax.experimental.pallas import tpu as pltpu
from jax.sharding import PartitionSpec as P

HEAD_DIM = 64
SLOT_S = 64
SLOT_L = 192
SPAN = 192
MOST_S = 50
USED = SPAN // SLOT_S * MOST_S
BLOCK = 160
EPS = 1e-06
AXES = ("dp", "fsdp")
BF = jnp.bfloat16
F32 = jnp.float32

Z_GROUPS = [[lo * 8 + 2 * z + c for z in range(4)] for lo in range(2) for c in range(2)]
SLICE_GROUPS = [[lo * 8 + 2 * z + c for z in range(4) for lo in range(2)] for c in range(2)]
X_GROUPS = [[0, 1, 2, 3], [4, 5, 6, 7]]


def place(linear):
    dp, fs = divmod(linear, 8)
    return fs % 4, (fs // 4) * 2 + dp // 8, (dp // 2) % 4, dp % 2


def linear_of(x, y, z, c):
    x, y, z = x % 4, y % 4, z % 4
    return (((y % 2) * 4 + z) * 2 + c) * 8 + (y // 2) * 4 + x


def permute(value, move):
    return lax.ppermute(
        value, AXES, [(l, linear_of(*move(*place(l)))) for l in range(128)]
    )


def ring_move(axis):
    def move(x, y, z, c):
        s = 1 - 2 * c
        return (x + s * (axis == "x"), y + s * (axis == "y"), z + s * (axis == "z"), c)

    return move


def shift(axis, s):
    def move(x, y, z, c):
        return (x + s * (axis == "x"), y + s * (axis == "y"), z + s * (axis == "z"), c)

    return move


HOPS = (1, 2, 3)


def swap_core(x, y, z, c):
    return x, y, z, 1 - c


def flip_hi(x, y, z, c):
    return x, 3 - y, z, c


def flip_lo(x, y, z, c):
    return x, y ^ 1, z, c


class Where:
    def __init__(self):
        dp, fs = lax.axis_index("dp"), lax.axis_index("fsdp")
        self.dp, self.fs = dp, fs
        self.c = dp % 2
        self.z = (dp // 2) % 4
        self.lo = dp // 8
        self.x = fs % 4
        self.hi = fs // 4
        self.y = self.hi * 2 + self.lo
        self.sign = 1 - 2 * self.c

    def along(self, axis):
        return {"x": self.x, "y": self.y, "z": self.z}[axis]

    def source(self, axis, step):
        return lax.rem(self.along(axis) - self.sign * step + 8, 4)

    def make_table(self):
        self.table = jnp.stack([self.c, self.z, self.lo, self.hi, self.x, self.y]).astype(jnp.int32)


C, Z, LO, HI, X, Y = range(6)


def source_in(table, at, step):
    return lax.rem(table[at] - (1 - 2 * table[C]) * step + 8, 4)


def place_in(table, at, r):
    return lax.rem(table[at] + r + 4, 4)


def pick(stacked, index, axis=0):
    return lax.dynamic_index_in_dim(stacked, index, axis, keepdims=False)


def ring_gather(here, value, axis, buffer, put):
    for step in range(4):
        if step:
            value = permute(value, ring_move(axis))
        buffer = put(buffer, value, here.source(axis, step))
    return buffer


def ring_reduce(here, axis, term):
    total = term(here.source(axis, 1))
    for step in range(2, 5):
        total = permute(total, ring_move(axis))
        total = (total.astype(F32) + term(here.source(axis, step)).astype(F32)).astype(BF)
    return total


def ring_blocks(value, axis):
    blocks = [value]
    for _ in range(3):
        blocks.append(permute(blocks[-1], ring_move(axis)))
    return blocks


def exchange(blocks, axis):
    return [blocks[0]] + [permute(blocks[r], shift(axis, r)) for r in HOPS]


ANY = pl.BlockSpec(memory_space=pl.ANY)
SMEM = pl.BlockSpec(memory_space=pltpu.SMEM)
VMEM = pl.BlockSpec(memory_space=pltpu.VMEM)


TOKEN = jax.ShapeDtypeStruct((8, 128), jnp.float32)
TOKEN_SPEC = pl.BlockSpec((8, 128), lambda i: (0, 0))


def in_hbm(value):
    return pltpu.with_memory_space_constraint(value, pltpu.HBM)


def kernel_call(
    kernel,
    name,
    out_shape,
    in_specs,
    us=1,
    vmem=16 << 20,
    pinned=(),
    pinned_out=(),
    late=(),
    **kwargs,
):
    count = len(in_specs)
    if pinned_out:
        shapes = out_shape if isinstance(out_shape, list) else [out_shape]
        shapes = [
            pltpu.HBM(s.shape, s.dtype) if n in pinned_out else s for n, s in enumerate(shapes)
        ]
        out_shape = shapes if isinstance(out_shape, list) else shapes[0]

    def body(*refs):
        kernel(*refs[:count], *refs[count + len(late) :])

    call = pl.pallas_call(
        body,
        out_shape=out_shape,
        in_specs=list(in_specs) + [ANY] * len(late),
        name=name,
        compiler_params=pltpu.CompilerParams(vmem_limit_bytes=vmem),
        cost_estimate=pl.CostEstimate(
            flops=int(us * 0.25 * 1.15e9), bytes_accessed=1 << 16, transcendentals=0
        ),
        **kwargs,
    )

    def run(*args):
        return call(
            *(in_hbm(a) if n in pinned else a for n, a in enumerate(args)),
            *(in_hbm(a) if a.size > 1 << 16 else a for a in late),
        )

    return run


def struct(shape, dtype):
    return jax.ShapeDtypeStruct(shape, dtype)


def assemble(here, name, parts, shape, target, source=lambda ref: ref, late=()):
    def kernel(table, *refs):
        ins, out, sems = refs[: len(parts)], refs[len(parts)], refs[len(parts) + 1]
        copies = [
            pltpu.make_async_copy(source(ins[n]), target(out, table, n), sems.at[n])
            for n in range(len(parts))
        ]
        for copy in copies:
            copy.start()
        for copy in copies:
            copy.wait()

    return kernel_call(
        kernel,
        name,
        struct(shape, BF),
        in_specs=[SMEM] + [ANY] * len(parts),
        us=2.5,
        pinned=range(1, 1 + len(parts)),
        late=late,
        out_specs=VMEM,
        scratch_shapes=[pltpu.SemaphoreType.DMA((len(parts),))],
    )(here.table, *parts)


def lane_halves(c, left, right):
    first = lax.broadcasted_iota(jnp.int32, left.shape, 1) < 64
    low = jnp.where(first, left, pltpu.roll(right, 64, 1))
    high = jnp.where(first, pltpu.roll(left, 64, 1), right)
    return jnp.where(c == 0, low, high)


def prepare_kernel(place_ref, qkv, fc1, fc2, out, *refs):
    vectors, (qkv_rep, fc1_part, fc2_half, out_half) = refs[:9], refs[9:]
    c, z, lo = place_ref[0], place_ref[1], place_ref[2]
    rows = pl.ds(pl.multiple_of(z * 32, 32), 32)
    for g in range(12):
        left = qkv[rows, g * 256 : g * 256 + 128].astype(F32)
        right = qkv[rows, g * 256 + 128 : g * 256 + 256].astype(F32)
        half = lane_halves(c, left, right).astype(BF)
        for d in range(8):
            qkv_rep[d, :, g * 128 : (g + 1) * 128] = half
    packed = [ref[...].astype(F32).reshape(-1, 128) for ref in vectors]
    packed = jnp.concatenate(packed + [jnp.zeros((20, 128), F32)]).astype(BF)
    for d in range(8):
        qkv_rep[d, :, 1536:] = packed
    out_half[...] = out[pl.ds(pl.multiple_of(c * 64, 64), 64), :]
    rows = pl.ds(pl.multiple_of(lo * 64, 64), 64)
    for f in range(8):
        half = jnp.where(
            c == 0, fc1[rows, f * 512 : f * 512 + 256], fc1[rows, f * 512 + 256 : (f + 1) * 512]
        )
        fc1_part[:, f * 256 : (f + 1) * 256] = half
    fc2_half[...] = fc2[pl.ds(pl.multiple_of(c * 256, 256), 256), :]


def row_choice(group):
    i = lax.broadcasted_iota(jnp.int32, (BLOCK, SPAN), 0)
    j = lax.broadcasted_iota(jnp.int32, (BLOCK, SPAN), 1)
    slot = (i >= MOST_S).astype(jnp.int32) + (i >= 2 * MOST_S).astype(jnp.int32)
    source = jnp.where(group == 1, i, i + slot * (SLOT_S - MOST_S))
    return jnp.where((j == source) & (i < USED), 1.0, 0.0)


def chosen_rows(group):
    j = lax.broadcasted_iota(jnp.int32, (SPAN, 1), 0)
    slot = (j >= SLOT_S).astype(jnp.int32) + (j >= 2 * SLOT_S).astype(jnp.int32)
    place = jnp.where(group == 1, j, j - slot * SLOT_S)
    return place < jnp.where(group == 1, USED, MOST_S)


def image_of(group, shape, axis):
    i = lax.broadcasted_iota(jnp.int32, shape, axis)
    slot = (i >= MOST_S).astype(jnp.int32) + (i >= 2 * MOST_S).astype(jnp.int32)
    return jnp.where(group == 1, 0, slot)


def compact_kernel(
    groups, shares, tokens, tokens_other, cot, cot_other, keep, keep_other, rows, cots, d_branch, column, blocked
):
    step = pl.program_id(0)
    own = step < 2
    group = groups[step // 2]
    choice = row_choice(group)
    low = choice.astype(BF)
    kept = jnp.where(own, keep[...], keep_other[...]).astype(F32)
    rows[...] = dot(low, jnp.where(own, tokens[...], tokens_other[...])).astype(BF)
    chosen = dot(low, jnp.where(own, cot[...], cot_other[...]))
    cots[...] = chosen.astype(BF)
    mask = jnp.sum(choice * kept, axis=-1, keepdims=True)
    column[...] = mask
    d_branch[...] = (mask * (chosen * shares[step // 2])).astype(BF)
    across = dot_nt(jnp.broadcast_to(kept, (16, SPAN)).astype(BF), low)[:1]
    same = image_of(group, (BLOCK, BLOCK), 0) == image_of(group, (BLOCK, BLOCK), 1)
    blocked[...] = jnp.where(same & (across > 0.5), 0.0, -1e30)


def compact(groups, shares, tokens, tokens_other, cot, cot_other, keep, keep_other):
    def mine(shape, rows):
        return pl.BlockSpec(shape, lambda i: (jnp.minimum(i, 1),) + (0,) * (len(shape) - 1))

    def theirs(shape, rows):
        return pl.BlockSpec(shape, lambda i: (jnp.maximum(i - 2, 0),) + (0,) * (len(shape) - 1))

    row = (SPAN, 1024)
    flag = (None, 1, SPAN)
    tile = pl.BlockSpec((BLOCK, 1024), lambda i: (i, 0))
    return kernel_call(
        compact_kernel,
        "compact",
        [struct((4 * BLOCK, 1024), BF)] * 3
        + [struct((4 * BLOCK, 1), F32), struct((4, BLOCK, BLOCK), F32)],
        us=5,
        grid=(4,),
        in_specs=[
            SMEM,
            SMEM,
            mine(row, 2),
            theirs(row, 2),
            mine(row, 2),
            theirs(row, 2),
            mine(flag, 2),
            theirs(flag, 2),
        ],
        out_specs=[
            tile,
            tile,
            tile,
            pl.BlockSpec((BLOCK, 1), lambda i: (i, 0)),
            pl.BlockSpec((None, BLOCK, BLOCK), lambda i: (i, 0, 0)),
        ],
    )(
        groups,
        shares,
        tokens,
        tokens_other,
        cot,
        cot_other,
        keep.reshape(2, 1, SPAN),
        keep_other.reshape(2, 1, SPAN),
    )


def spread(group, values, rest):
    back = dot_tn(row_choice(group).astype(BF), values)
    return jnp.where(chosen_rows(group), back, rest.astype(F32)).astype(BF)


def block_out_kernel(groups, branch, sent, middle, column, shift, tokens, out):
    total = branch[...] + sent[...].astype(F32) + shift[...]
    values = (middle[...] + column[...] * total).astype(BF)
    out[...] = spread(groups[0], values, tokens[...])


def block_out_layer(groups, branch, sent, middle, column, shift, tokens):
    tile = pl.BlockSpec((BLOCK, 1024), lambda i: (i, 0))
    span = pl.BlockSpec((SPAN, 1024), lambda i: (i, 0))
    return kernel_call(
        lambda *refs: block_out_kernel(*refs[:-1]),
        "block_out",
        [struct(tokens.shape, BF), TOKEN],
        us=4,
        grid=(2,),
        in_specs=[
            SMEM,
            tile,
            tile,
            tile,
            pl.BlockSpec((BLOCK, 1), lambda i: (i, 0)),
            pl.BlockSpec((1, 1024), lambda i: (0, 0)),
            span,
        ],
        out_specs=[span, TOKEN_SPEC],
    )(groups, branch, sent, middle, column, shift, tokens)


def vectors_kernel(place_ref, packed, *outs):
    c = place_ref[0]
    rows = [packed[f].astype(F32) for f in range(8)]

    def row(f, k):
        return rows[f][k : k + 1, :]

    for out, k in zip(outs[:6], (0, 1, 4, 5, 6, 7)):
        for f in range(8):
            out[:, f * 128 : (f + 1) * 128] = row(f, k)
    for out, k in zip(outs[6:8], (2, 3)):
        for p in range(4):
            out[:, p * 128 : (p + 1) * 128] = lane_halves(c, row(2 * p, k), row(2 * p + 1, k))
    for f in range(8):
        for j in range(2):
            at = f * 256 + j * 128
            outs[8][:, at : at + 128] = jnp.where(c == 0, row(f, 8 + j), row(f, 10 + j))


def vector_terms_kernel(place_ref, input_sums, packed_sums, middle_sums, fc1_sums, out):
    c = place_ref[0]
    first = lax.broadcasted_iota(jnp.int32, (1, 128), 1) < 64
    zero = jnp.zeros((1, 128), F32)
    out[...] = jnp.zeros_like(out)
    whole = (
        (0, input_sums, 0),
        (1, input_sums, 1),
        (4, middle_sums, 2),
        (5, middle_sums, 0),
        (6, middle_sums, 1),
        (7, middle_sums, 3),
    )
    for f in range(8):
        for k, ref, r in whole:
            out[f, k : k + 1, :] = ref[r : r + 1, f * 128 : (f + 1) * 128]
        for j in range(4):
            at = f * 256 + (j % 2) * 128
            out[f, 8 + j : 9 + j, :] = jnp.where(c == j // 2, fc1_sums[:, at : at + 128], zero)
    for k, base in ((2, 0), (3, 1024)):
        for p in range(4):
            pair = packed_sums[:, base + p * 128 : base + (p + 1) * 128]
            turned = pltpu.roll(pair, 64, 1)
            for e in range(2):
                low = jnp.where(first, pair if e == 0 else turned, zero)
                high = jnp.where(first, zero, turned if e == 0 else pair)
                out[2 * p + e, k : k + 1, :] = jnp.where(c == 0, low, high)


def grad_fc2_kernel(left, right, out):
    terms = dot_tn(left[...], right[...]).astype(BF)
    for x in range(2):
        for z in range(4):
            at = (4 * x + z) * 64
            out[z, x] = terms[at : at + 64]


def grad_fc2_terms(hidden, d_branch, late):
    m = hidden.shape[0]
    return kernel_call(
        lambda *refs: grad_fc2_kernel(*refs[:-1]),
        "grad_fc2",
        [struct((4, 8, 64, 1024), BF), TOKEN],
        us=5,
        late=late,
        pinned_out=(0,),
        grid=(4,),
        in_specs=[
            pl.BlockSpec((m, 512), lambda i: (0, i)),
            pl.BlockSpec((m, 1024), lambda i: (0, 0)),
        ],
        out_specs=[
            pl.BlockSpec((4, 2, 64, 1024), lambda i: (0, i, 0, 0)),
            TOKEN_SPEC,
        ],
    )(hidden, d_branch)


def grad_fc1_kernel(table, left, right, *refs):
    along_y, along_x = refs[:4], refs[4:8]
    terms = dot_tn(left[...], right[...]).astype(BF)
    hi, pair = lax.rem(pl.program_id(0), 2), pl.program_id(0) // 2
    for n in range(4):
        y, x = source_in(table, Y, n + 1), source_in(table, X, n + 1)
        for e in range(2):

            @pl.when(y == hi * 2 + e)
            def _():
                for k in range(2):
                    at = (2 * k + e) * 64
                    along_y[n][k] = terms[at : at + 64, :1024]

            @pl.when(x == pair * 2 + e)
            def _():
                along_x[n][hi] = terms[e * 128 : (e + 1) * 128, 1024:]


def grad_fc1_terms(here, normed, d_pre, late):
    m = normed.shape[0]
    results = kernel_call(
        grad_fc1_kernel,
        "grad_fc1",
        [struct((4, 64, 1024), BF)] * 4 + [struct((2, 128, 1024), BF)] * 4 + [TOKEN],
        us=5,
        late=late,
        pinned_out=range(8),
        grid=(4,),
        in_specs=[
            SMEM,
            pl.BlockSpec((m, 256), lambda i: (0, lax.rem(i, 2) * 2 + i // 2)),
            pl.BlockSpec((m, 2048), lambda i: (0, 0)),
        ],
        out_specs=[pl.BlockSpec((2, 64, 1024), lambda i: (i // 2, 0, 0))] * 4
        + [pl.BlockSpec((2, 128, 1024), lambda i: (0, 0, 0))] * 4
        + [TOKEN_SPEC],
    )(here.table, normed, d_pre)
    return results[:4], results[4:8], results[8]


def grad_qkv_kernel(normed, d_packed, mixed, d_attended, out):
    qkv = dot_tn(normed[...], d_packed[...]).astype(BF)
    rest = dot_tn(mixed[...], d_attended[...])
    for f in range(2):
        parts = []
        for k in range(8):
            rows = rest[f * 64 + k * 8 : f * 64 + (k + 1) * 8]
            parts += [rows[:, :512], rows[:, 512:]]
        parts = jnp.concatenate(parts).astype(BF)
        for z in range(4):
            out[z, f, :, :1536] = qkv[f * 128 + z * 32 : f * 128 + (z + 1) * 32]
            out[z, f, :, 1536:] = parts[z * 32 : (z + 1) * 32]


def grad_qkv_terms(normed, d_packed, mixed, d_attended, late):
    m = normed.shape[0]
    return kernel_call(
        grad_qkv_kernel,
        "grad_qkv",
        struct((4, 8, 32, 2048), BF),
        us=5,
        late=late,
        pinned_out=(0,),
        grid=(4,),
        in_specs=[
            pl.BlockSpec((m, 256), lambda i: (0, i)),
            pl.BlockSpec((m, 1536), lambda i: (0, 0)),
            pl.BlockSpec((m, 128), lambda i: (0, i)),
            pl.BlockSpec((m, 1024), lambda i: (0, 0)),
        ],
        out_specs=pl.BlockSpec((4, 2, 32, 2048), lambda i: (0, i, 0, 0)),
    )(normed, d_packed, mixed, d_attended)


def total_of(refs):
    total = refs[0][...].astype(F32)
    for ref in refs[1:]:
        total = total + ref[...].astype(F32)
    return total


def fc2_split_kernel(table, blocks, *outs):
    for r, out in enumerate(outs[:4]):
        x = place_in(table, X, r)
        for hi in range(2):
            out[hi] = blocks[hi * 4 + x]


def fc2_split(here, blocks):
    return kernel_call(
        fc2_split_kernel,
        "fc2_split",
        [struct((2, 64, 1024), BF)] * 4 + [TOKEN],
        us=1,
        grid=(1,),
        in_specs=[SMEM, pl.BlockSpec((8, 64, 1024), lambda i: (0, 0, 0))],
        out_specs=[pl.BlockSpec((2, 64, 1024), lambda i: (0, 0, 0))] * 4 + [TOKEN_SPEC],
    )(here.table, blocks)


def fc2_sum_kernel(table, *refs):
    ins, (kept, sent) = refs[:4], refs[4:]
    total = total_of(ins)
    kept[...] = jnp.where(table[HI] == 0, total[0], total[1])
    sent[...] = jnp.where(table[HI] == 0, total[1], total[0]).astype(BF)


def fc2_add_kernel(table, own, arrived, kept, sent):
    total = own[...] + arrived[...].astype(F32)
    low, high = total[:32], total[32:]
    kept[...] = jnp.where(table[LO] == 0, low, high)
    sent[...] = jnp.where(table[LO] == 0, high, low).astype(BF)


def fc2_sums(here, blocks):
    block = pl.BlockSpec((2, 64, 1024), lambda i: (0, 0, 0))
    half = pl.BlockSpec((64, 1024), lambda i: (0, 0))
    part = pl.BlockSpec((32, 1024), lambda i: (0, 0))
    kept, sent = kernel_call(
        fc2_sum_kernel,
        "fc2_sum",
        [struct((64, 1024), F32), struct((64, 1024), BF)],
        us=1,
        grid=(1,),
        in_specs=[SMEM] + [block] * 4,
        out_specs=[half, half],
    )(here.table, *blocks)
    kept, sent = kernel_call(
        fc2_add_kernel,
        "fc2_add",
        [struct((32, 1024), F32), struct((32, 1024), BF)],
        us=1,
        grid=(1,),
        in_specs=[SMEM, half, half],
        out_specs=[part, part],
    )(here.table, kept, permute(sent, flip_hi))
    return kept, permute(sent, flip_lo)


def add_kernel(y, y_terms, x, x_terms, y_out, x_out, done):
    y_out[...] = total_of((y, y_terms)).astype(BF)
    x_out[...] = total_of((x, x_terms)).astype(BF)


def add_both(arrived, terms, late=()):
    y = pl.BlockSpec((2, 64, 1024), lambda i: (i, 0, 0))
    x = pl.BlockSpec((1, 128, 1024), lambda i: (i, 0, 0))
    *sums, done = kernel_call(
        add_kernel,
        "fc1_add",
        [struct((4, 64, 1024), BF), struct((2, 128, 1024), BF), TOKEN],
        us=1,
        late=late,
        grid=(2,),
        in_specs=[y, y, x, x],
        out_specs=[y, x, TOKEN_SPEC],
    )(arrived[0], terms[0], arrived[1], terms[1])
    return sums, done


def ring_both(sums):
    return [permute(v, ring_move(axis)) for v, axis in zip(sums, "yx")]


def last_kernel(table, y, y_terms, x, x_terms, y_out, kept, sent):
    y_out[...] = total_of((y, y_terms)).astype(BF)
    total = total_of((x, x_terms))
    kept[...] = jnp.where(table[HI] == 0, total[0], total[1])
    sent[...] = jnp.where(table[HI] == 0, total[1], total[0]).astype(BF)


def last_both(here, arrived, terms, late):
    y = pl.BlockSpec((4, 64, 1024), lambda i: (0, 0, 0))
    x = pl.BlockSpec((2, 128, 1024), lambda i: (0, 0, 0))
    half = pl.BlockSpec((128, 1024), lambda i: (0, 0))
    return kernel_call(
        last_kernel,
        "fc1_last",
        [struct((4, 64, 1024), BF), struct((128, 1024), F32), struct((128, 1024), BF)],
        us=1,
        late=late,
        grid=(1,),
        in_specs=[SMEM, y, y, x, x],
        out_specs=[y, half, half],
    )(here.table, arrived[0], terms[0], arrived[1], terms[1])


def slices_kernel(table, y_blocks, x_kept, x_sent, out):
    y_sum = jnp.sum(y_blocks[...].astype(F32), axis=0).astype(BF)
    x_sum = (x_kept[...] + x_sent[...].astype(F32)).astype(BF)
    for k in range(8):
        z, lo = k // 2, k % 2
        rows = y_sum[z * 16 : (z + 1) * 16]
        out[k, :, :1024] = jnp.where(table[LO] == lo, rows, jnp.zeros_like(rows))
        at = lo * 64 + z * 16
        out[k, :, 1024:] = x_sum[at : at + 16]


def fc1_slices(here, y_blocks, x_kept, x_sent):
    def whole(*shape):
        return pl.BlockSpec(shape, lambda i: (0,) * len(shape))

    return kernel_call(
        slices_kernel,
        "fc1_slices",
        struct((8, 16, 2048), BF),
        us=1,
        grid=(1,),
        in_specs=[SMEM, whole(4, 64, 1024), whole(128, 1024), whole(128, 1024)],
        out_specs=whole(8, 16, 2048),
    )(here.table, y_blocks, x_kept, x_sent)


def join_kernel(qkv, vectors, out):
    for f in range(8):
        out[f, :, :2048] = qkv[f]
        out[f, :16, 2048:] = vectors[f].astype(BF)
        out[f, 16:, 2048:] = jnp.zeros((16, 128), BF)


def join(qkv, vectors, late):
    return kernel_call(
        join_kernel,
        "join",
        struct((8, 32, 2176), BF),
        us=1,
        late=late,
        grid=(1,),
        in_specs=[
            pl.BlockSpec((8, 32, 2048), lambda i: (0, 0, 0)),
            pl.BlockSpec((8, 16, 128), lambda i: (0, 0, 0)),
        ],
        out_specs=pl.BlockSpec((8, 32, 2176), lambda i: (0, 0, 0)),
    )(qkv, vectors)


def split_kernel(table, blocks, kept, sent, vectors):
    total = jnp.sum(blocks[...].astype(F32), axis=0)
    half, n = kept.shape
    low, high = total[:half, :n], total[half:, :n]
    kept[...] = jnp.where(table[LO] == 0, low, high)
    sent[...] = jnp.where(table[LO] == 0, high, low).astype(BF)
    if total.shape[1] > n:
        vectors[...] = total[:16, n:]


def sum_and_halve(here, name, blocks, n):
    k, r, wide = blocks.shape
    half = pl.BlockSpec((r // 2, n), lambda i: (0, 0))
    kept, sent, vectors = kernel_call(
        split_kernel,
        name,
        [struct((r // 2, n), F32), struct((r // 2, n), BF), struct((16, 128), F32)],
        us=1,
        grid=(1,),
        in_specs=[SMEM, pl.BlockSpec((k, r, wide), lambda i: (0, 0, 0))],
        out_specs=[half, half, pl.BlockSpec((16, 128), lambda i: (0, 0))],
    )(here.table, blocks)
    return kept, permute(sent, flip_lo), vectors


def pack_kernel(qkv_kept, qkv_sent, fc2_kept, fc2_sent, fc1, vectors, packed):
    qkv = (qkv_kept[...] + qkv_sent[...].astype(F32)).astype(BF)
    fc2 = (fc2_kept[...] + fc2_sent[...].astype(F32)).astype(BF)
    fc1 = jnp.sum(fc1[...].astype(F32), axis=0).astype(BF)
    for d in range(8):
        packed[d, :16, :2048] = qkv
        packed[d, 16:32, :2048] = fc1
        packed[d, 32:, :1024] = fc2[:16]
        packed[d, 32:, 1024:2048] = fc2[16:]
        packed[d, :16, 2048:] = vectors[...].astype(BF)
        packed[d, 16:, 2048:] = jnp.zeros((32, 128), BF)


def unpack_kernel(place_ref, own, other, qkv, out, fc1, fc2, *vectors):
    c = place_ref[0]
    low = jnp.where(c == 0, own[...], other[...]).astype(F32)
    high = jnp.where(c == 0, other[...], own[...]).astype(F32)
    for k, half in enumerate((low, high)):
        out[k, :, :512] = half[:8, 1536:2048]
        out[k, :, 512:] = half[8:16, 1536:2048]
        fc2[k, :16] = half[32:, :1024]
        fc2[k, 16:] = half[32:, 1024:2048]
        for f in range(8):
            at = f * 512 + k * 256
            fc1[:, at : at + 256] = half[16:32, f * 256 : (f + 1) * 256]
    terms = low[:16, 2048:] + high[:16, 2048:]

    start = pl.program_id(0) == 0
    for k, ref in enumerate(vectors):
        rows = terms[k : k + ref.shape[0]]
        ref[...] = jnp.where(start, rows, ref[...] + rows)

    first = lax.broadcasted_iota(jnp.int32, (16, 128), 1) < 64
    for p in range(12):
        left, right = low[:16, p * 128 : (p + 1) * 128], high[:16, p * 128 : (p + 1) * 128]
        qkv[:, p * 256 : p * 256 + 128] = jnp.where(first, left, pltpu.roll(right, 64, 1))
        qkv[:, p * 256 + 128 : (p + 1) * 256] = jnp.where(first, pltpu.roll(left, 64, 1), right)


def all_to_all(value, axis, groups=None):
    return lax.all_to_all(value, axis, 0, 0, tiled=True, axis_index_groups=groups)


def add_over(value, *moves):
    for move in moves:
        value = value + permute(value, move)
    return value


RATE = 0.51
ERFC = (
    0.28791757708249816,
    0.28415126012743,
    0.2790719172776486,
    0.055036978129087616,
    0.35846874221749475,
    -0.3591518512954867,
    0.09450494290776956,
)


def hidden_kernel(rows, weight, shift, hidden, slope):
    for k in range(weight.shape[1] // 256):
        at = slice(k * 256, (k + 1) * 256)
        u = jnp.dot(rows[...], weight[:, at], preferred_element_type=F32) + shift[:, at]
        bell = jnp.exp(-0.5 * u * u)
        t = 1.0 / (1.0 + (RATE * 0.5**0.5) * jnp.abs(u))
        tail = jnp.full_like(u, 0.5 * ERFC[-1])
        for coefficient in ERFC[-2::-1]:
            tail = tail * t + 0.5 * coefficient
        tail = tail * t * bell
        area = jnp.where(u >= 0, 1.0 - tail, tail)
        hidden[:, at] = (u * area).astype(BF)
        slope[:, at] = (area + u * bell * 0.3989422804014327).astype(BF)


def hidden_layer(rows, weight, shift):
    m, k = rows.shape
    n = weight.shape[1]
    cols = 512
    out = pl.BlockSpec((m, cols), lambda i: (0, i))
    return kernel_call(
        hidden_kernel,
        "hidden_layer",
        [struct((m, n), BF)] * 2,
        us=11,
        grid=(n // cols,),
        in_specs=[
            pl.BlockSpec((m, k), lambda i: (0, 0)),
            pl.BlockSpec((k, cols), lambda i: (0, i)),
            pl.BlockSpec((1, cols), lambda i: (0, i)),
        ],
        out_specs=[out, out],
    )(rows, weight, shift)


def d_pre_kernel(grad, weight, slope, d_pre, total):
    back = dot_nt(grad[...], weight[...]) * slope[...].astype(F32)
    low = back.astype(BF)
    d_pre[...] = low
    total[...] = jnp.sum(low.astype(F32), axis=0, keepdims=True)


def hidden_back(grad, weight, slope, late):
    m, k = grad.shape
    n = weight.shape[0]
    cols = 256
    out = pl.BlockSpec((m, cols), lambda i: (0, i))
    return kernel_call(
        d_pre_kernel,
        "hidden_back",
        [struct((m, n), BF), struct((1, n), F32)],
        late=late,
        us=6,
        grid=(n // cols,),
        in_specs=[
            pl.BlockSpec((m, k), lambda i: (0, 0)),
            pl.BlockSpec((cols, k), lambda i: (i, 0)),
            out,
        ],
        out_specs=[out, pl.BlockSpec((1, cols), lambda i: (0, i))],
    )(grad, weight, slope)


def head_pair(packed, query_shift, value_shift, p):
    at = slice(p * 128, (p + 1) * 128)
    query = (packed[:, p * 128 : (p + 1) * 128] + query_shift[:, at]).astype(BF)
    key = packed[:, 512 + p * 128 : 512 + (p + 1) * 128].astype(BF)
    value = (packed[:, 1024 + p * 128 : 1024 + (p + 1) * 128] + value_shift[:, at]).astype(BF)
    return query, key, value


SCALE = HEAD_DIM ** (-0.5)


def stacked(pair, first):
    zero = jnp.zeros_like(pair)
    return jnp.concatenate([jnp.where(first, pair, zero), jnp.where(first, zero, pair)])


def merged(both, first):
    half = both.shape[0] // 2
    return jnp.where(first, both[:half], both[half:])


def softmax_of(queries, key, blocked):
    scores = dot_nt(queries, key) * SCALE + blocked
    exps = jnp.exp(scores - jnp.max(scores, axis=-1, keepdims=True))
    return exps * (1.0 / jnp.sum(exps, axis=-1, keepdims=True))


def attention_kernel(packed, query_shift, value_shift, blocked, mixed):
    first = lax.broadcasted_iota(jnp.int32, (BLOCK, 128), 1) < 64
    both = jnp.concatenate([blocked[...], blocked[...]])
    for p in range(4):
        query, key, value = head_pair(packed, query_shift, value_shift, p)
        probs = softmax_of(stacked(query, first), key, both)
        parts = dot(probs.astype(BF), value)
        mixed[:, p * 128 : (p + 1) * 128] = merged(parts, first).astype(BF)


def attention(packed, query_shift, value_shift, blocked, late):
    rows = packed.shape[0]
    shift = pl.BlockSpec((1, 512), lambda i: (0, 0))
    return kernel_call(
        lambda *refs: attention_kernel(*refs[:-1]),
        "attention",
        [struct((rows, 512), BF), TOKEN],
        us=5,
        late=late,
        grid=(rows // BLOCK,),
        in_specs=[
            pl.BlockSpec((BLOCK, 1536), lambda i: (i, 0)),
            shift,
            shift,
            pl.BlockSpec((None, BLOCK, BLOCK), lambda i: (i, 0, 0)),
        ],
        out_specs=[pl.BlockSpec((BLOCK, 512), lambda i: (i, 0)), TOKEN_SPEC],
    )(packed, query_shift, value_shift, blocked)


def attention_back_kernel(packed, query_shift, value_shift, blocked, d_mixed, d_packed, total):
    first = lax.broadcasted_iota(jnp.int32, (BLOCK, 128), 1) < 64

    @pl.when(pl.program_id(0) == 0)
    def _():
        total[...] = jnp.zeros_like(total)

    both = jnp.concatenate([blocked[...], blocked[...]])
    for p in range(4):
        query, key, value = head_pair(packed, query_shift, value_shift, p)
        queries = stacked(query, first)
        grads = stacked(d_mixed[:, p * 128 : (p + 1) * 128], first)
        probs = softmax_of(queries, key, both)
        d_probs = dot_nt(grads, value)
        d_scores = probs * (d_probs - jnp.sum(probs * d_probs, axis=-1, keepdims=True))
        d_scores = d_scores.astype(BF)
        parts = (
            merged(dot(d_scores, key), first) * SCALE,
            dot_tn(d_scores, queries) * SCALE,
            dot_tn(probs.astype(BF), grads),
        )
        for k, part in enumerate(parts):
            at = slice(k * 512 + p * 128, k * 512 + (p + 1) * 128)
            low = part.astype(BF)
            d_packed[:, at] = low
            total[:, at] += jnp.sum(low.astype(F32), axis=0, keepdims=True)


def attention_back(packed, query_shift, value_shift, blocked, d_mixed, late):
    rows = packed.shape[0]
    shift = pl.BlockSpec((1, 512), lambda i: (0, 0))
    return kernel_call(
        attention_back_kernel,
        "attention_back",
        [struct((rows, 1536), BF), struct((1, 1536), F32)],
        us=16,
        late=late,
        grid=(rows // BLOCK,),
        in_specs=[
            pl.BlockSpec((BLOCK, 1536), lambda i: (i, 0)),
            shift,
            shift,
            pl.BlockSpec((None, BLOCK, BLOCK), lambda i: (i, 0, 0)),
            pl.BlockSpec((BLOCK, 512), lambda i: (i, 0)),
        ],
        out_specs=[
            pl.BlockSpec((BLOCK, 1536), lambda i: (i, 0)),
            pl.BlockSpec((1, 1536), lambda i: (0, 0)),
        ],
    )(packed, query_shift, value_shift, blocked, d_mixed)


def dot(left, right):
    return jnp.dot(left, right, preferred_element_type=F32)


def dot_nt(left, right):
    return lax.dot_general(left, right, (((1,), (1,)), ((), ())), preferred_element_type=F32)


def dot_tn(left, right):
    return lax.dot_general(left, right, (((0,), (0,)), ((), ())), preferred_element_type=F32)


def normalize(values):
    center = values - jnp.mean(values, axis=-1, keepdims=True)
    rstd = lax.rsqrt(jnp.mean(center * center, axis=-1, keepdims=True) + EPS)
    return center * rstd, rstd


def normalize_back(grad, yhat, rstd, gain):
    t = grad * gain
    return rstd * (
        t
        - jnp.mean(t, axis=-1, keepdims=True)
        - yhat * jnp.mean(t * yhat, axis=-1, keepdims=True)
    )


TILE = 160


def middle_kernel(part, other, tokens, keep, shift, gain, bias, middle, normed):
    attended = part[...].astype(F32) + other[...].astype(F32) + shift[...]
    rows = tokens[...].astype(F32) + keep[...] * attended
    middle[...] = rows
    yhat, _ = normalize(rows)
    normed[...] = (yhat * gain[...] + bias[...]).astype(BF)


def row_specs(count, width=1024):
    half = count // 2
    return (
        pl.BlockSpec((TILE, width), lambda i: (i, 0)),
        pl.BlockSpec((TILE, width), lambda i: (lax.rem(i + half, count), 0)),
        pl.BlockSpec((TILE, 1), lambda i: (i, 0)),
        pl.BlockSpec((1, width), lambda i: (0, 0)),
    )


def middle_layer(part, other, tokens, keep, shift, gain, bias):
    rows = part.shape[0]
    tile, swapped, column, vector = row_specs(rows // TILE)
    return kernel_call(
        middle_kernel,
        "middle_layer",
        [struct((rows, 1024), F32), struct((rows, 1024), BF)],
        us=6,
        pinned_out=(0,),
        grid=(rows // TILE,),
        in_specs=[tile, swapped, tile, column, vector, vector, vector],
        out_specs=[tile, tile],
    )(part, other, tokens, keep, shift, gain, bias)


def middle_back_kernel(shares, part, other, middle, cot, keep, gain, d_middle, d_attended, sums):
    step = pl.program_id(0)
    grad = part[...].astype(F32) + other[...].astype(F32)
    yhat, rstd = normalize(middle[...])
    incoming = cot[...].astype(F32) * shares[step // (pl.num_programs(0) // 2)]
    d_rows = incoming + normalize_back(grad, yhat, rstd, gain[...])
    d_middle[...] = d_rows
    low = (keep[...] * d_rows).astype(BF)
    d_attended[...] = low
    branch = (keep[...] * incoming).astype(BF)

    @pl.when(step == 0)
    def _():
        sums[...] = jnp.zeros_like(sums)

    @pl.when(step < pl.num_programs(0) // 2)
    def _():
        for k, v in enumerate((grad * yhat, grad, low.astype(F32), branch.astype(F32))):
            sums[k : k + 1, :] += jnp.sum(v, axis=0, keepdims=True)


def middle_back(shares, part, other, middle, cot, keep, gain, late):
    rows = part.shape[0]
    tile, swapped, column, vector = row_specs(rows // TILE)
    return kernel_call(
        middle_back_kernel,
        "middle_back",
        [struct((rows, 1024), F32), struct((rows, 1024), BF), struct((8, 1024), F32)],
        us=7,
        late=late,
        pinned=(3, 4),
        grid=(rows // TILE,),
        in_specs=[SMEM, tile, swapped, tile, tile, column, vector],
        out_specs=[tile, tile, pl.BlockSpec((8, 1024), lambda i: (0, 0))],
    )(shares, part, other, middle, cot, keep, gain)


def input_back_kernel(groups, shares, part, other, rows, d_middle, gain, cot, grad_rows, sums):
    grad = part[...].astype(F32) + other[...].astype(F32)
    yhat, rstd = normalize(rows[...].astype(F32))
    values = (d_middle[...] + normalize_back(grad, yhat, rstd, gain[...])).astype(BF)
    rest = (cot[...].astype(F32) * shares[0]).astype(BF)
    grad_rows[...] = spread(groups[0], values, rest)

    @pl.when(pl.program_id(0) == 0)
    def _():
        sums[...] = jnp.zeros_like(sums)

    for k, v in enumerate((grad * yhat, grad)):
        sums[k : k + 1, :] += jnp.sum(v, axis=0, keepdims=True)


def input_back(groups, shares, part, other, rows, d_middle, gain, cot, late):
    tile = pl.BlockSpec((BLOCK, 1024), lambda i: (i, 0))
    span = pl.BlockSpec((SPAN, 1024), lambda i: (i, 0))
    return kernel_call(
        input_back_kernel,
        "input_back",
        [struct(cot.shape, BF), struct((8, 1024), F32)],
        us=4,
        late=late,
        grid=(2,),
        in_specs=[
            SMEM,
            SMEM,
            tile,
            tile,
            tile,
            tile,
            pl.BlockSpec((1, 1024), lambda i: (0, 0)),
            span,
        ],
        out_specs=[span, pl.BlockSpec((8, 1024), lambda i: (0, 0))],
    )(groups, shares, part, other, rows, d_middle, gain, cot)


def body(
    tokens,
    norm1_gain,
    norm1_bias,
    qkv_weight,
    query_bias,
    value_bias,
    out_weight,
    out_bias,
    norm2_gain,
    norm2_bias,
    fc1_weight,
    fc1_bias,
    fc2_weight,
    fc2_bias,
    cotangent,
    group_of,
    keep_mask,
    group_tokens,
):
    here = Where()
    own_rows, width = tokens.shape
    c = here.c
    here.make_table()
    place_table = here.table

    vectors = (
        norm1_gain,
        norm1_bias,
        query_bias,
        value_bias,
        out_bias,
        norm2_gain,
        norm2_bias,
        fc2_bias,
        fc1_bias,
    )

    def whole(v):
        return pl.BlockSpec(v.shape, lambda i: (0,) * len(v.shape))

    shapes = [
        struct(shape, BF) for shape in ((8, 32, 1664), (64, 2048), (256, 1024), (64, 1024))
    ]
    weights = (qkv_weight, fc1_weight, fc2_weight, out_weight)
    qkv_rep, fc1_part, fc2_half, out_half = kernel_call(
        prepare_kernel,
        "prepare",
        shapes,
        us=3,
        pinned=range(1, 14),
        grid=(1,),
        in_specs=[SMEM] + [whole(v) for v in weights + vectors],
        out_specs=[whole(v) for v in shapes],
    )(place_table, *weights, *vectors)
    qkv_slab = all_to_all(qkv_rep, "fsdp")
    fc1_row = lax.all_gather(fc1_part, "fsdp", axis=0, axis_index_groups=X_GROUPS)
    out_all = lax.all_gather(out_half, "fsdp", axis=0, tiled=True)
    fc2_pair = assemble(
        here,
        "fc2_hi",
        [fc2_half, permute(fc2_half, flip_hi)],
        (2, 256, 1024),
        lambda o, t, n: o.at[t[HI] if n == 0 else 1 - t[HI]],
    )

    qkv_blocks = ring_blocks(qkv_slab, "z")
    fc1_blocks = ring_blocks(fc1_row, "y")
    fc2_blocks = ring_blocks(fc2_pair, "x")
    qkv_all = assemble(
        here,
        "qkv_z",
        qkv_blocks,
        (8, 4, 32, 1536),
        lambda o, t, n: o.at[:, source_in(t, Z, n)],
        lambda ref: ref.at[:, :, pl.ds(0, 1536)],
        late=fc2_blocks[3:],
    ).reshape(1024, 1536)
    (
        gain_one,
        shift_one,
        out_shift,
        gain_two,
        shift_two,
        fc2_shift,
        query_shift,
        value_shift,
        fc1_shift,
    ) = kernel_call(
        vectors_kernel,
        "vectors",
        [struct((1, 1024), F32)] * 6 + [struct((1, 512), F32)] * 2 + [struct((1, 2048), F32)],
        us=1,
        grid=(1,),
        in_specs=[SMEM, pl.BlockSpec((8, 16, 128), lambda i: (0, 0, 12))],
        out_specs=[pl.BlockSpec((1, n), lambda i: (0, 0)) for n in (1024,) * 6 + (512,) * 2 + (2048,)],
    )(place_table, qkv_slab)

    groups = jnp.stack([pick(group_of, here.dp), pick(group_of, here.dp + here.sign)])
    counts = group_tokens.astype(F32)
    shares = counts / jnp.sum(counts)
    shares = jnp.where(groups == 1, shares[1], shares[0])
    rows_low, cot, d_branch, mask_col, blocked = compact(
        groups,
        shares,
        tokens,
        permute(tokens, swap_core),
        cotangent,
        permute(cotangent, swap_core),
        keep_mask,
        permute(keep_mask, swap_core),
    )
    own_rows = 2 * BLOCK

    yhat_one, _ = normalize(rows_low.astype(F32))
    normed = (yhat_one * gain_one + shift_one).astype(BF)
    packed = dot(normed, qkv_all)
    mixed, attention_done = attention(packed, query_shift, value_shift, blocked, fc1_blocks[3:])
    attended = dot(mixed, out_all).astype(BF)
    middle, normed_two = middle_layer(
        attended, permute(attended, swap_core), rows_low, mask_col, out_shift, gain_two, shift_two
    )
    fc1_all = assemble(
        here,
        "fc1_y",
        fc1_blocks,
        (2, 4, 2, 64, 2048),
        lambda o, t, n: o.at[source_in(t, Y, n) // 2, :, lax.rem(source_in(t, Y, n), 2)],
        late=(attention_done,),
    ).reshape(1024, 2048)
    hidden, slope = hidden_layer(normed_two, fc1_all, fc1_shift)
    fc2_all = assemble(
        here,
        "fc2_x",
        fc2_blocks,
        (2, 4, 256, 1024),
        lambda o, t, n: o.at[:, source_in(t, X, n)],
        late=(attention_done,),
    ).reshape(2048, 1024)

    grad_fc2, fc2_done = grad_fc2_terms(hidden, d_branch, ())
    fc2_sum = lax.psum_scatter(
        grad_fc2.reshape(2048, 1024),
        "dp",
        scatter_dimension=0,
        axis_index_groups=Z_GROUPS,
        tiled=True,
    )
    d_pre, fc1_bias_sum = hidden_back(d_branch, fc2_all, slope, (fc2_done,))
    d_normed_two = dot_nt(d_pre, fc1_all).astype(BF)
    *grad_fc1, fc1_done = grad_fc1_terms(here, normed_two, d_pre, (d_normed_two,))
    grad_fc1 = list(zip(*grad_fc1))
    fc1_arrived = ring_both(grad_fc1[0])
    d_middle, d_attended, middle_sums = middle_back(
        shares,
        d_normed_two,
        permute(d_normed_two, swap_core),
        middle,
        cot,
        mask_col,
        gain_two,
        (fc1_done,),
    )
    d_mixed = dot_nt(d_attended, out_all).astype(BF)
    fc1_sum, add_done = add_both(fc1_arrived, grad_fc1[1], (middle_sums,))
    fc1_arrived = ring_both(fc1_sum)
    d_packed, packed_sums = attention_back(
        packed, query_shift, value_shift, blocked, d_mixed, (add_done,)
    )
    fc1_sum, add_done = add_both(fc1_arrived, grad_fc1[2], (packed_sums,))
    fc1_arrived = ring_both(fc1_sum)
    grad_qkv = grad_qkv_terms(normed, d_packed, mixed, d_attended, (add_done,))
    grad_qkv, d_packed, hidden = lax.optimization_barrier((grad_qkv, d_packed, hidden))
    qkv_sum = lax.psum_scatter(
        grad_qkv.reshape(1024, 2048),
        "dp",
        scatter_dimension=0,
        axis_index_groups=Z_GROUPS,
        tiled=True,
    ).reshape(8, 32, 2048)
    *fc2_blocks, split_done = fc2_split(here, fc2_sum.reshape(8, 64, 1024))
    fc2_kept, fc2_sent = fc2_sums(here, exchange(fc2_blocks, "x"))
    y_sum, x_kept, x_sent = last_both(here, fc1_arrived, grad_fc1[3], (split_done,))
    fc1_sum = fc1_slices(
        here, all_to_all(y_sum, "fsdp", X_GROUPS), x_kept, permute(x_sent, flip_hi)
    )
    fc1_sum = all_to_all(fc1_sum, "dp", SLICE_GROUPS)

    d_normed_sent = permute(dot_nt(d_packed[own_rows:], qkv_all).astype(BF), swap_core)
    d_normed_own = dot_nt(d_packed[:own_rows], qkv_all).astype(BF)
    input_grad, input_sums = input_back(
        groups,
        shares,
        d_normed_own,
        d_normed_sent,
        rows_low,
        d_middle,
        gain_one,
        cotangent,
        (),
    )

    branch_sent = permute(dot(hidden[own_rows:], fc2_all).astype(BF), swap_core)
    block_out, block_done = block_out_layer(
        groups,
        dot(hidden[:own_rows], fc2_all),
        branch_sent,
        middle,
        mask_col,
        fc2_shift,
        tokens,
    )

    vector_terms = kernel_call(
        vector_terms_kernel,
        "vector_terms",
        struct((8, 16, 128), F32),
        us=1,
        in_specs=[SMEM] + [VMEM] * 4,
        out_specs=VMEM,
    )(place_table, input_sums, packed_sums, middle_sums, fc1_bias_sum)
    qkv_sum = join(qkv_sum, vector_terms, (block_done, fc2_kept, fc1_sum))
    qkv_sum = all_to_all(qkv_sum, "fsdp")
    qkv_kept, qkv_sent, vector_sums = sum_and_halve(here, "qkv_lo", qkv_sum, 2048)
    sums = (qkv_kept, qkv_sent, fc2_kept, fc2_sent, fc1_sum, vector_sums)
    packed_slices = kernel_call(
        pack_kernel,
        "pack",
        struct((8, 48, 2176), BF),
        us=1.5,
        grid=(1,),
        in_specs=[whole(v) for v in sums],
        out_specs=whole(struct((8, 48, 2176), BF)),
    )(*sums)
    own = all_to_all(packed_slices, "dp", SLICE_GROUPS)
    half = pl.BlockSpec((None, 48, 2176), lambda i: (i, 0, 0))
    grad_qkv_weight, grad_out_weight, grad_fc1_weight, grad_fc2_weight, *vector_sums = kernel_call(
        unpack_kernel,
        "unpack",
        [
            struct((128, 3072), F32),
            struct((2, 8, 8, 1024), F32),
            struct((128, 4096), F32),
            struct((2, 8, 32, 1024), F32),
            *(struct((1, 128), F32),) * 8,
            struct((4, 128), F32),
        ],
        us=5,
        grid=(8,),
        in_specs=[SMEM, half, half],
        out_specs=[
            pl.BlockSpec((16, 3072), lambda i: (i, 0)),
            pl.BlockSpec((2, None, 8, 1024), lambda i: (0, i, 0, 0)),
            pl.BlockSpec((16, 4096), lambda i: (lax.rem(i, 2) * 4 + i // 2, 0)),
            pl.BlockSpec((2, None, 32, 1024), lambda i: (0, i, 0, 0)),
            *(pl.BlockSpec((1, 128), lambda i: (0, 0)),) * 8,
            pl.BlockSpec((4, 128), lambda i: (0, 0)),
        ],
    )(place_table, own, permute(own, swap_core))
    return (
        block_out,
        input_grad,
        vector_sums[0].reshape(128),
        vector_sums[1].reshape(128),
        grad_qkv_weight,
        vector_sums[2].reshape(128),
        vector_sums[3].reshape(128),
        grad_out_weight.reshape(128, 1024),
        vector_sums[4].reshape(128),
        vector_sums[5].reshape(128),
        vector_sums[6].reshape(128),
        grad_fc1_weight,
        vector_sums[8].reshape(512),
        grad_fc2_weight.reshape(512, 1024),
        vector_sums[7].reshape(128),
    )


def solution(mesh):
    rows, cols, both = P("fsdp", None), P("fsdp"), ("dp", "fsdp")
    in_specs = (
        P(both, None),
        cols,
        cols,
        rows,
        cols,
        cols,
        rows,
        cols,
        cols,
        cols,
        rows,
        cols,
        rows,
        cols,
        P(both, None),
        P(),
        P(both),
        P(),
    )
    out_specs = (
        P(both, None),
        P(both, None),
        cols,
        cols,
        rows,
        cols,
        cols,
        rows,
        cols,
        cols,
        cols,
        rows,
        cols,
        rows,
        cols,
    )
    return jax.shard_map(body, mesh=mesh, in_specs=in_specs, out_specs=out_specs, check_vma=False)
```

```python
import functools

import jax
import jax.numpy as jnp
from jax import lax
from jax.experimental import pallas as pl
from jax.experimental.pallas import tpu as pltpu
from jax.sharding import PartitionSpec as P

HEAD_DIM = 64
SLOT_S = 64
SPAN = 192
MOST_S = 50
USED = SPAN // SLOT_S * MOST_S
BLOCK = 160
EPS = 1e-06
AXES = ("dp", "fsdp")
BF = jnp.bfloat16
F32 = jnp.float32

Z_GROUPS = [[lo * 8 + 2 * z + c for z in range(4)] for lo in range(2) for c in range(2)]
SLICE_GROUPS = [[lo * 8 + 2 * z + c for z in range(4) for lo in range(2)] for c in range(2)]
X_GROUPS = [[0, 1, 2, 3], [4, 5, 6, 7]]


def place(linear):
    dp, fs = divmod(linear, 8)
    return fs % 4, (fs // 4) * 2 + dp // 8, (dp // 2) % 4, dp % 2


def linear_of(x, y, z, c):
    x, y, z = x % 4, y % 4, z % 4
    return (((y % 2) * 4 + z) * 2 + c) * 8 + (y // 2) * 4 + x


def permute(value, move):
    return lax.ppermute(
        value, AXES, [(l, linear_of(*move(*place(l)))) for l in range(128)]
    )


def ring_move(axis):
    def move(x, y, z, c):
        s = 1 - 2 * c
        return (x + s * (axis == "x"), y + s * (axis == "y"), z + s * (axis == "z"), c)

    return move


def shift(axis, s):
    def move(x, y, z, c):
        return (x + s * (axis == "x"), y + s * (axis == "y"), z + s * (axis == "z"), c)

    return move


HOPS = (1, 2, 3)


def swap_core(x, y, z, c):
    return x, y, z, 1 - c


def flip_hi(x, y, z, c):
    return x, 3 - y, z, c


def flip_lo(x, y, z, c):
    return x, y ^ 1, z, c


class Where:
    def __init__(self):
        dp, fs = lax.axis_index("dp"), lax.axis_index("fsdp")
        self.dp, self.fs = dp, fs
        self.c = dp % 2
        self.z = (dp // 2) % 4
        self.lo = dp // 8
        self.x = fs % 4
        self.hi = fs // 4
        self.y = self.hi * 2 + self.lo
        self.sign = 1 - 2 * self.c

    def along(self, axis):
        return {"x": self.x, "y": self.y, "z": self.z}[axis]

    def source(self, axis, step):
        return lax.rem(self.along(axis) - self.sign * step + 8, 4)

    def make_table(self):
        self.table = jnp.stack([self.c, self.z, self.lo, self.hi, self.x, self.y]).astype(jnp.int32)


C, Z, LO, HI, X, Y = range(6)


def source_in(table, at, step):
    return lax.rem(table[at] - (1 - 2 * table[C]) * step + 8, 4)


def place_in(table, at, r):
    return lax.rem(table[at] + r + 4, 4)


def pick(stacked, index, axis=0):
    return lax.dynamic_index_in_dim(stacked, index, axis, keepdims=False)


def ring_blocks(value, axis):
    blocks = [value]
    for _ in range(3):
        blocks.append(permute(blocks[-1], ring_move(axis)))
    return blocks


def exchange(blocks, axis):
    return [blocks[0]] + [permute(blocks[r], shift(axis, r)) for r in HOPS]


ANY = pl.BlockSpec(memory_space=pl.ANY)
SMEM = pl.BlockSpec(memory_space=pltpu.SMEM)
VMEM = pl.BlockSpec(memory_space=pltpu.VMEM)


TOKEN = jax.ShapeDtypeStruct((8, 128), jnp.float32)
TOKEN_SPEC = pl.BlockSpec((8, 128), lambda i: (0, 0))


def in_hbm(value):
    return pltpu.with_memory_space_constraint(value, pltpu.HBM)


def kernel_call(
    kernel,
    name,
    out_shape,
    in_specs,
    us=1,
    vmem=16 << 20,
    pinned=(),
    pinned_out=(),
    late=(),
    **kwargs,
):
    count = len(in_specs)
    if pinned_out:
        shapes = out_shape if isinstance(out_shape, list) else [out_shape]
        shapes = [
            pltpu.HBM(s.shape, s.dtype) if n in pinned_out else s for n, s in enumerate(shapes)
        ]
        out_shape = shapes if isinstance(out_shape, list) else shapes[0]

    def body(*refs):
        kernel(*refs[:count], *refs[count + len(late) :])

    call = pl.pallas_call(
        body,
        out_shape=out_shape,
        in_specs=list(in_specs) + [ANY] * len(late),
        name=name,
        compiler_params=pltpu.CompilerParams(vmem_limit_bytes=vmem),
        cost_estimate=pl.CostEstimate(
            flops=int(us * 0.25 * 1.15e9), bytes_accessed=1 << 16, transcendentals=0
        ),
        **kwargs,
    )

    def run(*args):
        return call(
            *(in_hbm(a) if n in pinned else a for n, a in enumerate(args)),
            *(in_hbm(a) if a.size > 1 << 16 else a for a in late),
        )

    return run


def struct(shape, dtype):
    return jax.ShapeDtypeStruct(shape, dtype)


def assemble(here, name, parts, shape, target, source=lambda ref: ref, late=()):
    def kernel(table, *refs):
        ins, out, sems = refs[: len(parts)], refs[len(parts)], refs[len(parts) + 1]
        copies = [
            pltpu.make_async_copy(source(ins[n]), target(out, table, n), sems.at[n])
            for n in range(len(parts))
        ]
        for copy in copies:
            copy.start()
        for copy in copies:
            copy.wait()

    return kernel_call(
        kernel,
        name,
        struct(shape, BF),
        in_specs=[SMEM] + [ANY] * len(parts),
        us=2.5,
        pinned=range(1, 1 + len(parts)),
        late=late,
        out_specs=VMEM,
        scratch_shapes=[pltpu.SemaphoreType.DMA((len(parts),))],
    )(here.table, *parts)


def lane_halves(c, left, right):
    first = lax.broadcasted_iota(jnp.int32, left.shape, 1) < 64
    low = jnp.where(first, left, pltpu.roll(right, 64, 1))
    high = jnp.where(first, pltpu.roll(left, 64, 1), right)
    return jnp.where(c == 0, low, high)


def prepare_kernel(place_ref, qkv, fc1, fc2, out, *refs):
    vectors, (qkv_rep, fc1_part, fc2_half, out_half) = refs[:9], refs[9:]
    c, z, lo = place_ref[0], place_ref[1], place_ref[2]
    rows = pl.ds(pl.multiple_of(z * 32, 32), 32)
    for g in range(12):
        left = qkv[rows, g * 256 : g * 256 + 128].astype(F32)
        right = qkv[rows, g * 256 + 128 : g * 256 + 256].astype(F32)
        half = lane_halves(c, left, right).astype(BF)
        for d in range(8):
            qkv_rep[d, :, g * 128 : (g + 1) * 128] = half
    packed = [ref[...].astype(F32).reshape(-1, 128) for ref in vectors]
    packed = jnp.concatenate(packed + [jnp.zeros((20, 128), F32)]).astype(BF)
    for d in range(8):
        qkv_rep[d, :, 1536:] = packed
    out_half[...] = out[pl.ds(pl.multiple_of(c * 64, 64), 64), :]
    rows = pl.ds(pl.multiple_of(lo * 64, 64), 64)
    for f in range(8):
        half = jnp.where(
            c == 0, fc1[rows, f * 512 : f * 512 + 256], fc1[rows, f * 512 + 256 : (f + 1) * 512]
        )
        fc1_part[:, f * 256 : (f + 1) * 256] = half
    fc2_half[...] = fc2[pl.ds(pl.multiple_of(c * 256, 256), 256), :]


def row_choice(group):
    i = lax.broadcasted_iota(jnp.int32, (BLOCK, SPAN), 0)
    j = lax.broadcasted_iota(jnp.int32, (BLOCK, SPAN), 1)
    slot = (i >= MOST_S).astype(jnp.int32) + (i >= 2 * MOST_S).astype(jnp.int32)
    source = jnp.where(group == 1, i, i + slot * (SLOT_S - MOST_S))
    return jnp.where((j == source) & (i < USED), 1.0, 0.0)


def chosen_rows(group):
    j = lax.broadcasted_iota(jnp.int32, (SPAN, 1), 0)
    slot = (j >= SLOT_S).astype(jnp.int32) + (j >= 2 * SLOT_S).astype(jnp.int32)
    place = jnp.where(group == 1, j, j - slot * SLOT_S)
    return place < jnp.where(group == 1, USED, MOST_S)


def image_of(group, shape, axis):
    i = lax.broadcasted_iota(jnp.int32, shape, axis)
    slot = (i >= MOST_S).astype(jnp.int32) + (i >= 2 * MOST_S).astype(jnp.int32)
    return jnp.where(group == 1, 0, slot)


def compact_kernel(
    groups, shares, tokens, tokens_other, cot, cot_other, keep, keep_other, rows, cots, d_branch, column, blocked
):
    step = pl.program_id(0)
    own = step < 2
    group = groups[step // 2]
    choice = row_choice(group)
    low = choice.astype(BF)
    kept = jnp.where(own, keep[...], keep_other[...]).astype(F32)
    rows[...] = dot(low, jnp.where(own, tokens[...], tokens_other[...])).astype(BF)
    chosen = dot(low, jnp.where(own, cot[...], cot_other[...]))
    cots[...] = chosen.astype(BF)
    mask = jnp.sum(choice * kept, axis=-1, keepdims=True)
    column[...] = mask
    d_branch[...] = (mask * (chosen * shares[step // 2])).astype(BF)
    across = dot_nt(jnp.broadcast_to(kept, (16, SPAN)).astype(BF), low)[:1]
    same = image_of(group, (BLOCK, BLOCK), 0) == image_of(group, (BLOCK, BLOCK), 1)
    blocked[...] = jnp.where(same & (across > 0.5), 0.0, -1e30)


def compact(groups, shares, tokens, tokens_other, cot, cot_other, keep, keep_other):
    def mine(shape, rows):
        return pl.BlockSpec(shape, lambda i: (jnp.minimum(i, 1),) + (0,) * (len(shape) - 1))

    def theirs(shape, rows):
        return pl.BlockSpec(shape, lambda i: (jnp.maximum(i - 2, 0),) + (0,) * (len(shape) - 1))

    row = (SPAN, 1024)
    flag = (None, 1, SPAN)
    tile = pl.BlockSpec((BLOCK, 1024), lambda i: (i, 0))
    return kernel_call(
        compact_kernel,
        "compact",
        [struct((4 * BLOCK, 1024), BF)] * 3
        + [struct((4 * BLOCK, 1), F32), struct((4, BLOCK, BLOCK), F32)],
        us=5,
        grid=(4,),
        in_specs=[
            SMEM,
            SMEM,
            mine(row, 2),
            theirs(row, 2),
            mine(row, 2),
            theirs(row, 2),
            mine(flag, 2),
            theirs(flag, 2),
        ],
        out_specs=[
            tile,
            tile,
            tile,
            pl.BlockSpec((BLOCK, 1), lambda i: (i, 0)),
            pl.BlockSpec((None, BLOCK, BLOCK), lambda i: (i, 0, 0)),
        ],
    )(
        groups,
        shares,
        tokens,
        tokens_other,
        cot,
        cot_other,
        keep.reshape(2, 1, SPAN),
        keep_other.reshape(2, 1, SPAN),
    )


def spread(group, values, rest):
    back = dot_tn(row_choice(group).astype(BF), values)
    return jnp.where(chosen_rows(group), back, rest.astype(F32)).astype(BF)


def block_out_kernel(groups, branch, sent, middle, column, shift, tokens, out):
    total = branch[...] + sent[...].astype(F32) + shift[...]
    values = (middle[...] + column[...] * total).astype(BF)
    out[...] = spread(groups[0], values, tokens[...])


def block_out_layer(groups, branch, sent, middle, column, shift, tokens):
    tile = pl.BlockSpec((BLOCK, 1024), lambda i: (i, 0))
    span = pl.BlockSpec((SPAN, 1024), lambda i: (i, 0))
    return kernel_call(
        lambda *refs: block_out_kernel(*refs[:-1]),
        "block_out",
        [struct(tokens.shape, BF), TOKEN],
        us=4,
        grid=(2,),
        in_specs=[
            SMEM,
            tile,
            tile,
            tile,
            pl.BlockSpec((BLOCK, 1), lambda i: (i, 0)),
            pl.BlockSpec((1, 1024), lambda i: (0, 0)),
            span,
        ],
        out_specs=[span, TOKEN_SPEC],
    )(groups, branch, sent, middle, column, shift, tokens)


def vectors_kernel(place_ref, packed, *outs):
    c = place_ref[0]
    rows = [packed[f].astype(F32) for f in range(8)]

    def row(f, k):
        return rows[f][k : k + 1, :]

    for out, k in zip(outs[:6], (0, 1, 4, 5, 6, 7)):
        for f in range(8):
            out[:, f * 128 : (f + 1) * 128] = row(f, k)
    for out, k in zip(outs[6:8], (2, 3)):
        for p in range(4):
            out[:, p * 128 : (p + 1) * 128] = lane_halves(c, row(2 * p, k), row(2 * p + 1, k))
    for f in range(8):
        for j in range(2):
            at = f * 256 + j * 128
            outs[8][:, at : at + 128] = jnp.where(c == 0, row(f, 8 + j), row(f, 10 + j))


def vector_terms_kernel(place_ref, input_sums, packed_sums, middle_sums, fc1_sums, out):
    c = place_ref[0]
    first = lax.broadcasted_iota(jnp.int32, (1, 128), 1) < 64
    zero = jnp.zeros((1, 128), F32)
    out[...] = jnp.zeros_like(out)
    whole = (
        (0, input_sums, 0),
        (1, input_sums, 1),
        (4, middle_sums, 2),
        (5, middle_sums, 0),
        (6, middle_sums, 1),
        (7, middle_sums, 3),
    )
    for f in range(8):
        for k, ref, r in whole:
            out[f, k : k + 1, :] = ref[r : r + 1, f * 128 : (f + 1) * 128]
        for j in range(4):
            at = f * 256 + (j % 2) * 128
            out[f, 8 + j : 9 + j, :] = jnp.where(c == j // 2, fc1_sums[:, at : at + 128], zero)
    for k, base in ((2, 0), (3, 1024)):
        for p in range(4):
            pair = packed_sums[:, base + p * 128 : base + (p + 1) * 128]
            turned = pltpu.roll(pair, 64, 1)
            for e in range(2):
                low = jnp.where(first, pair if e == 0 else turned, zero)
                high = jnp.where(first, zero, turned if e == 0 else pair)
                out[2 * p + e, k : k + 1, :] = jnp.where(c == 0, low, high)


def grad_fc2_kernel(left, right, out):
    terms = dot_tn(left[...], right[...]).astype(BF)
    for x in range(2):
        for z in range(4):
            at = (4 * x + z) * 64
            out[z, x] = terms[at : at + 64]


def grad_fc2_terms(hidden, d_branch, late):
    m = hidden.shape[0]
    return kernel_call(
        lambda *refs: grad_fc2_kernel(*refs[:-1]),
        "grad_fc2",
        [struct((4, 8, 64, 1024), BF), TOKEN],
        us=5,
        late=late,
        pinned_out=(0,),
        grid=(4,),
        in_specs=[
            pl.BlockSpec((m, 512), lambda i: (0, i)),
            pl.BlockSpec((m, 1024), lambda i: (0, 0)),
        ],
        out_specs=[
            pl.BlockSpec((4, 2, 64, 1024), lambda i: (0, i, 0, 0)),
            TOKEN_SPEC,
        ],
    )(hidden, d_branch)


def grad_fc1_kernel(table, left, right, *refs):
    along_y, along_x = refs[:4], refs[4:8]
    terms = dot_tn(left[...], right[...]).astype(BF)
    hi, pair = lax.rem(pl.program_id(0), 2), pl.program_id(0) // 2
    for n in range(4):
        y, x = source_in(table, Y, n + 1), source_in(table, X, n + 1)
        for e in range(2):

            @pl.when(y == hi * 2 + e)
            def _():
                for k in range(2):
                    at = (2 * k + e) * 64
                    along_y[n][k] = terms[at : at + 64, :1024]

            @pl.when(x == pair * 2 + e)
            def _():
                along_x[n][hi] = terms[e * 128 : (e + 1) * 128, 1024:]


def grad_fc1_terms(here, normed, d_pre, late):
    m = normed.shape[0]
    results = kernel_call(
        grad_fc1_kernel,
        "grad_fc1",
        [struct((4, 64, 1024), BF)] * 4 + [struct((2, 128, 1024), BF)] * 4 + [TOKEN],
        us=5,
        late=late,
        pinned_out=range(8),
        grid=(4,),
        in_specs=[
            SMEM,
            pl.BlockSpec((m, 256), lambda i: (0, lax.rem(i, 2) * 2 + i // 2)),
            pl.BlockSpec((m, 2048), lambda i: (0, 0)),
        ],
        out_specs=[pl.BlockSpec((2, 64, 1024), lambda i: (i // 2, 0, 0))] * 4
        + [pl.BlockSpec((2, 128, 1024), lambda i: (0, 0, 0))] * 4
        + [TOKEN_SPEC],
    )(here.table, normed, d_pre)
    return results[:4], results[4:8], results[8]


def grad_qkv_kernel(normed, d_packed, mixed, d_attended, out):
    qkv = dot_tn(normed[...], d_packed[...]).astype(BF)
    rest = dot_tn(mixed[...], d_attended[...])
    for f in range(2):
        parts = []
        for k in range(8):
            rows = rest[f * 64 + k * 8 : f * 64 + (k + 1) * 8]
            parts += [rows[:, :512], rows[:, 512:]]
        parts = jnp.concatenate(parts).astype(BF)
        for z in range(4):
            out[z, f, :, :1536] = qkv[f * 128 + z * 32 : f * 128 + (z + 1) * 32]
            out[z, f, :, 1536:] = parts[z * 32 : (z + 1) * 32]


def grad_qkv_terms(normed, d_packed, mixed, d_attended, late):
    m = normed.shape[0]
    return kernel_call(
        grad_qkv_kernel,
        "grad_qkv",
        struct((4, 8, 32, 2048), BF),
        us=5,
        late=late,
        pinned_out=(0,),
        grid=(4,),
        in_specs=[
            pl.BlockSpec((m, 256), lambda i: (0, i)),
            pl.BlockSpec((m, 1536), lambda i: (0, 0)),
            pl.BlockSpec((m, 128), lambda i: (0, i)),
            pl.BlockSpec((m, 1024), lambda i: (0, 0)),
        ],
        out_specs=pl.BlockSpec((4, 2, 32, 2048), lambda i: (0, i, 0, 0)),
    )(normed, d_packed, mixed, d_attended)


def total_of(refs):
    total = refs[0][...].astype(F32)
    for ref in refs[1:]:
        total = total + ref[...].astype(F32)
    return total


def fc2_split_kernel(table, blocks, *outs):
    for r, out in enumerate(outs[:4]):
        x = place_in(table, X, r)
        for hi in range(2):
            out[hi] = blocks[hi * 4 + x]


def fc2_split(here, blocks):
    return kernel_call(
        fc2_split_kernel,
        "fc2_split",
        [struct((2, 64, 1024), BF)] * 4 + [TOKEN],
        us=1,
        grid=(1,),
        in_specs=[SMEM, pl.BlockSpec((8, 64, 1024), lambda i: (0, 0, 0))],
        out_specs=[pl.BlockSpec((2, 64, 1024), lambda i: (0, 0, 0))] * 4 + [TOKEN_SPEC],
    )(here.table, blocks)


def fc2_sum_kernel(table, *refs):
    ins, (kept, sent) = refs[:4], refs[4:]
    total = total_of(ins)
    kept[...] = jnp.where(table[HI] == 0, total[0], total[1])
    sent[...] = jnp.where(table[HI] == 0, total[1], total[0]).astype(BF)


def fc2_add_kernel(table, own, arrived, kept, sent):
    total = own[...] + arrived[...].astype(F32)
    low, high = total[:32], total[32:]
    kept[...] = jnp.where(table[LO] == 0, low, high)
    sent[...] = jnp.where(table[LO] == 0, high, low).astype(BF)


def fc2_sums(here, blocks):
    block = pl.BlockSpec((2, 64, 1024), lambda i: (0, 0, 0))
    half = pl.BlockSpec((64, 1024), lambda i: (0, 0))
    part = pl.BlockSpec((32, 1024), lambda i: (0, 0))
    kept, sent = kernel_call(
        fc2_sum_kernel,
        "fc2_sum",
        [struct((64, 1024), F32), struct((64, 1024), BF)],
        us=1,
        grid=(1,),
        in_specs=[SMEM] + [block] * 4,
        out_specs=[half, half],
    )(here.table, *blocks)
    kept, sent = kernel_call(
        fc2_add_kernel,
        "fc2_add",
        [struct((32, 1024), F32), struct((32, 1024), BF)],
        us=1,
        grid=(1,),
        in_specs=[SMEM, half, half],
        out_specs=[part, part],
    )(here.table, kept, permute(sent, flip_hi))
    return kept, permute(sent, flip_lo)


def add_kernel(y, y_terms, x, x_terms, y_out, x_out, done):
    y_out[...] = total_of((y, y_terms)).astype(BF)
    x_out[...] = total_of((x, x_terms)).astype(BF)


def add_both(arrived, terms, late=()):
    y = pl.BlockSpec((2, 64, 1024), lambda i: (i, 0, 0))
    x = pl.BlockSpec((1, 128, 1024), lambda i: (i, 0, 0))
    *sums, done = kernel_call(
        add_kernel,
        "fc1_add",
        [struct((4, 64, 1024), BF), struct((2, 128, 1024), BF), TOKEN],
        us=1,
        late=late,
        grid=(2,),
        in_specs=[y, y, x, x],
        out_specs=[y, x, TOKEN_SPEC],
    )(arrived[0], terms[0], arrived[1], terms[1])
    return sums, done


def ring_both(sums):
    return [permute(v, ring_move(axis)) for v, axis in zip(sums, "yx")]


def last_kernel(table, y, y_terms, x, x_terms, y_out, kept, sent):
    y_out[...] = total_of((y, y_terms)).astype(BF)
    total = total_of((x, x_terms))
    kept[...] = jnp.where(table[HI] == 0, total[0], total[1])
    sent[...] = jnp.where(table[HI] == 0, total[1], total[0]).astype(BF)


def last_both(here, arrived, terms, late):
    y = pl.BlockSpec((4, 64, 1024), lambda i: (0, 0, 0))
    x = pl.BlockSpec((2, 128, 1024), lambda i: (0, 0, 0))
    half = pl.BlockSpec((128, 1024), lambda i: (0, 0))
    return kernel_call(
        last_kernel,
        "fc1_last",
        [struct((4, 64, 1024), BF), struct((128, 1024), F32), struct((128, 1024), BF)],
        us=1,
        late=late,
        grid=(1,),
        in_specs=[SMEM, y, y, x, x],
        out_specs=[y, half, half],
    )(here.table, arrived[0], terms[0], arrived[1], terms[1])


def slices_kernel(table, y_blocks, x_kept, x_sent, out):
    y_sum = jnp.sum(y_blocks[...].astype(F32), axis=0).astype(BF)
    x_sum = (x_kept[...] + x_sent[...].astype(F32)).astype(BF)
    for k in range(8):
        z, lo = k // 2, k % 2
        rows = y_sum[z * 16 : (z + 1) * 16]
        out[k, :, :1024] = jnp.where(table[LO] == lo, rows, jnp.zeros_like(rows))
        at = lo * 64 + z * 16
        out[k, :, 1024:] = x_sum[at : at + 16]


def fc1_slices(here, y_blocks, x_kept, x_sent):
    def whole(*shape):
        return pl.BlockSpec(shape, lambda i: (0,) * len(shape))

    return kernel_call(
        slices_kernel,
        "fc1_slices",
        struct((8, 16, 2048), BF),
        us=1,
        grid=(1,),
        in_specs=[SMEM, whole(4, 64, 1024), whole(128, 1024), whole(128, 1024)],
        out_specs=whole(8, 16, 2048),
    )(here.table, y_blocks, x_kept, x_sent)


def join_kernel(qkv, vectors, out):
    for f in range(8):
        out[f, :, :2048] = qkv[f]
        out[f, :16, 2048:] = vectors[f].astype(BF)
        out[f, 16:, 2048:] = jnp.zeros((16, 128), BF)


def join(qkv, vectors, late):
    return kernel_call(
        join_kernel,
        "join",
        struct((8, 32, 2176), BF),
        us=1,
        late=late,
        grid=(1,),
        in_specs=[
            pl.BlockSpec((8, 32, 2048), lambda i: (0, 0, 0)),
            pl.BlockSpec((8, 16, 128), lambda i: (0, 0, 0)),
        ],
        out_specs=pl.BlockSpec((8, 32, 2176), lambda i: (0, 0, 0)),
    )(qkv, vectors)


def split_kernel(table, blocks, kept, sent, vectors):
    total = jnp.sum(blocks[...].astype(F32), axis=0)
    half, n = kept.shape
    low, high = total[:half, :n], total[half:, :n]
    kept[...] = jnp.where(table[LO] == 0, low, high)
    sent[...] = jnp.where(table[LO] == 0, high, low).astype(BF)
    if total.shape[1] > n:
        vectors[...] = total[:16, n:]


def sum_and_halve(here, name, blocks, n):
    k, r, wide = blocks.shape
    half = pl.BlockSpec((r // 2, n), lambda i: (0, 0))
    kept, sent, vectors = kernel_call(
        split_kernel,
        name,
        [struct((r // 2, n), F32), struct((r // 2, n), BF), struct((16, 128), F32)],
        us=1,
        grid=(1,),
        in_specs=[SMEM, pl.BlockSpec((k, r, wide), lambda i: (0, 0, 0))],
        out_specs=[half, half, pl.BlockSpec((16, 128), lambda i: (0, 0))],
    )(here.table, blocks)
    return kept, permute(sent, flip_lo), vectors


def pack_mlp_kernel(fc2_kept, fc2_sent, fc1, packed):
    fc2 = (fc2_kept[...] + fc2_sent[...].astype(F32)).astype(BF)
    packed[:16] = jnp.sum(fc1[...].astype(F32), axis=0).astype(BF)
    packed[16:, :1024] = fc2[:16]
    packed[16:, 1024:] = fc2[16:]


def pack_kernel(qkv_kept, qkv_sent, vectors, packed):
    qkv = (qkv_kept[...] + qkv_sent[...].astype(F32)).astype(BF)
    for d in range(8):
        packed[d, :, :2048] = qkv
        packed[d, :, 2048:] = vectors[...].astype(BF)


def by_core(table, own, other):
    first = table[C] == 0
    low = jnp.where(first, own[...], other[...]).astype(F32)
    return low, jnp.where(first, other[...], own[...]).astype(F32)


def unpack_mlp_kernel(table, own, other, fc1, fc2):
    for k, halves in enumerate(by_core(table, own, other)):
        for lo in range(2):
            half = halves[lo]
            fc2[k, lo, :16] = half[16:, :1024]
            fc2[k, lo, 16:] = half[16:, 1024:]
            for f in range(8):
                at = f * 512 + k * 256
                fc1[lo, :, at : at + 256] = half[:16, f * 256 : (f + 1) * 256]


def unpack_kernel(table, own, other, qkv, out, *vectors):
    lows, highs = by_core(table, own, other)
    terms = (lows[:, :, 2048:] + highs[:, :, 2048:])[0] + (lows[:, :, 2048:] + highs[:, :, 2048:])[1]
    start = pl.program_id(0) == 0
    for k, ref in enumerate(vectors):
        rows = terms[k : k + ref.shape[0]]
        ref[...] = jnp.where(start, rows, ref[...] + rows)
    first = lax.broadcasted_iota(jnp.int32, (16, 128), 1) < 64
    for lo in range(2):
        low, high = lows[lo], highs[lo]
        for k, half in enumerate((low, high)):
            out[k, lo, :, :512] = half[:8, 1536:2048]
            out[k, lo, :, 512:] = half[8:, 1536:2048]
        rows = slice(16 * lo, 16 * (lo + 1))
        for p in range(12):
            left, right = low[:, p * 128 : (p + 1) * 128], high[:, p * 128 : (p + 1) * 128]
            at = p * 256
            qkv[rows, at : at + 128] = jnp.where(first, left, pltpu.roll(right, 64, 1))
            qkv[rows, at + 128 : at + 256] = jnp.where(first, pltpu.roll(left, 64, 1), right)


def all_to_all(value, axis, groups=None):
    return lax.all_to_all(value, axis, 0, 0, tiled=True, axis_index_groups=groups)


RATE = 0.51
ERFC = (
    0.28791757708249816,
    0.28415126012743,
    0.2790719172776486,
    0.055036978129087616,
    0.35846874221749475,
    -0.3591518512954867,
    0.09450494290776956,
)


def hidden_kernel(rows, weight, shift, hidden, slope):
    for k in range(weight.shape[1] // 256):
        at = slice(k * 256, (k + 1) * 256)
        u = jnp.dot(rows[...], weight[:, at], preferred_element_type=F32) + shift[:, at]
        bell = jnp.exp(-0.5 * u * u)
        t = 1.0 / (1.0 + (RATE * 0.5**0.5) * jnp.abs(u))
        tail = jnp.full_like(u, 0.5 * ERFC[-1])
        for coefficient in ERFC[-2::-1]:
            tail = tail * t + 0.5 * coefficient
        tail = tail * t * bell
        area = jnp.where(u >= 0, 1.0 - tail, tail)
        hidden[:, at] = (u * area).astype(BF)
        slope[:, at] = (area + u * bell * 0.3989422804014327).astype(BF)


def hidden_layer(rows, weight, shift):
    m, k = rows.shape
    n = weight.shape[1]
    cols = 512
    out = pl.BlockSpec((m, cols), lambda i: (0, i))
    return kernel_call(
        hidden_kernel,
        "hidden_layer",
        [struct((m, n), BF)] * 2,
        us=11,
        grid=(n // cols,),
        in_specs=[
            pl.BlockSpec((m, k), lambda i: (0, 0)),
            pl.BlockSpec((k, cols), lambda i: (0, i)),
            pl.BlockSpec((1, cols), lambda i: (0, i)),
        ],
        out_specs=[out, out],
    )(rows, weight, shift)


def d_pre_kernel(grad, weight, slope, d_pre, total):
    back = dot_nt(grad[...], weight[...]) * slope[...].astype(F32)
    low = back.astype(BF)
    d_pre[...] = low
    total[...] = jnp.sum(low.astype(F32), axis=0, keepdims=True)


def hidden_back(grad, weight, slope, late):
    m, k = grad.shape
    n = weight.shape[0]
    cols = 256
    out = pl.BlockSpec((m, cols), lambda i: (0, i))
    return kernel_call(
        d_pre_kernel,
        "hidden_back",
        [struct((m, n), BF), struct((1, n), F32)],
        late=late,
        us=6,
        grid=(n // cols,),
        in_specs=[
            pl.BlockSpec((m, k), lambda i: (0, 0)),
            pl.BlockSpec((cols, k), lambda i: (i, 0)),
            out,
        ],
        out_specs=[out, pl.BlockSpec((1, cols), lambda i: (0, i))],
    )(grad, weight, slope)


def head_pair(packed, query_shift, value_shift, p):
    at = slice(p * 128, (p + 1) * 128)
    query = (packed[:, p * 128 : (p + 1) * 128] + query_shift[:, at]).astype(BF)
    key = packed[:, 512 + p * 128 : 512 + (p + 1) * 128].astype(BF)
    value = (packed[:, 1024 + p * 128 : 1024 + (p + 1) * 128] + value_shift[:, at]).astype(BF)
    return query, key, value


SCALE = HEAD_DIM ** (-0.5)


def stacked(pair, first):
    zero = jnp.zeros_like(pair)
    return jnp.concatenate([jnp.where(first, pair, zero), jnp.where(first, zero, pair)])


def merged(both, first):
    half = both.shape[0] // 2
    return jnp.where(first, both[:half], both[half:])


def softmax_of(queries, key, blocked):
    scores = dot_nt(queries, key) * SCALE + blocked
    exps = jnp.exp(scores - jnp.max(scores, axis=-1, keepdims=True))
    return exps * (1.0 / jnp.sum(exps, axis=-1, keepdims=True))


def attention_kernel(packed, query_shift, value_shift, blocked, mixed):
    first = lax.broadcasted_iota(jnp.int32, (BLOCK, 128), 1) < 64
    both = jnp.concatenate([blocked[...], blocked[...]])
    for p in range(4):
        query, key, value = head_pair(packed, query_shift, value_shift, p)
        probs = softmax_of(stacked(query, first), key, both)
        parts = dot(probs.astype(BF), value)
        mixed[:, p * 128 : (p + 1) * 128] = merged(parts, first).astype(BF)


def attention(packed, query_shift, value_shift, blocked, late):
    rows = packed.shape[0]
    shift = pl.BlockSpec((1, 512), lambda i: (0, 0))
    return kernel_call(
        lambda *refs: attention_kernel(*refs[:-1]),
        "attention",
        [struct((rows, 512), BF), TOKEN],
        us=5,
        late=late,
        grid=(rows // BLOCK,),
        in_specs=[
            pl.BlockSpec((BLOCK, 1536), lambda i: (i, 0)),
            shift,
            shift,
            pl.BlockSpec((None, BLOCK, BLOCK), lambda i: (i, 0, 0)),
        ],
        out_specs=[pl.BlockSpec((BLOCK, 512), lambda i: (i, 0)), TOKEN_SPEC],
    )(packed, query_shift, value_shift, blocked)


def attention_back_kernel(packed, query_shift, value_shift, blocked, d_mixed, d_packed, total):
    first = lax.broadcasted_iota(jnp.int32, (BLOCK, 128), 1) < 64

    @pl.when(pl.program_id(0) == 0)
    def _():
        total[...] = jnp.zeros_like(total)

    both = jnp.concatenate([blocked[...], blocked[...]])
    for p in range(4):
        query, key, value = head_pair(packed, query_shift, value_shift, p)
        queries = stacked(query, first)
        grads = stacked(d_mixed[:, p * 128 : (p + 1) * 128], first)
        probs = softmax_of(queries, key, both)
        d_probs = dot_nt(grads, value)
        d_scores = probs * (d_probs - jnp.sum(probs * d_probs, axis=-1, keepdims=True))
        d_scores = d_scores.astype(BF)
        parts = (
            merged(dot(d_scores, key), first) * SCALE,
            dot_tn(d_scores, queries) * SCALE,
            dot_tn(probs.astype(BF), grads),
        )
        for k, part in enumerate(parts):
            at = slice(k * 512 + p * 128, k * 512 + (p + 1) * 128)
            low = part.astype(BF)
            d_packed[:, at] = low
            total[:, at] += jnp.sum(low.astype(F32), axis=0, keepdims=True)


def attention_back(packed, query_shift, value_shift, blocked, d_mixed, late):
    rows = packed.shape[0]
    shift = pl.BlockSpec((1, 512), lambda i: (0, 0))
    return kernel_call(
        attention_back_kernel,
        "attention_back",
        [struct((rows, 1536), BF), struct((1, 1536), F32)],
        us=16,
        late=late,
        grid=(rows // BLOCK,),
        in_specs=[
            pl.BlockSpec((BLOCK, 1536), lambda i: (i, 0)),
            shift,
            shift,
            pl.BlockSpec((None, BLOCK, BLOCK), lambda i: (i, 0, 0)),
            pl.BlockSpec((BLOCK, 512), lambda i: (i, 0)),
        ],
        out_specs=[
            pl.BlockSpec((BLOCK, 1536), lambda i: (i, 0)),
            pl.BlockSpec((1, 1536), lambda i: (0, 0)),
        ],
    )(packed, query_shift, value_shift, blocked, d_mixed)


def dot(left, right):
    return jnp.dot(left, right, preferred_element_type=F32)


def dot_nt(left, right):
    return lax.dot_general(left, right, (((1,), (1,)), ((), ())), preferred_element_type=F32)


def dot_tn(left, right):
    return lax.dot_general(left, right, (((0,), (0,)), ((), ())), preferred_element_type=F32)


def normalize(values):
    center = values - jnp.mean(values, axis=-1, keepdims=True)
    rstd = lax.rsqrt(jnp.mean(center * center, axis=-1, keepdims=True) + EPS)
    return center * rstd, rstd


def normalize_back(grad, yhat, rstd, gain):
    t = grad * gain
    return rstd * (
        t
        - jnp.mean(t, axis=-1, keepdims=True)
        - yhat * jnp.mean(t * yhat, axis=-1, keepdims=True)
    )


TILE = 160


def middle_kernel(part, other, tokens, keep, shift, gain, bias, middle, normed):
    attended = part[...].astype(F32) + other[...].astype(F32) + shift[...]
    rows = tokens[...].astype(F32) + keep[...] * attended
    middle[...] = rows
    yhat, _ = normalize(rows)
    normed[...] = (yhat * gain[...] + bias[...]).astype(BF)


def row_specs(count, width=1024):
    half = count // 2
    return (
        pl.BlockSpec((TILE, width), lambda i: (i, 0)),
        pl.BlockSpec((TILE, width), lambda i: (lax.rem(i + half, count), 0)),
        pl.BlockSpec((TILE, 1), lambda i: (i, 0)),
        pl.BlockSpec((1, width), lambda i: (0, 0)),
    )


def middle_layer(part, other, tokens, keep, shift, gain, bias):
    rows = part.shape[0]
    tile, swapped, column, vector = row_specs(rows // TILE)
    return kernel_call(
        middle_kernel,
        "middle_layer",
        [struct((rows, 1024), F32), struct((rows, 1024), BF)],
        us=6,
        pinned_out=(0,),
        grid=(rows // TILE,),
        in_specs=[tile, swapped, tile, column, vector, vector, vector],
        out_specs=[tile, tile],
    )(part, other, tokens, keep, shift, gain, bias)


def middle_back_kernel(shares, part, other, middle, cot, keep, gain, d_middle, d_attended, sums):
    step = pl.program_id(0)
    grad = part[...].astype(F32) + other[...].astype(F32)
    yhat, rstd = normalize(middle[...])
    incoming = cot[...].astype(F32) * shares[step // (pl.num_programs(0) // 2)]
    d_rows = incoming + normalize_back(grad, yhat, rstd, gain[...])
    d_middle[...] = d_rows
    low = (keep[...] * d_rows).astype(BF)
    d_attended[...] = low
    branch = (keep[...] * incoming).astype(BF)

    @pl.when(step == 0)
    def _():
        sums[...] = jnp.zeros_like(sums)

    @pl.when(step < pl.num_programs(0) // 2)
    def _():
        for k, v in enumerate((grad * yhat, grad, low.astype(F32), branch.astype(F32))):
            sums[k : k + 1, :] += jnp.sum(v, axis=0, keepdims=True)


def middle_back(shares, part, other, middle, cot, keep, gain, late):
    rows = part.shape[0]
    tile, swapped, column, vector = row_specs(rows // TILE)
    return kernel_call(
        middle_back_kernel,
        "middle_back",
        [struct((rows, 1024), F32), struct((rows, 1024), BF), struct((8, 1024), F32)],
        us=7,
        late=late,
        pinned=(3, 4),
        grid=(rows // TILE,),
        in_specs=[SMEM, tile, swapped, tile, tile, column, vector],
        out_specs=[tile, tile, pl.BlockSpec((8, 1024), lambda i: (0, 0))],
    )(shares, part, other, middle, cot, keep, gain)


def input_back_kernel(groups, shares, part, other, rows, d_middle, gain, cot, grad_rows, sums):
    grad = part[...].astype(F32) + other[...].astype(F32)
    yhat, rstd = normalize(rows[...].astype(F32))
    values = (d_middle[...] + normalize_back(grad, yhat, rstd, gain[...])).astype(BF)
    rest = (cot[...].astype(F32) * shares[0]).astype(BF)
    grad_rows[...] = spread(groups[0], values, rest)

    @pl.when(pl.program_id(0) == 0)
    def _():
        sums[...] = jnp.zeros_like(sums)

    for k, v in enumerate((grad * yhat, grad)):
        sums[k : k + 1, :] += jnp.sum(v, axis=0, keepdims=True)


def input_back(groups, shares, part, other, rows, d_middle, gain, cot, late):
    tile = pl.BlockSpec((BLOCK, 1024), lambda i: (i, 0))
    span = pl.BlockSpec((SPAN, 1024), lambda i: (i, 0))
    return kernel_call(
        input_back_kernel,
        "input_back",
        [struct(cot.shape, BF), struct((8, 1024), F32)],
        us=4,
        late=late,
        grid=(2,),
        in_specs=[
            SMEM,
            SMEM,
            tile,
            tile,
            tile,
            tile,
            pl.BlockSpec((1, 1024), lambda i: (0, 0)),
            span,
        ],
        out_specs=[span, pl.BlockSpec((8, 1024), lambda i: (0, 0))],
    )(groups, shares, part, other, rows, d_middle, gain, cot)


def body(
    tokens,
    norm1_gain,
    norm1_bias,
    qkv_weight,
    query_bias,
    value_bias,
    out_weight,
    out_bias,
    norm2_gain,
    norm2_bias,
    fc1_weight,
    fc1_bias,
    fc2_weight,
    fc2_bias,
    cotangent,
    group_of,
    keep_mask,
    group_tokens,
):
    here = Where()
    c = here.c
    here.make_table()
    place_table = here.table

    vectors = (
        norm1_gain,
        norm1_bias,
        query_bias,
        value_bias,
        out_bias,
        norm2_gain,
        norm2_bias,
        fc2_bias,
        fc1_bias,
    )

    def whole(v):
        return pl.BlockSpec(v.shape, lambda i: (0,) * len(v.shape))

    shapes = [
        struct(shape, BF) for shape in ((8, 32, 1664), (64, 2048), (256, 1024), (64, 1024))
    ]
    weights = (qkv_weight, fc1_weight, fc2_weight, out_weight)
    qkv_rep, fc1_part, fc2_half, out_half = kernel_call(
        prepare_kernel,
        "prepare",
        shapes,
        us=3,
        pinned=range(1, 14),
        grid=(1,),
        in_specs=[SMEM] + [whole(v) for v in weights + vectors],
        out_specs=[whole(v) for v in shapes],
    )(place_table, *weights, *vectors)
    qkv_slab = all_to_all(qkv_rep, "fsdp")
    fc1_row = lax.all_gather(fc1_part, "fsdp", axis=0, axis_index_groups=X_GROUPS)
    out_all = lax.all_gather(out_half, "fsdp", axis=0, tiled=True)
    fc2_pair = assemble(
        here,
        "fc2_hi",
        [fc2_half, permute(fc2_half, flip_hi)],
        (2, 256, 1024),
        lambda o, t, n: o.at[t[HI] if n == 0 else 1 - t[HI]],
    )

    qkv_blocks = ring_blocks(qkv_slab, "z")
    fc1_blocks = ring_blocks(fc1_row, "y")
    fc2_blocks = ring_blocks(fc2_pair, "x")
    qkv_all = assemble(
        here,
        "qkv_z",
        qkv_blocks,
        (8, 4, 32, 1536),
        lambda o, t, n: o.at[:, source_in(t, Z, n)],
        lambda ref: ref.at[:, :, pl.ds(0, 1536)],
        late=fc2_blocks[3:],
    ).reshape(1024, 1536)
    (
        gain_one,
        shift_one,
        out_shift,
        gain_two,
        shift_two,
        fc2_shift,
        query_shift,
        value_shift,
        fc1_shift,
    ) = kernel_call(
        vectors_kernel,
        "vectors",
        [struct((1, 1024), F32)] * 6 + [struct((1, 512), F32)] * 2 + [struct((1, 2048), F32)],
        us=1,
        grid=(1,),
        in_specs=[SMEM, pl.BlockSpec((8, 16, 128), lambda i: (0, 0, 12))],
        out_specs=[pl.BlockSpec((1, n), lambda i: (0, 0)) for n in (1024,) * 6 + (512,) * 2 + (2048,)],
    )(place_table, qkv_slab)

    groups = jnp.stack([pick(group_of, here.dp), pick(group_of, here.dp + here.sign)])
    counts = group_tokens.astype(F32)
    shares = counts / jnp.sum(counts)
    shares = jnp.where(groups == 1, shares[1], shares[0])
    rows_low, cot, d_branch, mask_col, blocked = compact(
        groups,
        shares,
        tokens,
        permute(tokens, swap_core),
        cotangent,
        permute(cotangent, swap_core),
        keep_mask,
        permute(keep_mask, swap_core),
    )
    own_rows = 2 * BLOCK

    yhat_one, _ = normalize(rows_low.astype(F32))
    normed = (yhat_one * gain_one + shift_one).astype(BF)
    packed = dot(normed, qkv_all)
    mixed, attention_done = attention(packed, query_shift, value_shift, blocked, fc1_blocks[3:])
    attended = dot(mixed, out_all).astype(BF)
    middle, normed_two = middle_layer(
        attended, permute(attended, swap_core), rows_low, mask_col, out_shift, gain_two, shift_two
    )
    fc1_all = assemble(
        here,
        "fc1_y",
        fc1_blocks,
        (2, 4, 2, 64, 2048),
        lambda o, t, n: o.at[source_in(t, Y, n) // 2, :, lax.rem(source_in(t, Y, n), 2)],
        late=(attention_done,),
    ).reshape(1024, 2048)
    hidden, slope = hidden_layer(normed_two, fc1_all, fc1_shift)
    fc2_all = assemble(
        here,
        "fc2_x",
        fc2_blocks,
        (2, 4, 256, 1024),
        lambda o, t, n: o.at[:, source_in(t, X, n)],
        late=(attention_done,),
    ).reshape(2048, 1024)

    grad_fc2, fc2_done = grad_fc2_terms(hidden, d_branch, ())
    fc2_sum = lax.psum_scatter(
        grad_fc2.reshape(2048, 1024),
        "dp",
        scatter_dimension=0,
        axis_index_groups=Z_GROUPS,
        tiled=True,
    )
    d_pre, fc1_bias_sum = hidden_back(d_branch, fc2_all, slope, (fc2_done,))
    d_normed_two = dot_nt(d_pre, fc1_all).astype(BF)
    *grad_fc1, fc1_done = grad_fc1_terms(here, normed_two, d_pre, (d_normed_two,))
    grad_fc1 = list(zip(*grad_fc1))
    fc1_arrived = ring_both(grad_fc1[0])
    d_middle, d_attended, middle_sums = middle_back(
        shares,
        d_normed_two,
        permute(d_normed_two, swap_core),
        middle,
        cot,
        mask_col,
        gain_two,
        (fc1_done,),
    )
    d_mixed = dot_nt(d_attended, out_all).astype(BF)
    fc1_sum, add_done = add_both(fc1_arrived, grad_fc1[1], (middle_sums,))
    fc1_arrived = ring_both(fc1_sum)
    d_packed, packed_sums = attention_back(
        packed, query_shift, value_shift, blocked, d_mixed, (add_done,)
    )
    fc1_sum, add_done = add_both(fc1_arrived, grad_fc1[2], (packed_sums,))
    fc1_arrived = ring_both(fc1_sum)
    grad_qkv = grad_qkv_terms(normed, d_packed, mixed, d_attended, (add_done,))
    grad_qkv, d_packed, hidden = lax.optimization_barrier((grad_qkv, d_packed, hidden))
    qkv_sum = lax.psum_scatter(
        grad_qkv.reshape(1024, 2048),
        "dp",
        scatter_dimension=0,
        axis_index_groups=Z_GROUPS,
        tiled=True,
    ).reshape(8, 32, 2048)
    *fc2_blocks, split_done = fc2_split(here, fc2_sum.reshape(8, 64, 1024))
    fc2_kept, fc2_sent = fc2_sums(here, exchange(fc2_blocks, "x"))
    y_sum, x_kept, x_sent = last_both(here, fc1_arrived, grad_fc1[3], (split_done,))
    fc1_sum = fc1_slices(
        here, all_to_all(y_sum, "fsdp", X_GROUPS), x_kept, permute(x_sent, flip_hi)
    )
    fc1_sum = all_to_all(fc1_sum, "dp", SLICE_GROUPS)

    d_normed_sent = permute(dot_nt(d_packed[own_rows:], qkv_all).astype(BF), swap_core)
    d_normed_own = dot_nt(d_packed[:own_rows], qkv_all).astype(BF)
    input_grad, input_sums = input_back(
        groups,
        shares,
        d_normed_own,
        d_normed_sent,
        rows_low,
        d_middle,
        gain_one,
        cotangent,
        (),
    )

    vector_terms = kernel_call(
        vector_terms_kernel,
        "vector_terms",
        struct((8, 16, 128), F32),
        us=1,
        in_specs=[SMEM] + [VMEM] * 4,
        out_specs=VMEM,
    )(place_table, input_sums, packed_sums, middle_sums, fc1_bias_sum)
    qkv_sum = join(qkv_sum, vector_terms, (fc2_kept, fc1_sum))
    qkv_sum, hidden = lax.optimization_barrier((qkv_sum, hidden))

    branch_sent = permute(dot(hidden[own_rows:], fc2_all).astype(BF), swap_core)
    block_out, block_done = block_out_layer(
        groups,
        dot(hidden[:own_rows], fc2_all),
        branch_sent,
        middle,
        mask_col,
        fc2_shift,
        tokens,
    )

    qkv_sum = all_to_all(qkv_sum, "fsdp")
    qkv_kept, qkv_sent, vector_sums = sum_and_halve(here, "qkv_lo", qkv_sum, 2048)
    mlp_piece = kernel_call(
        pack_mlp_kernel,
        "pack_mlp",
        struct((32, 2048), BF),
        us=1,
        late=(vector_terms,),
        grid=(1,),
        in_specs=[whole(v) for v in (fc2_kept, fc2_sent, fc1_sum)],
        out_specs=pl.BlockSpec((32, 2048), lambda i: (0, 0)),
    )(fc2_kept, fc2_sent, fc1_sum)
    mlp_own = lax.all_gather(mlp_piece, "dp", axis=0, axis_index_groups=SLICE_GROUPS)
    sums = (qkv_kept, qkv_sent, vector_sums)
    packed_slices = kernel_call(
        pack_kernel,
        "pack",
        struct((8, 16, 2176), BF),
        us=1,
        late=(block_done,),
        grid=(1,),
        in_specs=[whole(v) for v in sums],
        out_specs=whole(struct((8, 16, 2176), BF)),
    )(*sums)
    own = all_to_all(packed_slices, "dp", SLICE_GROUPS)
    own, mlp_own = lax.optimization_barrier((own, mlp_own))
    half = pl.BlockSpec((2, 16, 2176), lambda i: (i, 0, 0))
    grad_qkv_weight, grad_out_weight, *vector_sums = kernel_call(
        unpack_kernel,
        "unpack",
        [
            struct((128, 3072), F32),
            struct((2, 8, 8, 1024), F32),
            *(struct((1, 128), F32),) * 8,
            struct((4, 128), F32),
        ],
        us=3,
        grid=(4,),
        in_specs=[SMEM, half, half],
        out_specs=[
            pl.BlockSpec((32, 3072), lambda i: (i, 0)),
            pl.BlockSpec((2, 2, 8, 1024), lambda i: (0, i, 0, 0)),
            *(pl.BlockSpec((1, 128), lambda i: (0, 0)),) * 8,
            pl.BlockSpec((4, 128), lambda i: (0, 0)),
        ],
    )(place_table, own, permute(own, swap_core))
    half = pl.BlockSpec((2, 32, 2048), lambda i: (i, 0, 0))
    grad_fc1_weight, grad_fc2_weight = kernel_call(
        unpack_mlp_kernel,
        "unpack_mlp",
        [struct((2, 4, 16, 4096), F32), struct((2, 8, 32, 1024), F32)],
        us=3,
        grid=(4,),
        in_specs=[SMEM, half, half],
        out_specs=[
            pl.BlockSpec((2, None, 16, 4096), lambda i: (0, i, 0, 0)),
            pl.BlockSpec((2, 2, 32, 1024), lambda i: (0, i, 0, 0)),
        ],
    )(place_table, mlp_own, permute(mlp_own, swap_core))
    return (
        block_out,
        input_grad,
        vector_sums[0].reshape(128),
        vector_sums[1].reshape(128),
        grad_qkv_weight,
        vector_sums[2].reshape(128),
        vector_sums[3].reshape(128),
        grad_out_weight.reshape(128, 1024),
        vector_sums[4].reshape(128),
        vector_sums[5].reshape(128),
        vector_sums[6].reshape(128),
        grad_fc1_weight.reshape(128, 4096),
        vector_sums[8].reshape(512),
        grad_fc2_weight.reshape(512, 1024),
        vector_sums[7].reshape(128),
    )


def solution(mesh):
    rows, cols, both = P("fsdp", None), P("fsdp"), ("dp", "fsdp")
    in_specs = (
        P(both, None),
        cols,
        cols,
        rows,
        cols,
        cols,
        rows,
        cols,
        cols,
        cols,
        rows,
        cols,
        rows,
        cols,
        P(both, None),
        P(),
        P(both),
        P(),
    )
    out_specs = (
        P(both, None),
        P(both, None),
        cols,
        cols,
        rows,
        cols,
        cols,
        rows,
        cols,
        cols,
        cols,
        rows,
        cols,
        rows,
        cols,
    )
    return jax.shard_map(body, mesh=mesh, in_specs=in_specs, out_specs=out_specs, check_vma=False)
```

```python
import functools

import jax
import jax.numpy as jnp
from jax import lax
from jax.experimental import pallas as pl
from jax.experimental.pallas import tpu as pltpu
from jax.sharding import PartitionSpec as P

HEAD_DIM = 64
SLOT_S = 64
SPAN = 192
MOST_S = 50
USED = SPAN // SLOT_S * MOST_S
BLOCK = 160
EPS = 1e-06
AXES = ("dp", "fsdp")
BF = jnp.bfloat16
F32 = jnp.float32

Z_GROUPS = [[lo * 8 + 2 * z + c for z in range(4)] for lo in range(2) for c in range(2)]
SLICE_GROUPS = [[lo * 8 + 2 * z + c for z in range(4) for lo in range(2)] for c in range(2)]
X_GROUPS = [[0, 1, 2, 3], [4, 5, 6, 7]]


def place(linear):
    dp, fs = divmod(linear, 8)
    return fs % 4, (fs // 4) * 2 + dp // 8, (dp // 2) % 4, dp % 2


def linear_of(x, y, z, c):
    x, y, z = x % 4, y % 4, z % 4
    return (((y % 2) * 4 + z) * 2 + c) * 8 + (y // 2) * 4 + x


def permute(value, move):
    return lax.ppermute(
        value, AXES, [(l, linear_of(*move(*place(l)))) for l in range(128)]
    )


def ring_move(axis):
    def move(x, y, z, c):
        s = 1 - 2 * c
        return (x + s * (axis == "x"), y + s * (axis == "y"), z + s * (axis == "z"), c)

    return move


def shift(axis, s):
    def move(x, y, z, c):
        return (x + s * (axis == "x"), y + s * (axis == "y"), z + s * (axis == "z"), c)

    return move


HOPS = (1, 2, 3)


def swap_core(x, y, z, c):
    return x, y, z, 1 - c


def flip_hi(x, y, z, c):
    return x, 3 - y, z, c


def flip_lo(x, y, z, c):
    return x, y ^ 1, z, c


class Where:
    def __init__(self):
        dp, fs = lax.axis_index("dp"), lax.axis_index("fsdp")
        self.dp, self.fs = dp, fs
        self.c = dp % 2
        self.z = (dp // 2) % 4
        self.lo = dp // 8
        self.x = fs % 4
        self.hi = fs // 4
        self.y = self.hi * 2 + self.lo
        self.sign = 1 - 2 * self.c

    def along(self, axis):
        return {"x": self.x, "y": self.y, "z": self.z}[axis]

    def source(self, axis, step):
        return lax.rem(self.along(axis) - self.sign * step + 8, 4)

    def make_table(self):
        self.table = jnp.stack([self.c, self.z, self.lo, self.hi, self.x, self.y]).astype(jnp.int32)


C, Z, LO, HI, X, Y = range(6)


def source_in(table, at, step):
    return lax.rem(table[at] - (1 - 2 * table[C]) * step + 8, 4)


def place_in(table, at, r):
    return lax.rem(table[at] + r + 4, 4)


def pick(stacked, index, axis=0):
    return lax.dynamic_index_in_dim(stacked, index, axis, keepdims=False)


def ring_blocks(value, axis):
    blocks = [value]
    for _ in range(3):
        blocks.append(permute(blocks[-1], ring_move(axis)))
    return blocks


def exchange(blocks, axis):
    return [blocks[0]] + [permute(blocks[r], shift(axis, r)) for r in HOPS]


ANY = pl.BlockSpec(memory_space=pl.ANY)
SMEM = pl.BlockSpec(memory_space=pltpu.SMEM)
VMEM = pl.BlockSpec(memory_space=pltpu.VMEM)


TOKEN = jax.ShapeDtypeStruct((8, 128), jnp.float32)
TOKEN_SPEC = pl.BlockSpec((8, 128), lambda i: (0, 0))


def in_hbm(value):
    return pltpu.with_memory_space_constraint(value, pltpu.HBM)


def kernel_call(
    kernel,
    name,
    out_shape,
    in_specs,
    us=1,
    vmem=16 << 20,
    pinned=(),
    pinned_out=(),
    late=(),
    **kwargs,
):
    count = len(in_specs)
    if pinned_out:
        shapes = out_shape if isinstance(out_shape, list) else [out_shape]
        shapes = [
            pltpu.HBM(s.shape, s.dtype) if n in pinned_out else s for n, s in enumerate(shapes)
        ]
        out_shape = shapes if isinstance(out_shape, list) else shapes[0]

    def body(*refs):
        kernel(*refs[:count], *refs[count + len(late) :])

    call = pl.pallas_call(
        body,
        out_shape=out_shape,
        in_specs=list(in_specs) + [ANY] * len(late),
        name=name,
        compiler_params=pltpu.CompilerParams(vmem_limit_bytes=vmem),
        cost_estimate=pl.CostEstimate(
            flops=int(us * 0.25 * 1.15e9), bytes_accessed=1 << 16, transcendentals=0
        ),
        **kwargs,
    )

    def run(*args):
        return call(
            *(in_hbm(a) if n in pinned else a for n, a in enumerate(args)),
            *(in_hbm(a) if a.size > 1 << 16 else a for a in late),
        )

    return run


def struct(shape, dtype):
    return jax.ShapeDtypeStruct(shape, dtype)


def assemble(here, name, parts, shape, target, source=lambda ref: ref, late=()):
    def kernel(table, *refs):
        ins, out, sems = refs[: len(parts)], refs[len(parts)], refs[len(parts) + 1]
        copies = [
            pltpu.make_async_copy(source(ins[n]), target(out, table, n), sems.at[n])
            for n in range(len(parts))
        ]
        for copy in copies:
            copy.start()
        for copy in copies:
            copy.wait()

    return kernel_call(
        kernel,
        name,
        struct(shape, BF),
        in_specs=[SMEM] + [ANY] * len(parts),
        us=2.5,
        pinned=range(1, 1 + len(parts)),
        late=late,
        out_specs=VMEM,
        scratch_shapes=[pltpu.SemaphoreType.DMA((len(parts),))],
    )(here.table, *parts)


def lane_halves(c, left, right):
    first = lax.broadcasted_iota(jnp.int32, left.shape, 1) < 64
    low = jnp.where(first, left, pltpu.roll(right, 64, 1))
    high = jnp.where(first, pltpu.roll(left, 64, 1), right)
    return jnp.where(c == 0, low, high)


def prepare_kernel(place_ref, qkv, fc1, fc2, out, *refs):
    vectors, (qkv_rep, fc1_part, fc2_half, out_half) = refs[:9], refs[9:]
    c, z, lo = place_ref[0], place_ref[1], place_ref[2]
    rows = pl.ds(pl.multiple_of(z * 32, 32), 32)
    for g in range(12):
        left = qkv[rows, g * 256 : g * 256 + 128].astype(F32)
        right = qkv[rows, g * 256 + 128 : g * 256 + 256].astype(F32)
        half = lane_halves(c, left, right).astype(BF)
        for d in range(8):
            qkv_rep[d, :, g * 128 : (g + 1) * 128] = half
    packed = [ref[...].astype(F32).reshape(-1, 128) for ref in vectors]
    packed = jnp.concatenate(packed + [jnp.zeros((20, 128), F32)]).astype(BF)
    for d in range(8):
        qkv_rep[d, :, 1536:] = packed
    out_half[...] = out[pl.ds(pl.multiple_of(c * 64, 64), 64), :]
    rows = pl.ds(pl.multiple_of(lo * 64, 64), 64)
    for f in range(8):
        half = jnp.where(
            c == 0, fc1[rows, f * 512 : f * 512 + 256], fc1[rows, f * 512 + 256 : (f + 1) * 512]
        )
        fc1_part[:, f * 256 : (f + 1) * 256] = half
    fc2_half[...] = fc2[pl.ds(pl.multiple_of(c * 256, 256), 256), :]


def row_choice(group):
    i = lax.broadcasted_iota(jnp.int32, (BLOCK, SPAN), 0)
    j = lax.broadcasted_iota(jnp.int32, (BLOCK, SPAN), 1)
    slot = (i >= MOST_S).astype(jnp.int32) + (i >= 2 * MOST_S).astype(jnp.int32)
    source = jnp.where(group == 1, i, i + slot * (SLOT_S - MOST_S))
    return jnp.where((j == source) & (i < USED), 1.0, 0.0)


def chosen_rows(group):
    j = lax.broadcasted_iota(jnp.int32, (SPAN, 1), 0)
    slot = (j >= SLOT_S).astype(jnp.int32) + (j >= 2 * SLOT_S).astype(jnp.int32)
    place = jnp.where(group == 1, j, j - slot * SLOT_S)
    return place < jnp.where(group == 1, USED, MOST_S)


def image_of(group, shape, axis):
    i = lax.broadcasted_iota(jnp.int32, shape, axis)
    slot = (i >= MOST_S).astype(jnp.int32) + (i >= 2 * MOST_S).astype(jnp.int32)
    return jnp.where(group == 1, 0, slot)


def compact_kernel(
    groups, shares, tokens, tokens_other, cot, cot_other, keep, keep_other, rows, cots, d_branch, column, blocked
):
    step = pl.program_id(0)
    own = step < 2
    group = groups[step // 2]
    choice = row_choice(group)
    low = choice.astype(BF)
    kept = jnp.where(own, keep[...], keep_other[...]).astype(F32)
    rows[...] = dot(low, jnp.where(own, tokens[...], tokens_other[...])).astype(BF)
    chosen = dot(low, jnp.where(own, cot[...], cot_other[...]))
    cots[...] = chosen.astype(BF)
    mask = jnp.sum(choice * kept, axis=-1, keepdims=True)
    column[...] = mask
    d_branch[...] = (mask * (chosen * shares[step // 2])).astype(BF)
    across = dot_nt(jnp.broadcast_to(kept, (16, SPAN)).astype(BF), low)[:1]
    same = image_of(group, (BLOCK, BLOCK), 0) == image_of(group, (BLOCK, BLOCK), 1)
    blocked[...] = jnp.where(same & (across > 0.5), 0.0, -1e30)


def compact(groups, shares, tokens, tokens_other, cot, cot_other, keep, keep_other):
    def mine(shape, rows):
        return pl.BlockSpec(shape, lambda i: (jnp.minimum(i, 1),) + (0,) * (len(shape) - 1))

    def theirs(shape, rows):
        return pl.BlockSpec(shape, lambda i: (jnp.maximum(i - 2, 0),) + (0,) * (len(shape) - 1))

    row = (SPAN, 1024)
    flag = (None, 1, SPAN)
    tile = pl.BlockSpec((BLOCK, 1024), lambda i: (i, 0))
    return kernel_call(
        compact_kernel,
        "compact",
        [struct((4 * BLOCK, 1024), BF)] * 3
        + [struct((4 * BLOCK, 1), F32), struct((4, BLOCK, BLOCK), F32)],
        us=5,
        grid=(4,),
        in_specs=[
            SMEM,
            SMEM,
            mine(row, 2),
            theirs(row, 2),
            mine(row, 2),
            theirs(row, 2),
            mine(flag, 2),
            theirs(flag, 2),
        ],
        out_specs=[
            tile,
            tile,
            tile,
            pl.BlockSpec((BLOCK, 1), lambda i: (i, 0)),
            pl.BlockSpec((None, BLOCK, BLOCK), lambda i: (i, 0, 0)),
        ],
    )(
        groups,
        shares,
        tokens,
        tokens_other,
        cot,
        cot_other,
        keep.reshape(2, 1, SPAN),
        keep_other.reshape(2, 1, SPAN),
    )


def spread(group, values, rest):
    back = dot_tn(row_choice(group).astype(BF), values)
    return jnp.where(chosen_rows(group), back, rest.astype(F32)).astype(BF)


def block_out_kernel(groups, branch, sent, middle, column, shift, tokens, out):
    total = branch[...] + sent[...].astype(F32) + shift[...]
    values = (middle[...] + column[...] * total).astype(BF)
    out[...] = spread(groups[0], values, tokens[...])


def block_out_layer(groups, branch, sent, middle, column, shift, tokens):
    tile = pl.BlockSpec((BLOCK, 1024), lambda i: (i, 0))
    span = pl.BlockSpec((SPAN, 1024), lambda i: (i, 0))
    return kernel_call(
        lambda *refs: block_out_kernel(*refs[:-1]),
        "block_out",
        [struct(tokens.shape, BF), TOKEN],
        us=4,
        grid=(2,),
        in_specs=[
            SMEM,
            tile,
            tile,
            tile,
            pl.BlockSpec((BLOCK, 1), lambda i: (i, 0)),
            pl.BlockSpec((1, 1024), lambda i: (0, 0)),
            span,
        ],
        out_specs=[span, TOKEN_SPEC],
    )(groups, branch, sent, middle, column, shift, tokens)


def vectors_kernel(place_ref, packed, *outs):
    c = place_ref[0]
    rows = [packed[f].astype(F32) for f in range(8)]

    def row(f, k):
        return rows[f][k : k + 1, :]

    for out, k in zip(outs[:6], (0, 1, 4, 5, 6, 7)):
        for f in range(8):
            out[:, f * 128 : (f + 1) * 128] = row(f, k)
    for out, k in zip(outs[6:8], (2, 3)):
        for p in range(4):
            out[:, p * 128 : (p + 1) * 128] = lane_halves(c, row(2 * p, k), row(2 * p + 1, k))
    for f in range(8):
        for j in range(2):
            at = f * 256 + j * 128
            outs[8][:, at : at + 128] = jnp.where(c == 0, row(f, 8 + j), row(f, 10 + j))


def vector_terms_kernel(place_ref, input_sums, packed_sums, middle_sums, fc1_sums, out):
    c = place_ref[0]
    first = lax.broadcasted_iota(jnp.int32, (1, 128), 1) < 64
    zero = jnp.zeros((1, 128), F32)
    out[...] = jnp.zeros_like(out)
    whole = (
        (0, input_sums, 0),
        (1, input_sums, 1),
        (4, middle_sums, 2),
        (5, middle_sums, 0),
        (6, middle_sums, 1),
        (7, middle_sums, 3),
    )
    for f in range(8):
        for k, ref, r in whole:
            out[f, k : k + 1, :] = ref[r : r + 1, f * 128 : (f + 1) * 128]
        for j in range(4):
            at = f * 256 + (j % 2) * 128
            out[f, 8 + j : 9 + j, :] = jnp.where(c == j // 2, fc1_sums[:, at : at + 128], zero)
    for k, base in ((2, 0), (3, 1024)):
        for p in range(4):
            pair = packed_sums[:, base + p * 128 : base + (p + 1) * 128]
            turned = pltpu.roll(pair, 64, 1)
            for e in range(2):
                low = jnp.where(first, pair if e == 0 else turned, zero)
                high = jnp.where(first, zero, turned if e == 0 else pair)
                out[2 * p + e, k : k + 1, :] = jnp.where(c == 0, low, high)


def grad_fc2_kernel(left, right, out):
    terms = dot_tn(left[...], right[...]).astype(BF)
    for x in range(2):
        for z in range(4):
            at = (4 * x + z) * 64
            out[z, x] = terms[at : at + 64]


def grad_fc2_terms(hidden, d_branch, late):
    m = hidden.shape[0]
    return kernel_call(
        lambda *refs: grad_fc2_kernel(*refs[:-1]),
        "grad_fc2",
        [struct((4, 8, 64, 1024), BF), TOKEN],
        us=5,
        late=late,
        pinned_out=(0,),
        grid=(4,),
        in_specs=[
            pl.BlockSpec((m, 512), lambda i: (0, i)),
            pl.BlockSpec((m, 1024), lambda i: (0, 0)),
        ],
        out_specs=[
            pl.BlockSpec((4, 2, 64, 1024), lambda i: (0, i, 0, 0)),
            TOKEN_SPEC,
        ],
    )(hidden, d_branch)


def grad_fc1_kernel(table, left, right, *refs):
    along_y, along_x = refs[:4], refs[4:8]
    terms = dot_tn(left[...], right[...]).astype(BF)
    hi, pair = lax.rem(pl.program_id(0), 2), pl.program_id(0) // 2
    for n in range(4):
        y, x = source_in(table, Y, n + 1), source_in(table, X, n + 1)
        for e in range(2):

            @pl.when(y == hi * 2 + e)
            def _():
                for k in range(2):
                    at = (2 * k + e) * 64
                    along_y[n][k] = terms[at : at + 64, :1024]

            @pl.when(x == pair * 2 + e)
            def _():
                along_x[n][hi] = terms[e * 128 : (e + 1) * 128, 1024:]


def grad_fc1_terms(here, normed, d_pre, late):
    m = normed.shape[0]
    results = kernel_call(
        grad_fc1_kernel,
        "grad_fc1",
        [struct((4, 64, 1024), BF)] * 4 + [struct((2, 128, 1024), BF)] * 4 + [TOKEN],
        us=5,
        late=late,
        pinned_out=range(8),
        grid=(4,),
        in_specs=[
            SMEM,
            pl.BlockSpec((m, 256), lambda i: (0, lax.rem(i, 2) * 2 + i // 2)),
            pl.BlockSpec((m, 2048), lambda i: (0, 0)),
        ],
        out_specs=[pl.BlockSpec((2, 64, 1024), lambda i: (i // 2, 0, 0))] * 4
        + [pl.BlockSpec((2, 128, 1024), lambda i: (0, 0, 0))] * 4
        + [TOKEN_SPEC],
    )(here.table, normed, d_pre)
    return results[:4], results[4:8], results[8]


def grad_qkv_kernel(normed, d_packed, mixed, d_attended, out):
    qkv = dot_tn(normed[...], d_packed[...]).astype(BF)
    rest = dot_tn(mixed[...], d_attended[...])
    for f in range(2):
        parts = []
        for k in range(8):
            rows = rest[f * 64 + k * 8 : f * 64 + (k + 1) * 8]
            parts += [rows[:, :512], rows[:, 512:]]
        parts = jnp.concatenate(parts).astype(BF)
        for z in range(4):
            out[z, f, :, :1536] = qkv[f * 128 + z * 32 : f * 128 + (z + 1) * 32]
            out[z, f, :, 1536:] = parts[z * 32 : (z + 1) * 32]


def grad_qkv_terms(normed, d_packed, mixed, d_attended, late):
    m = normed.shape[0]
    return kernel_call(
        grad_qkv_kernel,
        "grad_qkv",
        struct((4, 8, 32, 2048), BF),
        us=5,
        late=late,
        pinned_out=(0,),
        grid=(4,),
        in_specs=[
            pl.BlockSpec((m, 256), lambda i: (0, i)),
            pl.BlockSpec((m, 1536), lambda i: (0, 0)),
            pl.BlockSpec((m, 128), lambda i: (0, i)),
            pl.BlockSpec((m, 1024), lambda i: (0, 0)),
        ],
        out_specs=pl.BlockSpec((4, 2, 32, 2048), lambda i: (0, i, 0, 0)),
    )(normed, d_packed, mixed, d_attended)


def total_of(refs):
    total = refs[0][...].astype(F32)
    for ref in refs[1:]:
        total = total + ref[...].astype(F32)
    return total


def fc2_split_kernel(table, blocks, *outs):
    for r, out in enumerate(outs[:4]):
        x = place_in(table, X, r)
        for hi in range(2):
            out[hi] = blocks[hi * 4 + x]


def fc2_split(here, blocks):
    return kernel_call(
        fc2_split_kernel,
        "fc2_split",
        [struct((2, 64, 1024), BF)] * 4 + [TOKEN],
        us=1,
        grid=(1,),
        in_specs=[SMEM, pl.BlockSpec((8, 64, 1024), lambda i: (0, 0, 0))],
        out_specs=[pl.BlockSpec((2, 64, 1024), lambda i: (0, 0, 0))] * 4 + [TOKEN_SPEC],
    )(here.table, blocks)


def fc2_sum_kernel(table, *refs):
    ins, (kept, sent) = refs[:4], refs[4:]
    total = total_of(ins)
    kept[...] = jnp.where(table[HI] == 0, total[0], total[1])
    sent[...] = jnp.where(table[HI] == 0, total[1], total[0]).astype(BF)


def fc2_add_kernel(table, own, arrived, kept, sent):
    total = own[...] + arrived[...].astype(F32)
    low, high = total[:32], total[32:]
    kept[...] = jnp.where(table[LO] == 0, low, high)
    sent[...] = jnp.where(table[LO] == 0, high, low).astype(BF)


def fc2_sums(here, blocks):
    block = pl.BlockSpec((2, 64, 1024), lambda i: (0, 0, 0))
    half = pl.BlockSpec((64, 1024), lambda i: (0, 0))
    part = pl.BlockSpec((32, 1024), lambda i: (0, 0))
    kept, sent = kernel_call(
        fc2_sum_kernel,
        "fc2_sum",
        [struct((64, 1024), F32), struct((64, 1024), BF)],
        us=1,
        grid=(1,),
        in_specs=[SMEM] + [block] * 4,
        out_specs=[half, half],
    )(here.table, *blocks)
    kept, sent = kernel_call(
        fc2_add_kernel,
        "fc2_add",
        [struct((32, 1024), F32), struct((32, 1024), BF)],
        us=1,
        grid=(1,),
        in_specs=[SMEM, half, half],
        out_specs=[part, part],
    )(here.table, kept, permute(sent, flip_hi))
    return kept, permute(sent, flip_lo)


def add_kernel(y, y_terms, x, x_terms, y_out, x_out, done):
    y_out[...] = total_of((y, y_terms)).astype(BF)
    x_out[...] = total_of((x, x_terms)).astype(BF)


def add_both(arrived, terms, late=()):
    y = pl.BlockSpec((2, 64, 1024), lambda i: (i, 0, 0))
    x = pl.BlockSpec((1, 128, 1024), lambda i: (i, 0, 0))
    *sums, done = kernel_call(
        add_kernel,
        "fc1_add",
        [struct((4, 64, 1024), BF), struct((2, 128, 1024), BF), TOKEN],
        us=1,
        late=late,
        grid=(2,),
        in_specs=[y, y, x, x],
        out_specs=[y, x, TOKEN_SPEC],
    )(arrived[0], terms[0], arrived[1], terms[1])
    return sums, done


def ring_both(sums):
    return [permute(v, ring_move(axis)) for v, axis in zip(sums, "yx")]


def last_kernel(table, y, y_terms, x, x_terms, y_out, kept, sent):
    y_out[...] = total_of((y, y_terms)).astype(BF)
    total = total_of((x, x_terms))
    kept[...] = jnp.where(table[HI] == 0, total[0], total[1])
    sent[...] = jnp.where(table[HI] == 0, total[1], total[0]).astype(BF)


def last_both(here, arrived, terms, late):
    y = pl.BlockSpec((4, 64, 1024), lambda i: (0, 0, 0))
    x = pl.BlockSpec((2, 128, 1024), lambda i: (0, 0, 0))
    half = pl.BlockSpec((128, 1024), lambda i: (0, 0))
    return kernel_call(
        last_kernel,
        "fc1_last",
        [struct((4, 64, 1024), BF), struct((128, 1024), F32), struct((128, 1024), BF)],
        us=1,
        late=late,
        grid=(1,),
        in_specs=[SMEM, y, y, x, x],
        out_specs=[y, half, half],
    )(here.table, arrived[0], terms[0], arrived[1], terms[1])


def slices_kernel(table, y_blocks, x_kept, x_sent, out):
    y_sum = jnp.sum(y_blocks[...].astype(F32), axis=0).astype(BF)
    x_sum = (x_kept[...] + x_sent[...].astype(F32)).astype(BF)
    for k in range(8):
        z, lo = k // 2, k % 2
        rows = y_sum[z * 16 : (z + 1) * 16]
        out[k, :, :1024] = jnp.where(table[LO] == lo, rows, jnp.zeros_like(rows))
        at = lo * 64 + z * 16
        out[k, :, 1024:] = x_sum[at : at + 16]


def fc1_slices(here, y_blocks, x_kept, x_sent):
    def whole(*shape):
        return pl.BlockSpec(shape, lambda i: (0,) * len(shape))

    return kernel_call(
        slices_kernel,
        "fc1_slices",
        struct((8, 16, 2048), BF),
        us=1,
        grid=(1,),
        in_specs=[SMEM, whole(4, 64, 1024), whole(128, 1024), whole(128, 1024)],
        out_specs=whole(8, 16, 2048),
    )(here.table, y_blocks, x_kept, x_sent)


def join_kernel(qkv, vectors, out):
    for f in range(8):
        out[f, :, :2048] = qkv[f]
        out[f, :16, 2048:] = vectors[f].astype(BF)
        out[f, 16:, 2048:] = jnp.zeros((16, 128), BF)


def join(qkv, vectors, late):
    return kernel_call(
        join_kernel,
        "join",
        struct((8, 32, 2176), BF),
        us=1,
        late=late,
        grid=(1,),
        in_specs=[
            pl.BlockSpec((8, 32, 2048), lambda i: (0, 0, 0)),
            pl.BlockSpec((8, 16, 128), lambda i: (0, 0, 0)),
        ],
        out_specs=pl.BlockSpec((8, 32, 2176), lambda i: (0, 0, 0)),
    )(qkv, vectors)


def split_kernel(table, blocks, kept, sent, vectors):
    total = jnp.sum(blocks[...].astype(F32), axis=0)
    half, n = kept.shape
    low, high = total[:half, :n], total[half:, :n]
    kept[...] = jnp.where(table[LO] == 0, low, high)
    sent[...] = jnp.where(table[LO] == 0, high, low).astype(BF)
    if total.shape[1] > n:
        vectors[...] = total[:16, n:]


def sum_and_halve(here, name, blocks, n):
    k, r, wide = blocks.shape
    half = pl.BlockSpec((r // 2, n), lambda i: (0, 0))
    kept, sent, vectors = kernel_call(
        split_kernel,
        name,
        [struct((r // 2, n), F32), struct((r // 2, n), BF), struct((16, 128), F32)],
        us=1,
        grid=(1,),
        in_specs=[SMEM, pl.BlockSpec((k, r, wide), lambda i: (0, 0, 0))],
        out_specs=[half, half, pl.BlockSpec((16, 128), lambda i: (0, 0))],
    )(here.table, blocks)
    return kept, permute(sent, flip_lo), vectors


def pack_mlp_kernel(fc2_kept, fc2_sent, fc1, packed):
    fc2 = (fc2_kept[...] + fc2_sent[...].astype(F32)).astype(BF)
    packed[:16] = jnp.sum(fc1[...].astype(F32), axis=0).astype(BF)
    packed[16:, :1024] = fc2[:16]
    packed[16:, 1024:] = fc2[16:]


def pack_kernel(qkv_kept, qkv_sent, vectors, packed):
    qkv = (qkv_kept[...] + qkv_sent[...].astype(F32)).astype(BF)
    for d in range(8):
        packed[d, :, :2048] = qkv
        packed[d, :, 2048:] = vectors[...].astype(BF)


def by_core(table, own, other):
    first = table[C] == 0
    low = jnp.where(first, own[...], other[...]).astype(F32)
    return low, jnp.where(first, other[...], own[...]).astype(F32)


def unpack_mlp_kernel(table, own, other, fc1, fc2):
    for k, half in enumerate(by_core(table, own, other)):
        fc2[k, :16] = half[16:, :1024]
        fc2[k, 16:] = half[16:, 1024:]
        for f in range(8):
            at = f * 512 + k * 256
            fc1[:, at : at + 256] = half[:16, f * 256 : (f + 1) * 256]


def unpack_kernel(table, own, other, qkv, out, *vectors):
    low, high = by_core(table, own, other)
    for k, half in enumerate((low, high)):
        out[k, :, :512] = half[:8, 1536:2048]
        out[k, :, 512:] = half[8:, 1536:2048]
    terms = low[:, 2048:] + high[:, 2048:]
    start = pl.program_id(0) == 0
    for k, ref in enumerate(vectors):
        rows = terms[k : k + ref.shape[0]]
        ref[...] = jnp.where(start, rows, ref[...] + rows)
    first = lax.broadcasted_iota(jnp.int32, (16, 128), 1) < 64
    for p in range(12):
        left, right = low[:, p * 128 : (p + 1) * 128], high[:, p * 128 : (p + 1) * 128]
        qkv[:, p * 256 : p * 256 + 128] = jnp.where(first, left, pltpu.roll(right, 64, 1))
        qkv[:, p * 256 + 128 : (p + 1) * 256] = jnp.where(first, pltpu.roll(left, 64, 1), right)


def all_to_all(value, axis, groups=None):
    return lax.all_to_all(value, axis, 0, 0, tiled=True, axis_index_groups=groups)


RATE = 0.51
ERFC = (
    0.28791757708249816,
    0.28415126012743,
    0.2790719172776486,
    0.055036978129087616,
    0.35846874221749475,
    -0.3591518512954867,
    0.09450494290776956,
)


def hidden_kernel(rows, weight, shift, hidden, slope):
    for k in range(weight.shape[1] // 256):
        at = slice(k * 256, (k + 1) * 256)
        u = jnp.dot(rows[...], weight[:, at], preferred_element_type=F32) + shift[:, at]
        bell = jnp.exp(-0.5 * u * u)
        t = 1.0 / (1.0 + (RATE * 0.5**0.5) * jnp.abs(u))
        tail = jnp.full_like(u, 0.5 * ERFC[-1])
        for coefficient in ERFC[-2::-1]:
            tail = tail * t + 0.5 * coefficient
        tail = tail * t * bell
        area = jnp.where(u >= 0, 1.0 - tail, tail)
        hidden[:, at] = (u * area).astype(BF)
        slope[:, at] = (area + u * bell * 0.3989422804014327).astype(BF)


def hidden_layer(rows, weight, shift):
    m, k = rows.shape
    n = weight.shape[1]
    cols = 512
    out = pl.BlockSpec((m, cols), lambda i: (0, i))
    return kernel_call(
        hidden_kernel,
        "hidden_layer",
        [struct((m, n), BF)] * 2,
        us=11,
        grid=(n // cols,),
        in_specs=[
            pl.BlockSpec((m, k), lambda i: (0, 0)),
            pl.BlockSpec((k, cols), lambda i: (0, i)),
            pl.BlockSpec((1, cols), lambda i: (0, i)),
        ],
        out_specs=[out, out],
    )(rows, weight, shift)


def d_pre_kernel(grad, weight, slope, d_pre, total):
    back = dot_nt(grad[...], weight[...]) * slope[...].astype(F32)
    low = back.astype(BF)
    d_pre[...] = low
    total[...] = jnp.sum(low.astype(F32), axis=0, keepdims=True)


def hidden_back(grad, weight, slope, late):
    m, k = grad.shape
    n = weight.shape[0]
    cols = 256
    out = pl.BlockSpec((m, cols), lambda i: (0, i))
    return kernel_call(
        d_pre_kernel,
        "hidden_back",
        [struct((m, n), BF), struct((1, n), F32)],
        late=late,
        us=6,
        grid=(n // cols,),
        in_specs=[
            pl.BlockSpec((m, k), lambda i: (0, 0)),
            pl.BlockSpec((cols, k), lambda i: (i, 0)),
            out,
        ],
        out_specs=[out, pl.BlockSpec((1, cols), lambda i: (0, i))],
    )(grad, weight, slope)


def head_pair(packed, query_shift, value_shift, p):
    at = slice(p * 128, (p + 1) * 128)
    query = (packed[:, p * 128 : (p + 1) * 128] + query_shift[:, at]).astype(BF)
    key = packed[:, 512 + p * 128 : 512 + (p + 1) * 128].astype(BF)
    value = (packed[:, 1024 + p * 128 : 1024 + (p + 1) * 128] + value_shift[:, at]).astype(BF)
    return query, key, value


SCALE = HEAD_DIM ** (-0.5)


def stacked(pair, first):
    zero = jnp.zeros_like(pair)
    return jnp.concatenate([jnp.where(first, pair, zero), jnp.where(first, zero, pair)])


def merged(both, first):
    half = both.shape[0] // 2
    return jnp.where(first, both[:half], both[half:])


def softmax_of(queries, key, blocked):
    scores = dot_nt(queries, key) * SCALE + blocked
    exps = jnp.exp(scores - jnp.max(scores, axis=-1, keepdims=True))
    return exps * (1.0 / jnp.sum(exps, axis=-1, keepdims=True))


def attention_kernel(packed, query_shift, value_shift, blocked, mixed):
    first = lax.broadcasted_iota(jnp.int32, (BLOCK, 128), 1) < 64
    both = jnp.concatenate([blocked[...], blocked[...]])
    for p in range(4):
        query, key, value = head_pair(packed, query_shift, value_shift, p)
        probs = softmax_of(stacked(query, first), key, both)
        parts = dot(probs.astype(BF), value)
        mixed[:, p * 128 : (p + 1) * 128] = merged(parts, first).astype(BF)


def attention(packed, query_shift, value_shift, blocked, late):
    rows = packed.shape[0]
    shift = pl.BlockSpec((1, 512), lambda i: (0, 0))
    return kernel_call(
        lambda *refs: attention_kernel(*refs[:-1]),
        "attention",
        [struct((rows, 512), BF), TOKEN],
        us=5,
        late=late,
        grid=(rows // BLOCK,),
        in_specs=[
            pl.BlockSpec((BLOCK, 1536), lambda i: (i, 0)),
            shift,
            shift,
            pl.BlockSpec((None, BLOCK, BLOCK), lambda i: (i, 0, 0)),
        ],
        out_specs=[pl.BlockSpec((BLOCK, 512), lambda i: (i, 0)), TOKEN_SPEC],
    )(packed, query_shift, value_shift, blocked)


def attention_back_kernel(packed, query_shift, value_shift, blocked, d_mixed, d_packed, total):
    first = lax.broadcasted_iota(jnp.int32, (BLOCK, 128), 1) < 64

    @pl.when(pl.program_id(0) == 0)
    def _():
        total[...] = jnp.zeros_like(total)

    both = jnp.concatenate([blocked[...], blocked[...]])
    for p in range(4):
        query, key, value = head_pair(packed, query_shift, value_shift, p)
        queries = stacked(query, first)
        grads = stacked(d_mixed[:, p * 128 : (p + 1) * 128], first)
        probs = softmax_of(queries, key, both)
        d_probs = dot_nt(grads, value)
        d_scores = probs * (d_probs - jnp.sum(probs * d_probs, axis=-1, keepdims=True))
        d_scores = d_scores.astype(BF)
        parts = (
            merged(dot(d_scores, key), first) * SCALE,
            dot_tn(d_scores, queries) * SCALE,
            dot_tn(probs.astype(BF), grads),
        )
        for k, part in enumerate(parts):
            at = slice(k * 512 + p * 128, k * 512 + (p + 1) * 128)
            low = part.astype(BF)
            d_packed[:, at] = low
            total[:, at] += jnp.sum(low.astype(F32), axis=0, keepdims=True)


def attention_back(packed, query_shift, value_shift, blocked, d_mixed, late):
    rows = packed.shape[0]
    shift = pl.BlockSpec((1, 512), lambda i: (0, 0))
    return kernel_call(
        attention_back_kernel,
        "attention_back",
        [struct((rows, 1536), BF), struct((1, 1536), F32)],
        us=16,
        late=late,
        grid=(rows // BLOCK,),
        in_specs=[
            pl.BlockSpec((BLOCK, 1536), lambda i: (i, 0)),
            shift,
            shift,
            pl.BlockSpec((None, BLOCK, BLOCK), lambda i: (i, 0, 0)),
            pl.BlockSpec((BLOCK, 512), lambda i: (i, 0)),
        ],
        out_specs=[
            pl.BlockSpec((BLOCK, 1536), lambda i: (i, 0)),
            pl.BlockSpec((1, 1536), lambda i: (0, 0)),
        ],
    )(packed, query_shift, value_shift, blocked, d_mixed)


def dot(left, right):
    return jnp.dot(left, right, preferred_element_type=F32)


def dot_nt(left, right):
    return lax.dot_general(left, right, (((1,), (1,)), ((), ())), preferred_element_type=F32)


def dot_tn(left, right):
    return lax.dot_general(left, right, (((0,), (0,)), ((), ())), preferred_element_type=F32)


def normalize(values):
    center = values - jnp.mean(values, axis=-1, keepdims=True)
    rstd = lax.rsqrt(jnp.mean(center * center, axis=-1, keepdims=True) + EPS)
    return center * rstd, rstd


def normalize_back(grad, yhat, rstd, gain):
    t = grad * gain
    return rstd * (
        t
        - jnp.mean(t, axis=-1, keepdims=True)
        - yhat * jnp.mean(t * yhat, axis=-1, keepdims=True)
    )


TILE = 160


def middle_kernel(part, other, tokens, keep, shift, gain, bias, middle, normed):
    attended = part[...].astype(F32) + other[...].astype(F32) + shift[...]
    rows = tokens[...].astype(F32) + keep[...] * attended
    middle[...] = rows
    yhat, _ = normalize(rows)
    normed[...] = (yhat * gain[...] + bias[...]).astype(BF)


def row_specs(count, width=1024):
    half = count // 2
    return (
        pl.BlockSpec((TILE, width), lambda i: (i, 0)),
        pl.BlockSpec((TILE, width), lambda i: (lax.rem(i + half, count), 0)),
        pl.BlockSpec((TILE, 1), lambda i: (i, 0)),
        pl.BlockSpec((1, width), lambda i: (0, 0)),
    )


def middle_layer(part, other, tokens, keep, shift, gain, bias):
    rows = part.shape[0]
    tile, swapped, column, vector = row_specs(rows // TILE)
    return kernel_call(
        middle_kernel,
        "middle_layer",
        [struct((rows, 1024), F32), struct((rows, 1024), BF)],
        us=6,
        pinned_out=(0,),
        grid=(rows // TILE,),
        in_specs=[tile, swapped, tile, column, vector, vector, vector],
        out_specs=[tile, tile],
    )(part, other, tokens, keep, shift, gain, bias)


def middle_back_kernel(shares, part, other, middle, cot, keep, gain, d_middle, d_attended, sums):
    step = pl.program_id(0)
    grad = part[...].astype(F32) + other[...].astype(F32)
    yhat, rstd = normalize(middle[...])
    incoming = cot[...].astype(F32) * shares[step // (pl.num_programs(0) // 2)]
    d_rows = incoming + normalize_back(grad, yhat, rstd, gain[...])
    d_middle[...] = d_rows
    low = (keep[...] * d_rows).astype(BF)
    d_attended[...] = low
    branch = (keep[...] * incoming).astype(BF)

    @pl.when(step == 0)
    def _():
        sums[...] = jnp.zeros_like(sums)

    @pl.when(step < pl.num_programs(0) // 2)
    def _():
        for k, v in enumerate((grad * yhat, grad, low.astype(F32), branch.astype(F32))):
            sums[k : k + 1, :] += jnp.sum(v, axis=0, keepdims=True)


def middle_back(shares, part, other, middle, cot, keep, gain, late):
    rows = part.shape[0]
    tile, swapped, column, vector = row_specs(rows // TILE)
    return kernel_call(
        middle_back_kernel,
        "middle_back",
        [struct((rows, 1024), F32), struct((rows, 1024), BF), struct((8, 1024), F32)],
        us=7,
        late=late,
        pinned=(3, 4),
        grid=(rows // TILE,),
        in_specs=[SMEM, tile, swapped, tile, tile, column, vector],
        out_specs=[tile, tile, pl.BlockSpec((8, 1024), lambda i: (0, 0))],
    )(shares, part, other, middle, cot, keep, gain)


def input_back_kernel(groups, shares, part, other, rows, d_middle, gain, cot, grad_rows, sums):
    grad = part[...].astype(F32) + other[...].astype(F32)
    yhat, rstd = normalize(rows[...].astype(F32))
    values = (d_middle[...] + normalize_back(grad, yhat, rstd, gain[...])).astype(BF)
    rest = (cot[...].astype(F32) * shares[0]).astype(BF)
    grad_rows[...] = spread(groups[0], values, rest)

    @pl.when(pl.program_id(0) == 0)
    def _():
        sums[...] = jnp.zeros_like(sums)

    for k, v in enumerate((grad * yhat, grad)):
        sums[k : k + 1, :] += jnp.sum(v, axis=0, keepdims=True)


def input_back(groups, shares, part, other, rows, d_middle, gain, cot, late):
    tile = pl.BlockSpec((BLOCK, 1024), lambda i: (i, 0))
    span = pl.BlockSpec((SPAN, 1024), lambda i: (i, 0))
    return kernel_call(
        input_back_kernel,
        "input_back",
        [struct(cot.shape, BF), struct((8, 1024), F32)],
        us=4,
        late=late,
        grid=(2,),
        in_specs=[
            SMEM,
            SMEM,
            tile,
            tile,
            tile,
            tile,
            pl.BlockSpec((1, 1024), lambda i: (0, 0)),
            span,
        ],
        out_specs=[span, pl.BlockSpec((8, 1024), lambda i: (0, 0))],
    )(groups, shares, part, other, rows, d_middle, gain, cot)


def body(
    tokens,
    norm1_gain,
    norm1_bias,
    qkv_weight,
    query_bias,
    value_bias,
    out_weight,
    out_bias,
    norm2_gain,
    norm2_bias,
    fc1_weight,
    fc1_bias,
    fc2_weight,
    fc2_bias,
    cotangent,
    group_of,
    keep_mask,
    group_tokens,
):
    here = Where()
    c = here.c
    here.make_table()
    place_table = here.table

    vectors = (
        norm1_gain,
        norm1_bias,
        query_bias,
        value_bias,
        out_bias,
        norm2_gain,
        norm2_bias,
        fc2_bias,
        fc1_bias,
    )

    def whole(v):
        return pl.BlockSpec(v.shape, lambda i: (0,) * len(v.shape))

    shapes = [
        struct(shape, BF) for shape in ((8, 32, 1664), (64, 2048), (256, 1024), (64, 1024))
    ]
    weights = (qkv_weight, fc1_weight, fc2_weight, out_weight)
    qkv_rep, fc1_part, fc2_half, out_half = kernel_call(
        prepare_kernel,
        "prepare",
        shapes,
        us=3,
        pinned=range(1, 14),
        grid=(1,),
        in_specs=[SMEM] + [whole(v) for v in weights + vectors],
        out_specs=[whole(v) for v in shapes],
    )(place_table, *weights, *vectors)
    qkv_slab = all_to_all(qkv_rep, "fsdp")
    fc1_row = lax.all_gather(fc1_part, "fsdp", axis=0, axis_index_groups=X_GROUPS)
    out_all = lax.all_gather(out_half, "fsdp", axis=0, tiled=True)
    fc2_pair = assemble(
        here,
        "fc2_hi",
        [fc2_half, permute(fc2_half, flip_hi)],
        (2, 256, 1024),
        lambda o, t, n: o.at[t[HI] if n == 0 else 1 - t[HI]],
    )

    qkv_blocks = ring_blocks(qkv_slab, "z")
    fc1_blocks = ring_blocks(fc1_row, "y")
    fc2_blocks = ring_blocks(fc2_pair, "x")
    qkv_all = assemble(
        here,
        "qkv_z",
        qkv_blocks,
        (8, 4, 32, 1536),
        lambda o, t, n: o.at[:, source_in(t, Z, n)],
        lambda ref: ref.at[:, :, pl.ds(0, 1536)],
        late=fc2_blocks[3:],
    ).reshape(1024, 1536)
    (
        gain_one,
        shift_one,
        out_shift,
        gain_two,
        shift_two,
        fc2_shift,
        query_shift,
        value_shift,
        fc1_shift,
    ) = kernel_call(
        vectors_kernel,
        "vectors",
        [struct((1, 1024), F32)] * 6 + [struct((1, 512), F32)] * 2 + [struct((1, 2048), F32)],
        us=1,
        grid=(1,),
        in_specs=[SMEM, pl.BlockSpec((8, 16, 128), lambda i: (0, 0, 12))],
        out_specs=[pl.BlockSpec((1, n), lambda i: (0, 0)) for n in (1024,) * 6 + (512,) * 2 + (2048,)],
    )(place_table, qkv_slab)

    groups = jnp.stack([pick(group_of, here.dp), pick(group_of, here.dp + here.sign)])
    counts = group_tokens.astype(F32)
    shares = counts / jnp.sum(counts)
    shares = jnp.where(groups == 1, shares[1], shares[0])
    rows_low, cot, d_branch, mask_col, blocked = compact(
        groups,
        shares,
        tokens,
        permute(tokens, swap_core),
        cotangent,
        permute(cotangent, swap_core),
        keep_mask,
        permute(keep_mask, swap_core),
    )
    own_rows = 2 * BLOCK

    yhat_one, _ = normalize(rows_low.astype(F32))
    normed = (yhat_one * gain_one + shift_one).astype(BF)
    packed = dot(normed, qkv_all)
    mixed, attention_done = attention(packed, query_shift, value_shift, blocked, fc1_blocks[3:])
    attended = dot(mixed, out_all).astype(BF)
    middle, normed_two = middle_layer(
        attended, permute(attended, swap_core), rows_low, mask_col, out_shift, gain_two, shift_two
    )
    fc1_all = assemble(
        here,
        "fc1_y",
        fc1_blocks,
        (2, 4, 2, 64, 2048),
        lambda o, t, n: o.at[source_in(t, Y, n) // 2, :, lax.rem(source_in(t, Y, n), 2)],
        late=(attention_done,),
    ).reshape(1024, 2048)
    hidden, slope = hidden_layer(normed_two, fc1_all, fc1_shift)
    fc2_all = assemble(
        here,
        "fc2_x",
        fc2_blocks,
        (2, 4, 256, 1024),
        lambda o, t, n: o.at[:, source_in(t, X, n)],
        late=(attention_done,),
    ).reshape(2048, 1024)

    grad_fc2, fc2_done = grad_fc2_terms(hidden, d_branch, ())
    fc2_sum = lax.psum_scatter(
        grad_fc2.reshape(2048, 1024),
        "dp",
        scatter_dimension=0,
        axis_index_groups=Z_GROUPS,
        tiled=True,
    )
    d_pre, fc1_bias_sum = hidden_back(d_branch, fc2_all, slope, (fc2_done,))
    d_normed_two = dot_nt(d_pre, fc1_all).astype(BF)
    *grad_fc1, fc1_done = grad_fc1_terms(here, normed_two, d_pre, (d_normed_two,))
    grad_fc1 = list(zip(*grad_fc1))
    fc1_arrived = ring_both(grad_fc1[0])
    d_middle, d_attended, middle_sums = middle_back(
        shares,
        d_normed_two,
        permute(d_normed_two, swap_core),
        middle,
        cot,
        mask_col,
        gain_two,
        (fc1_done,),
    )
    d_mixed = dot_nt(d_attended, out_all).astype(BF)
    fc1_sum, add_done = add_both(fc1_arrived, grad_fc1[1], (middle_sums,))
    fc1_arrived = ring_both(fc1_sum)
    d_packed, packed_sums = attention_back(
        packed, query_shift, value_shift, blocked, d_mixed, (add_done,)
    )
    fc1_sum, add_done = add_both(fc1_arrived, grad_fc1[2], (packed_sums,))
    fc1_arrived = ring_both(fc1_sum)
    grad_qkv = grad_qkv_terms(normed, d_packed, mixed, d_attended, (add_done,))
    grad_qkv, d_packed, hidden = lax.optimization_barrier((grad_qkv, d_packed, hidden))
    qkv_sum = lax.psum_scatter(
        grad_qkv.reshape(1024, 2048),
        "dp",
        scatter_dimension=0,
        axis_index_groups=Z_GROUPS,
        tiled=True,
    ).reshape(8, 32, 2048)
    *fc2_blocks, split_done = fc2_split(here, fc2_sum.reshape(8, 64, 1024))
    fc2_kept, fc2_sent = fc2_sums(here, exchange(fc2_blocks, "x"))
    y_sum, x_kept, x_sent = last_both(here, fc1_arrived, grad_fc1[3], (split_done,))
    fc1_sum = fc1_slices(
        here, all_to_all(y_sum, "fsdp", X_GROUPS), x_kept, permute(x_sent, flip_hi)
    )
    fc1_sum = all_to_all(fc1_sum, "dp", SLICE_GROUPS)

    d_normed_sent = permute(dot_nt(d_packed[own_rows:], qkv_all).astype(BF), swap_core)
    d_normed_own = dot_nt(d_packed[:own_rows], qkv_all).astype(BF)
    input_grad, input_sums = input_back(
        groups,
        shares,
        d_normed_own,
        d_normed_sent,
        rows_low,
        d_middle,
        gain_one,
        cotangent,
        (),
    )

    vector_terms = kernel_call(
        vector_terms_kernel,
        "vector_terms",
        struct((8, 16, 128), F32),
        us=1,
        in_specs=[SMEM] + [VMEM] * 4,
        out_specs=VMEM,
    )(place_table, input_sums, packed_sums, middle_sums, fc1_bias_sum)
    qkv_sum = join(qkv_sum, vector_terms, (fc2_kept, fc1_sum))
    qkv_sum, hidden = lax.optimization_barrier((qkv_sum, hidden))

    branch_sent = permute(dot(hidden[own_rows:], fc2_all).astype(BF), swap_core)
    block_out, block_done = block_out_layer(
        groups,
        dot(hidden[:own_rows], fc2_all),
        branch_sent,
        middle,
        mask_col,
        fc2_shift,
        tokens,
    )

    qkv_sum = all_to_all(qkv_sum, "fsdp")
    qkv_kept, qkv_sent, vector_sums = sum_and_halve(here, "qkv_lo", qkv_sum, 2048)
    mlp_piece = kernel_call(
        pack_mlp_kernel,
        "pack_mlp",
        struct((32, 2048), BF),
        us=1,
        late=(vector_terms,),
        grid=(1,),
        in_specs=[whole(v) for v in (fc2_kept, fc2_sent, fc1_sum)],
        out_specs=pl.BlockSpec((32, 2048), lambda i: (0, 0)),
    )(fc2_kept, fc2_sent, fc1_sum)
    mlp_own = lax.all_gather(mlp_piece, "dp", axis=0, axis_index_groups=SLICE_GROUPS)
    sums = (qkv_kept, qkv_sent, vector_sums)
    packed_slices = kernel_call(
        pack_kernel,
        "pack",
        struct((8, 16, 2176), BF),
        us=1,
        late=(block_done,),
        grid=(1,),
        in_specs=[whole(v) for v in sums],
        out_specs=whole(struct((8, 16, 2176), BF)),
    )(*sums)
    own = all_to_all(packed_slices, "dp", SLICE_GROUPS)
    own, mlp_own = lax.optimization_barrier((own, mlp_own))
    half = pl.BlockSpec((None, 16, 2176), lambda i: (i, 0, 0))
    grad_qkv_weight, grad_out_weight, *vector_sums = kernel_call(
        unpack_kernel,
        "unpack",
        [
            struct((128, 3072), F32),
            struct((2, 8, 8, 1024), F32),
            *(struct((1, 128), F32),) * 8,
            struct((4, 128), F32),
        ],
        us=3,
        grid=(8,),
        in_specs=[SMEM, half, half],
        out_specs=[
            pl.BlockSpec((16, 3072), lambda i: (i, 0)),
            pl.BlockSpec((2, None, 8, 1024), lambda i: (0, i, 0, 0)),
            *(pl.BlockSpec((1, 128), lambda i: (0, 0)),) * 8,
            pl.BlockSpec((4, 128), lambda i: (0, 0)),
        ],
    )(place_table, own, permute(own, swap_core))
    half = pl.BlockSpec((None, 32, 2048), lambda i: (i, 0, 0))
    grad_fc1_weight, grad_fc2_weight = kernel_call(
        unpack_mlp_kernel,
        "unpack_mlp",
        [struct((128, 4096), F32), struct((2, 8, 32, 1024), F32)],
        us=3,
        grid=(8,),
        in_specs=[SMEM, half, half],
        out_specs=[
            pl.BlockSpec((16, 4096), lambda i: (lax.rem(i, 2) * 4 + i // 2, 0)),
            pl.BlockSpec((2, None, 32, 1024), lambda i: (0, i, 0, 0)),
        ],
    )(place_table, mlp_own, permute(mlp_own, swap_core))
    return (
        block_out,
        input_grad,
        vector_sums[0].reshape(128),
        vector_sums[1].reshape(128),
        grad_qkv_weight,
        vector_sums[2].reshape(128),
        vector_sums[3].reshape(128),
        grad_out_weight.reshape(128, 1024),
        vector_sums[4].reshape(128),
        vector_sums[5].reshape(128),
        vector_sums[6].reshape(128),
        grad_fc1_weight,
        vector_sums[8].reshape(512),
        grad_fc2_weight.reshape(512, 1024),
        vector_sums[7].reshape(128),
    )


def solution(mesh):
    rows, cols, both = P("fsdp", None), P("fsdp"), ("dp", "fsdp")
    in_specs = (
        P(both, None),
        cols,
        cols,
        rows,
        cols,
        cols,
        rows,
        cols,
        cols,
        cols,
        rows,
        cols,
        rows,
        cols,
        P(both, None),
        P(),
        P(both),
        P(),
    )
    out_specs = (
        P(both, None),
        P(both, None),
        cols,
        cols,
        rows,
        cols,
        cols,
        rows,
        cols,
        cols,
        cols,
        rows,
        cols,
        rows,
        cols,
    )
    return jax.shard_map(body, mesh=mesh, in_specs=in_specs, out_specs=out_specs, check_vma=False)
```
